32 devices in a mesh: dp: 8 (over z, y), shard: 4 (over x, core).
Axes of the slice: x: 2, y: 2, z: 4, core: 2. Of those that a mesh axis runs over, the one named last changes fastest.
Arguments:
- char_ids: int32 [2048, 4], P(('dp', 'shard')), may hold values from 0 to 274
- targets: int32 [2048, 4], P(('dp', 'shard')), may hold values from 0 to 274
- hidden_start: float32 [2048, 2048], P(('dp', 'shard')), may hold values from -0.9 to 0.9
- cell_start: float32 [2048, 2048], P(('dp', 'shard')), may hold values from -4 to 4
- embedding: float32 [275, 100], replicated, may hold values from -5 to 5
- input_weight: float32 [8192, 100], P(('dp', 'shard')), may hold values from -0.625 to 0.625
- hidden_weight: float32 [8192, 2048], P(('dp', 'shard')), may hold values from -0.125 to 0.125
- gate_bias: float32 [8192], P(('dp', 'shard')), may hold values from -3 to 3
- decoder_weight: float32 [2048, 275], P(('dp', 'shard')), may hold values from -0.5 to 0.5
- decoder_bias: float32 [275], replicated, may hold values from -3 to 3
- momentum_embed: float32 [275, 100], replicated, may hold values from -0.0008544922 to 0.0008544922
- momentum_input: float32 [8192, 100], P(('dp', 'shard')), may hold values from -0.001953125 to 0.001953125
- momentum_hidden: float32 [8192, 2048], P(('dp', 'shard')), may hold values from -0.00061035156 to 0.00061035156
- momentum_gate: float32 [8192], P(('dp', 'shard')), may hold values from -0.0078125 to 0.0078125
- momentum_decoder: float32 [2048, 275], P(('dp', 'shard')), may hold values from -0.00390625 to 0.00390625
- momentum_outbias: float32 [275], replicated, may hold values from -0.75 to 0.75
Outputs:
- loss: float32 [1], replicated
- grad_norm: float32 [1], replicated
- grad_hidden_start: float32 [2048, 2048], P(('dp', 'shard'))
- grad_cell_start: float32 [2048, 2048], P(('dp', 'shard'))
- grad_embedding: float32 [275, 100], replicated
- grad_input_weight: float32 [8192, 100], P(('dp', 'shard'))
- grad_hidden_weight: float32 [8192, 2048], P(('dp', 'shard'))
- grad_gate_bias: float32 [8192], P(('dp', 'shard'))
- grad_decoder_weight: float32 [2048, 275], P(('dp', 'shard'))
- grad_decoder_bias: float32 [275], replicated
- new_momentum_embed: float32 [275, 100], replicated
- new_momentum_input: float32 [8192, 100], P(('dp', 'shard'))
- new_momentum_hidden: float32 [8192, 2048], P(('dp', 'shard'))
- new_momentum_gate: float32 [8192], P(('dp', 'shard'))
- new_momentum_decoder: float32 [2048, 275], P(('dp', 'shard'))
- new_momentum_outbias: float32 [275], replicated
The draws below stay inside these ranges and needn't reach their ends.
All inputs are finite; a program needn't handle non-finite values.
Results may differ from the reference program's by a relative error of at most 0.0097.
Values may be sent and summed in bfloat16 or wider, within the bound.
A program may use at most 192 MiB of HBM per device.

```python
import math
import jax
import jax.numpy as jnp
import numpy as np
from jax import lax

E = 100
H = 2048
V = 275
SEQ = 4
G = 8192
STREAMS = 2048


def with_ends(entries, own_key, smallest, high):
    dims = entries.shape
    index_at = [jax.random.randint(jax.random.fold_in(own_key, axis), (), 0, dims[axis]) for axis in range(len(dims))]
    entries = entries.at[tuple(index_at)].set(smallest)
    longest = dims.index(max(dims))
    index_at[longest] = (index_at[longest] + 1) % dims[longest]
    return entries.at[tuple(index_at)].set(high)


def block_scale(rng, dims, cuts, low, largest):
    level = 1.0
    for dim, parts in cuts:
        steps = jax.random.uniform(jax.random.fold_in(jax.random.fold_in(rng, 6), dim), (parts,), jnp.float32, low / len(cuts), largest / len(cuts))
        level = level * jnp.repeat(jnp.exp(steps), dims[dim] // parts).reshape((-1,) + (1,) * (len(dims) - 1 - dim))
    return level


def rank_bounds(number_of, skew):
    weights = [(1 << 20) // math.isqrt(rank ** skew) + 1 for rank in range(1, number_of + 1)]
    scale = 1 + sum(weights) // (1 << 30)
    return np.cumsum(np.array([max(1, weight // scale) for weight in weights]))


def ranked_ids(own_key, shape, count, skew):
    table = rank_bounds(count, skew)
    pick = jax.random.randint(jax.random.fold_in(own_key, 1), shape, 0, int(table[count - 1]))
    rank = jnp.searchsorted(jnp.asarray(table, jnp.int32), pick, side="right")
    return jax.random.permutation(jax.random.fold_in(own_key, 2), count)[rank].astype(jnp.int32)


def scatter_about(key, extent, deviation, bound, shards=(), held_as=jnp.bfloat16):
    gain = block_scale(key, extent, shards, -0.22, 0.18) if shards else 1.0
    result = jax.random.normal(key, extent, jnp.float32) * deviation * gain
    return jnp.minimum(jnp.maximum(result, -bound), bound).astype(held_as)


def setup_inputs(seed: int = 0) -> dict:
    streams_of = jax.random.split(jax.random.key(seed), 17)
    char_ids = with_ends(ranked_ids(streams_of[0], (STREAMS, SEQ), V, 2), jax.random.fold_in(streams_of[0], 3), 0, V - 1).astype(jnp.int32)
    targets = with_ends(ranked_ids(streams_of[1], (STREAMS, SEQ), V, 2), jax.random.fold_in(streams_of[1], 3), 0, V - 1).astype(jnp.int32)
    hidden_start = jnp.clip(jax.random.uniform(streams_of[2], (STREAMS, H), jnp.float32, -0.9, 0.9) * block_scale(streams_of[2], (STREAMS, H), ((0, 32),), -0.4, 0.0), -0.9, 0.9)
    cell_start = scatter_about(streams_of[3], (STREAMS, H), 1.0, 4.0, ((0, 32),), jnp.float32)
    embedding = scatter_about(streams_of[4], (V, E), 1.0, 5.0, (), jnp.float32)
    input_weight = scatter_about(streams_of[5], (G, E), E ** -0.5, 0.625, ((0, 32),), jnp.float32)
    hidden_weight = scatter_about(streams_of[6], (G, H), H ** -0.5, 0.125, ((0, 32),), jnp.float32)
    gate_bias = scatter_about(streams_of[7], (G,), 0.5, 3.0, ((0, 32),), jnp.float32)
    decoder_weight = scatter_about(streams_of[8], (H, V), (H // 16) ** -0.5, 0.5, ((0, 32),), jnp.float32)
    decoder_bias = scatter_about(streams_of[9], (V,), 0.5, 3.0, (), jnp.float32)
    momentum_embed = scatter_about(streams_of[10], (V, E), 0.00006, 0.0008544922, (), jnp.float32)
    momentum_input = scatter_about(streams_of[11], (G, E), 0.00015, 0.001953125, ((0, 32),), jnp.float32)
    momentum_hidden = scatter_about(streams_of[12], (G, H), 0.00004, 0.00061035156, ((0, 32),), jnp.float32)
    momentum_gate = scatter_about(streams_of[13], (G,), 0.0006, 0.0078125, ((0, 32),), jnp.float32)
    momentum_decoder = scatter_about(streams_of[14], (H, V), 0.00027, 0.00390625, ((0, 32),), jnp.float32)
    momentum_outbias = scatter_about(streams_of[15], (V,), 0.05, 0.75, (), jnp.float32)
    return {"char_ids": char_ids, "targets": targets, "hidden_start": hidden_start, "cell_start": cell_start, "embedding": embedding, "input_weight": input_weight, "hidden_weight": hidden_weight, "gate_bias": gate_bias, "decoder_weight": decoder_weight, "decoder_bias": decoder_bias, "momentum_embed": momentum_embed, "momentum_input": momentum_input, "momentum_hidden": momentum_hidden, "momentum_gate": momentum_gate, "momentum_decoder": momentum_decoder, "momentum_outbias": momentum_outbias}


@jax.custom_vjp
def low(v):
    return lax.optimization_barrier(v.astype(jnp.bfloat16)).astype(jnp.float32)

@jax.custom_vjp
def low_back(v):
    return v

def low_keep(v):
    return (low(v), None)

def low_pass(kept, grad):
    return (grad,)

def back_keep(v):
    return (v, None)

def back_low(kept, grad):
    return (low(grad),)
low.defvjp(low_keep, low_pass)
low_back.defvjp(back_keep, back_low)
CLIP = 0.25
MOMENTUM = 0.5

def matmul(left, right):
    return jnp.dot(left, right, precision=lax.Precision.HIGHEST, preferred_element_type=jnp.float32)

def objective(embedding, input_weight, hidden_weight, gate_bias, decoder_weight, decoder_bias, hidden_start, cell_start, char_ids, targets):
    vocab_size = embedding.shape[0]
    hidden_size = hidden_start.shape[1]
    table = low(embedding)
    weight_in = low(input_weight)
    weight_rec = low(hidden_weight)
    bias_low = low(gate_bias)
    weight_out = low(decoder_weight)
    columns = jnp.arange(vocab_size, dtype=jnp.int32)

    def time_step(carried, inputs):
        hidden_low, cell = carried
        ids_now, target_now = inputs
        embedded = table[ids_now]
        preact = low_back(matmul(embedded, weight_in.T) + matmul(hidden_low, weight_rec.T) + bias_low)
        input_gate = jax.nn.sigmoid(preact[:, :hidden_size])
        forget_gate = jax.nn.sigmoid(preact[:, hidden_size:2 * hidden_size])
        candidate = jnp.tanh(preact[:, 2 * hidden_size:3 * hidden_size])
        output_gate = jax.nn.sigmoid(preact[:, 3 * hidden_size:])
        cell_next = forget_gate * cell + input_gate * candidate
        hidden_next = low(output_gate * jnp.tanh(cell_next))
        logits = low_back(matmul(hidden_next, weight_out) + decoder_bias)
        log_total = jax.nn.logsumexp(logits, axis=1)
        picked = lax.optimization_barrier(jnp.sum(jnp.where(target_now[:, None] == columns[None, :], logits, 0.0), axis=1))
        return ((hidden_next, cell_next), jnp.sum(log_total - picked))
    carried_end, losses = lax.scan(jax.checkpoint(time_step), (low(hidden_start), cell_start), (char_ids.T, targets.T))
    return jnp.sum(losses) / SEQ

def reference(char_ids, targets, hidden_start, cell_start, embedding, input_weight, hidden_weight, gate_bias, decoder_weight, decoder_bias, momentum_embed, momentum_input, momentum_hidden, momentum_gate, momentum_decoder, momentum_outbias):

    def wrapped(embed_arg, input_arg, hidden_arg, gate_arg, decoder_arg, outbias_arg, start_arg, cell_arg):
        return objective(embed_arg, input_arg, hidden_arg, gate_arg, decoder_arg, outbias_arg, start_arg, cell_arg, char_ids, targets)
    objective_value, pullback = jax.vjp(wrapped, embedding, input_weight, hidden_weight, gate_bias, decoder_weight, decoder_bias, hidden_start, cell_start)
    gradients = pullback(jnp.ones_like(objective_value))
    weight_grads = gradients[:6]
    square_total = jnp.sum(weight_grads[0] * weight_grads[0])
    for gradient in weight_grads[1:]:
        square_total = square_total + jnp.sum(gradient * gradient)
    grad_norm = jnp.sqrt(square_total)
    factor = CLIP / jnp.maximum(grad_norm, CLIP)
    momenta = (momentum_embed, momentum_input, momentum_hidden, momentum_gate, momentum_decoder, momentum_outbias)
    new_momenta = [MOMENTUM * momenta[index] + factor * weight_grads[index] for index in range(6)]
    loss = objective_value / char_ids.shape[0]
    return (loss.reshape(1), grad_norm.reshape(1), gradients[6], gradients[7], weight_grads[0], weight_grads[1], weight_grads[2], weight_grads[3], weight_grads[4], weight_grads[5], new_momenta[0], new_momenta[1], new_momenta[2], new_momenta[3], new_momenta[4], new_momenta[5])
```

```python
import functools

import jax
import jax.numpy as jnp
from jax import lax
from jax.experimental import pallas as pl
from jax.experimental.pallas import tpu as pltpu
from jax.sharding import PartitionSpec as P

MESH = pl.DeviceIdType.MESH
F32 = jnp.float32
BF16 = jnp.bfloat16

MICRO = 2


CLIP = 0.25
MOMENTUM = 0.5


def contract_rows(left, right):
    return lax.dot_general(
        left, right, (((0,), (0,)), ((), ())), preferred_element_type=jnp.float32
    )


def contract_last(left, right):
    return lax.dot_general(
        left, right, (((1,), (1,)), ((), ())), preferred_element_type=jnp.float32
    )


def local(
    char_ids,
    targets,
    hidden_start,
    cell_start,
    embedding,
    input_weight,
    hidden_weight,
    gate_bias,
    decoder_weight,
    decoder_bias,
    momentum_embed,
    momentum_input,
    momentum_hidden,
    momentum_gate,
    momentum_decoder,
    momentum_outbias,
):
    streams, seq_len = char_ids.shape
    micro_rows = streams // MICRO
    vocab_size = embedding.shape[0]
    hidden_size = hidden_start.shape[1]
    low_input = input_weight.astype(jnp.bfloat16)
    low_hidden = hidden_weight.astype(jnp.bfloat16)
    low_bias = gate_bias.astype(jnp.bfloat16)
    low_decoder = decoder_weight.astype(jnp.bfloat16)
    inner_rows = (
        lax.all_gather(low_input, "shard", axis=0, tiled=True),
        lax.all_gather(low_hidden, "shard", axis=0, tiled=True),
        lax.all_gather(low_bias, "shard", axis=0, tiled=True),
        lax.all_gather(low_decoder, "shard", axis=0, tiled=True),
    )
    weight_in, weight_rec, bias_low, weight_out = (
        lax.all_gather(inner_rows[0], "dp", axis=0, tiled=True),
        lax.all_gather(inner_rows[1], "dp", axis=0, tiled=True),
        lax.all_gather(inner_rows[2], "dp", axis=0, tiled=True),
        lax.all_gather(inner_rows[3], "dp", axis=0, tiled=True),
    )
    columns = jnp.arange(vocab_size, dtype=jnp.int32)
    table = embedding.astype(jnp.bfloat16)
    bias_row = bias_low.astype(jnp.float32)[None, :]

    def forward_step(carried, input_now):
        hidden_low, cell = carried
        preact = input_now + contract_last(hidden_low, weight_rec)
        input_gate = jax.nn.sigmoid(preact[:, :hidden_size])
        forget_gate = jax.nn.sigmoid(preact[:, hidden_size : 2 * hidden_size])
        candidate = jnp.tanh(preact[:, 2 * hidden_size : 3 * hidden_size])
        output_gate = jax.nn.sigmoid(preact[:, 3 * hidden_size :])
        cell_next = forget_gate * cell + input_gate * candidate
        hidden_next = (output_gate * jnp.tanh(cell_next)).astype(jnp.bfloat16)
        activations = jnp.concatenate([input_gate, forget_gate, candidate, output_gate], axis=1)
        return ((hidden_next, cell_next), (hidden_low, cell, activations, cell_next, hidden_next))

    def backward_step(carried, inputs):
        hidden_grad_next, cell_grad_next = carried
        out_grad, cell_before, gate_values, cell_now = inputs
        hidden_grad = out_grad + hidden_grad_next
        input_gate = gate_values[:, :hidden_size]
        forget_gate = gate_values[:, hidden_size : 2 * hidden_size]
        candidate = gate_values[:, 2 * hidden_size : 3 * hidden_size]
        output_gate = gate_values[:, 3 * hidden_size :]
        cell_tanh = jnp.tanh(cell_now)
        cell_grad = cell_grad_next + hidden_grad * output_gate * (1.0 - cell_tanh * cell_tanh)
        input_term = cell_grad * candidate * input_gate * (1.0 - input_gate)
        forget_term = cell_grad * cell_before * forget_gate * (1.0 - forget_gate)
        candidate_term = cell_grad * input_gate * (1.0 - candidate * candidate)
        output_term = hidden_grad * cell_tanh * output_gate * (1.0 - output_gate)
        gate_grad = jnp.concatenate(
            [input_term, forget_term, candidate_term, output_term], axis=1
        ).astype(jnp.bfloat16)
        hidden_grad_prev = jnp.dot(gate_grad, weight_rec, preferred_element_type=jnp.float32)
        return ((hidden_grad_prev, cell_grad * forget_gate), gate_grad)

    def micro_pass(loss_total, inputs):
        ids_part, target_part, hidden_part, cell_part = inputs
        batch_rows = ids_part.shape[0]
        token_ids = ids_part.T.reshape(-1)
        token_targets = target_part.T.reshape(-1)
        one_input = (token_ids[:, None] == columns[None, :]).astype(jnp.bfloat16)
        one_target = (token_targets[:, None] == columns[None, :]).astype(jnp.float32)
        embedded = jnp.dot(one_input, table, preferred_element_type=jnp.float32).astype(
            jnp.bfloat16
        )
        input_part = contract_last(embedded, weight_in) + bias_row
        input_part = input_part.reshape(seq_len, batch_rows, 4 * hidden_size)
        start_pair = (hidden_part.astype(jnp.bfloat16), cell_part)
        final_pair, saved = lax.scan(forward_step, start_pair, input_part)
        hidden_prev, cell_prev, activations, cell_after, hidden_after = saved
        hidden_rows = hidden_after.reshape(seq_len * batch_rows, hidden_size)
        logits = (
            jnp.dot(hidden_rows, weight_out, preferred_element_type=jnp.float32)
            + decoder_bias[None, :]
        )
        log_total = jax.nn.logsumexp(logits, axis=1)
        local_loss = jnp.sum(log_total - jnp.sum(one_target * logits, axis=1)) / seq_len
        probs = jnp.exp(logits - log_total[:, None])
        logit_grad = ((probs - one_target) / seq_len).astype(jnp.bfloat16)
        hidden_from_out = contract_last(logit_grad, weight_out).reshape(
            seq_len, batch_rows, hidden_size
        )
        zero_state = jnp.zeros((batch_rows, hidden_size), jnp.float32)
        start_grads, gate_grads = lax.scan(
            backward_step,
            (zero_state, zero_state),
            (hidden_from_out, cell_prev, activations, cell_after),
            reverse=True,
        )
        gate_rows = gate_grads.reshape(seq_len * batch_rows, 4 * hidden_size)
        prev_rows = hidden_prev.reshape(seq_len * batch_rows, hidden_size)
        return (
            loss_total + local_loss,
            (
                token_ids,
                embedded,
                logit_grad,
                hidden_rows,
                gate_rows,
                prev_rows,
                start_grads[0],
                start_grads[1],
            ),
        )

    def by_micro(array):
        return array.reshape((MICRO, micro_rows) + array.shape[1:])

    local_loss, stacked = lax.scan(
        micro_pass,
        jnp.zeros((), jnp.float32),
        (by_micro(char_ids), by_micro(targets), by_micro(hidden_start), by_micro(cell_start)),
    )
    token_ids, embedded, logit_grad, hidden_rows, gate_rows, prev_rows, hidden_grads, cell_grads = (
        stacked
    )
    token_ids = token_ids.reshape(-1)
    embedded = embedded.reshape(-1, embedded.shape[-1])
    logit_grad = logit_grad.reshape(-1, vocab_size)
    hidden_rows = hidden_rows.reshape(-1, hidden_size)
    gate_rows = gate_rows.reshape(-1, 4 * hidden_size)
    prev_rows = prev_rows.reshape(-1, hidden_size)
    grad_hidden_start = hidden_grads.reshape(streams, hidden_size)
    grad_cell_start = cell_grads.reshape(streams, hidden_size)
    grad_outbias_local = jnp.sum(logit_grad.astype(jnp.float32), axis=0)
    grad_decoder_local = contract_rows(hidden_rows, logit_grad)
    grad_input_local = contract_rows(gate_rows, embedded)
    grad_hidden_local = contract_rows(gate_rows, prev_rows)
    grad_bias_local = jnp.sum(gate_rows.astype(jnp.float32), axis=0)
    embed_rows_grad = jnp.dot(gate_rows, weight_in, preferred_element_type=jnp.float32)
    one_all = (token_ids[:, None] == columns[None, :]).astype(jnp.float32)
    grad_embed_local = lax.dot_general(
        one_all,
        embed_rows_grad,
        (((0,), (0,)), ((), ())),
        precision=lax.Precision.HIGHEST,
        preferred_element_type=jnp.float32,
    )
    grad_embedding, grad_decoder_bias, loss_sum = lax.psum(
        (grad_embed_local, grad_outbias_local, local_loss), ("dp", "shard")
    )
    outer_sums = (
        lax.psum_scatter(
            grad_input_local.astype(jnp.bfloat16), "dp", scatter_dimension=0, tiled=True
        ).astype(jnp.float32),
        lax.psum_scatter(
            grad_hidden_local.astype(jnp.bfloat16), "dp", scatter_dimension=0, tiled=True
        ).astype(jnp.float32),
        lax.psum_scatter(
            grad_bias_local.astype(jnp.bfloat16), "dp", scatter_dimension=0, tiled=True
        ).astype(jnp.float32),
        lax.psum_scatter(
            grad_decoder_local.astype(jnp.bfloat16), "dp", scatter_dimension=0, tiled=True
        ).astype(jnp.float32),
    )
    grad_input_weight, grad_hidden_weight, grad_gate_bias, grad_decoder_weight = (
        lax.psum_scatter(
            outer_sums[0].astype(jnp.bfloat16), "shard", scatter_dimension=0, tiled=True
        ).astype(jnp.float32),
        lax.psum_scatter(
            outer_sums[1].astype(jnp.bfloat16), "shard", scatter_dimension=0, tiled=True
        ).astype(jnp.float32),
        lax.psum_scatter(
            outer_sums[2].astype(jnp.bfloat16), "shard", scatter_dimension=0, tiled=True
        ).astype(jnp.float32),
        lax.psum_scatter(
            outer_sums[3].astype(jnp.bfloat16), "shard", scatter_dimension=0, tiled=True
        ).astype(jnp.float32),
    )
    shard_squares = jnp.sum(grad_input_weight * grad_input_weight) + jnp.sum(
        grad_hidden_weight * grad_hidden_weight
    )
    shard_squares = (
        shard_squares
        + jnp.sum(grad_gate_bias * grad_gate_bias)
        + jnp.sum(grad_decoder_weight * grad_decoder_weight)
    )
    square_total = lax.psum(shard_squares, ("dp", "shard"))
    square_total = (
        square_total
        + jnp.sum(grad_embedding * grad_embedding)
        + jnp.sum(grad_decoder_bias * grad_decoder_bias)
    )
    grad_norm = jnp.sqrt(square_total)
    factor = CLIP / jnp.maximum(grad_norm, CLIP)
    streams_all = streams * lax.axis_size("dp") * lax.axis_size("shard")
    loss = loss_sum / streams_all
    momenta = (
        momentum_embed,
        momentum_input,
        momentum_hidden,
        momentum_gate,
        momentum_decoder,
        momentum_outbias,
    )
    weight_grads = (
        grad_embedding,
        grad_input_weight,
        grad_hidden_weight,
        grad_gate_bias,
        grad_decoder_weight,
        grad_decoder_bias,
    )
    new_momenta = [MOMENTUM * momenta[index] + factor * weight_grads[index] for index in range(6)]
    return (
        loss.reshape(1),
        grad_norm.reshape(1),
        grad_hidden_start,
        grad_cell_start,
        grad_embedding,
        grad_input_weight,
        grad_hidden_weight,
        grad_gate_bias,
        grad_decoder_weight,
        grad_decoder_bias,
        new_momenta[0],
        new_momenta[1],
        new_momenta[2],
        new_momenta[3],
        new_momenta[4],
        new_momenta[5],
    )


ROWS = 256
HID = 2048
WIDE = 2176
INPUTS = 100
CHARS = 384
SPLIT = 2
PART = ROWS // SPLIT
SLICES = 4
SLICE = ROWS // SLICES
STEPS = 4


def spots():
    dp = lax.axis_index("dp")
    shard = lax.axis_index("shard")
    return dict(
        p=dp // 4,
        zi=(dp // 2) % 2,
        z=dp // 2,
        y=dp % 2,
        k=dp % 4,
        x=shard // 2,
        c=shard % 2,
        dp=dp,
        shard=shard,
    )


def device(s, z=None, y=None, x=None, c=None):
    z = s["z"] if z is None else z
    y = s["y"] if y is None else y
    x = s["x"] if x is None else x
    c = s["c"] if c is None else c
    return (z * 2 + y, x * 2 + c)


def peer(s, d):
    y = 1 - s["y"] if d % 2 else s["y"]
    zi = 1 - s["zi"] if d // 2 else s["zi"]
    z = 2 * s["p"] + zi
    return dict(y=y, zi=zi, k=2 * zi + y, dev=(z * 2 + y, s["shard"]))


def stripe(y, zi, xb):
    return 4 * y + 2 * xb + zi


def cols(index):
    return pl.ds(pl.multiple_of(index * ROWS, ROWS), ROWS)


def aligned(start, size):
    return pl.ds(pl.multiple_of(start, size), size)


def remote(src, dst, send, recv, dev):
    return pltpu.make_async_remote_copy(
        src_ref=src, dst_ref=dst, send_sem=send, recv_sem=recv, device_id=dev, device_id_type=MESH
    )


def dot(left, right):
    return jnp.dot(left, right, preferred_element_type=F32)


def dot_nt(left, right):
    return lax.dot_general(left, right, (((1,), (1,)), ((), ())), preferred_element_type=F32)


def dot_tn(left, right):
    return lax.dot_general(left, right, (((0,), (0,)), ((), ())), preferred_element_type=F32)


def signal(dev):
    pl.semaphore_signal(
        pltpu.get_barrier_semaphore(), inc=1, device_id=dev, device_id_type=MESH
    )


def step_kernel(
    wext,
    h_own,
    cell_own,
    meta_own,
    wout_own,
    table,
    dbias,
    hx_o,
    dg_o,
    dh0_o,
    dc0_o,
    emb_o,
    gdec_o,
    w2,
    wt,
    hx,
    act,
    call,
    dg,
    pbuf,
    rbuf,
    ownp,
    dcn,
    wo,
    dlog,
    metas,
    emb,
    g_send,
    g_recv,
    wz_send,
    wz_recv,
    wx_send,
    wx_recv,
    wc_send,
    wc_recv,
    o_send,
    o_recv,
    h_send,
    h_recv,
    b_send,
    b_recv,
    out_sem,
):
    s = spots()
    z, y, x, c, k, zi, p = s["z"], s["y"], s["x"], s["c"], s["k"], s["zi"], s["p"]
    dp, shard = s["dp"], s["shard"]
    across = device(s, x=1 - x)
    twin = device(s, c=1 - c)
    far = device(s, z=2 * (1 - p) + zi)
    peers = {d: peer(s, d) for d in (1, 2, 3)}
    mine = [stripe(y, zi, xb) for xb in (0, 1)]
    core = z % 2
    off_core = jnp.where(core == c, 0, 1)

    for d in (1, 2, 3):
        signal(peers[d]["dev"])
    signal(across)
    signal(twin)
    signal(far)

    @pl.when(core != c)
    def _():
        for i in (0, 1):
            signal(device(s, z=c + 2 * i, c=core))

    pl.semaphore_wait(pltpu.get_barrier_semaphore(), 6 + 2 * off_core)

    def z_copy(target, q):
        rows = pl.ds(q * SLICE, SLICE)
        slot = aligned((2 * z + x) * ROWS + q * SLICE, SLICE)
        return remote(
            wext.at[rows],
            w2.at[slot],
            wz_send.at[target, q],
            wz_recv.at[z // 2, q],
            device(s, z=c + 2 * target, c=core),
        )

    def z_wait(i, q):
        slot = aligned((2 * (c + 2 * i) + x) * ROWS + q * SLICE, SLICE)
        remote(wext.at[pl.ds(q * SLICE, SLICE)], w2.at[slot], wz_send.at[0, q], wz_recv.at[i, q], across).wait_recv()

    def x_copy(i, q, sender=True):
        xs = x if sender else 1 - x
        slot = aligned((2 * (c + 2 * i) + xs) * ROWS + q * SLICE, SLICE)
        return remote(w2.at[slot], w2.at[slot], wx_send.at[i, q], wx_recv.at[i, q], across)

    def c_copy(i, q, other, sender=True):
        xs = 1 - x if other else x
        cs = c if sender else 1 - c
        slot = aligned((2 * (cs + 2 * i) + xs) * ROWS + q * SLICE, SLICE)
        return remote(
            w2.at[slot], w2.at[slot], wc_send.at[i, int(other), q], wc_recv.at[i, int(other), q], twin
        )

    for target in (0, 1):

        @pl.when(c + 2 * target == z)
        def _():
            w2[aligned((2 * z + x) * ROWS, ROWS), :] = wext[...]

    for q in range(SLICES):
        for target in (0, 1):

            @pl.when(c + 2 * target != z)
            def _():
                z_copy(target, q).start()

    own = aligned(k * 64, 64)
    group = []
    for d in (3, 1, 2):
        dev = peers[d]["dev"]
        group += [
            remote(meta_own, metas.at[own], g_send.at[d - 1, 0], g_recv.at[d - 1, 0], dev),
            remote(h_own, hx.at[0, own, pl.ds(0, HID)], g_send.at[d - 1, 1], g_recv.at[d - 1, 1], dev),
            remote(wout_own, wo.at[dp, shard], g_send.at[d - 1, 2], g_recv.at[d - 1, 2], dev),
        ]
        for xb in (0, 1):
            theirs = stripe(peers[d]["y"], peers[d]["zi"], xb)
            group.append(
                remote(
                    cell_own.at[:, cols(theirs)],
                    call.at[0, xb, own],
                    g_send.at[d - 1, 3 + xb],
                    g_recv.at[d - 1, 3 + xb],
                    dev,
                )
            )
    for copy in group:
        copy.start()
    metas[own, :] = meta_own[...]
    hx[0, own, pl.ds(0, HID)] = h_own[...]
    wo[dp, shard] = wout_own[...]
    for xb in (0, 1):
        call[0, xb, own] = cell_own[:, cols(mine[xb])]

    def group_wait(d, n):
        there = peers[d]
        rows = aligned(there["k"] * 64, 64)
        if n == 0:
            copy = remote(meta_own, metas.at[rows], g_send.at[d - 1, 0], g_recv.at[d - 1, 0], there["dev"])
        elif n == 1:
            copy = remote(h_own, hx.at[0, rows, pl.ds(0, HID)], g_send.at[d - 1, 1], g_recv.at[d - 1, 1], there["dev"])
        elif n == 2:
            copy = remote(wout_own, wo.at[there["dev"][0], shard], g_send.at[d - 1, 2], g_recv.at[d - 1, 2], there["dev"])
        else:
            copy = remote(
                cell_own.at[:, cols(mine[n - 3])],
                call.at[0, n - 3, rows],
                g_send.at[d - 1, n],
                g_recv.at[d - 1, n],
                there["dev"],
            )
        copy.wait_recv()

    for d in (1, 2, 3):
        group_wait(d, 0)
    lanes = lax.broadcasted_iota(jnp.int32, (ROWS, CHARS), 1)
    for t in range(STEPS):
        one = jnp.where(metas[:, t : t + 1] == lanes, 1.0, 0.0).astype(BF16)
        hx[t, :, pl.ds(HID, WIDE - HID)] = dot(one, table[...]).astype(BF16)

    def turn(i):
        def _():
            w = pl.ds(pl.multiple_of(i * ROWS, ROWS), ROWS)
            wt[i] = w2[w, :].T

        _()

    for i in (0, 1):
        for q in range(SLICES):

            @pl.when(c + 2 * i != z)
            def _():
                z_wait(i, q)

            x_copy(i, q).start()
            c_copy(i, q, False).start()
            if q > 0:
                x_copy(i, q - 1, False).wait_recv()
                c_copy(i, q - 1, True).start()
            elif i > 0:
                x_copy(i - 1, SLICES - 1, False).wait_recv()
                c_copy(i - 1, SLICES - 1, True).start()
        if i == 1:
            for xs in (0, 1):
                turn(2 * c + xs)
    x_copy(1, SLICES - 1, False).wait_recv()
    c_copy(1, SLICES - 1, True).start()
    for i in (0, 1):
        for other in (False, True):
            for q in range(SLICES):
                c_copy(i, q, other, False).wait_recv()
        for xs in (0, 1):
            turn(2 * (1 - c + 2 * i) + xs)
    for xs in (0, 1):
        turn(2 * (c + 2) + xs)
    for d in (1, 2, 3):
        for n in (1, 2, 3, 4):
            group_wait(d, n)

    def far_copy(sender=True):
        first = 4 * p if sender else 4 * (1 - p)
        part = wo.at[pl.ds(first, 4), shard]
        return remote(part, part, o_send.at[0], o_recv.at[0], far)

    def over_copy(sender=True):
        part = wo.at[:, 2 * x + c if sender else 2 * (1 - x) + c]
        return remote(part, part, o_send.at[1], o_recv.at[1], across)

    def twin_copy(xs, sender=True):
        part = wo.at[:, 2 * xs + (c if sender else 1 - c)]
        return remote(part, part, o_send.at[2 + xs], o_recv.at[2 + xs], twin)

    def h_copy(t, part, xb, d, sender=True):
        there = peers[d]
        rows = pl.ds(part * PART, PART)
        at = mine[xb] if sender else stripe(there["y"], there["zi"], xb)
        block = hx.at[t + 1, rows, cols(at)]
        return remote(block, block, h_send.at[t, part, xb, d - 1], h_recv.at[t, part, xb, d - 1], there["dev"])

    def forward(t, part):
        rows = pl.ds(part * PART, PART)
        for xb in (0, 1):

            def pre(g):
                return dot(hx[t, rows, :], wt[2 * g + xb])

            gate_i = jax.nn.sigmoid(pre(0))
            act[t, xb, rows] = gate_i
            gate_f = jax.nn.sigmoid(pre(1))
            act[t, 2 + xb, rows] = gate_f
            gate_g = jnp.tanh(pre(2))
            act[t, 4 + xb, rows] = gate_g
            gate_o = jax.nn.sigmoid(pre(3))
            act[t, 6 + xb, rows] = gate_o
            cell = gate_f * call[t, xb, rows] + gate_i * gate_g
            call[t + 1, xb, rows] = cell
            hx[t + 1, rows, cols(mine[xb])] = (gate_o * jnp.tanh(cell)).astype(BF16)
            for d in (3, 1, 2):
                h_copy(t, part, xb, d).start()

    def h_wait(t, part):
        for xb in (0, 1):
            for d in (1, 2, 3):
                h_copy(t, part, xb, d, False).wait_recv()

    part_lanes = lax.broadcasted_iota(jnp.int32, (PART, CHARS), 1)
    part_rows = lax.broadcasted_iota(jnp.int32, (PART, 1), 0)
    totals = dict(loss=jnp.zeros((1, 1), F32), bias=jnp.zeros((1, CHARS), F32))

    def decode(t, part):
        rows = pl.ds(part * PART, PART)
        logits = dot(hx[t + 1, rows, pl.ds(0, HID)], wo[...].reshape(HID, CHARS)) + dbias[0:1, :]
        top = jnp.max(logits, axis=1, keepdims=True)
        grown = jnp.exp(logits - top)
        total = jnp.sum(grown, axis=1, keepdims=True)
        hit = metas[rows, STEPS + t : STEPS + t + 1] == part_lanes
        picked = jnp.sum(jnp.where(hit, logits, 0.0), axis=1, keepdims=True)
        low = ((grown / total - jnp.where(hit, 1.0, 0.0)) / STEPS).astype(BF16)
        dlog[t, rows] = low
        at = part_rows + part * PART
        ours = (at >= k * 64) & (at < k * 64 + 64)
        term = jnp.where(ours, (top + jnp.log(total) - picked) / STEPS, 0.0)
        totals["loss"] = totals["loss"] + jnp.sum(term, axis=0, keepdims=True)
        totals["bias"] = totals["bias"] + jnp.sum(jnp.where(ours, low.astype(F32), 0.0), axis=0, keepdims=True)

    far_copy().start()
    for part in range(SPLIT):
        forward(0, part)
    far_copy(False).wait_recv()
    over_copy().start()
    for part in range(SPLIT):
        h_wait(0, part)
        forward(1, part)
    over_copy(False).wait_recv()
    for xs in (0, 1):
        twin_copy(xs).start()
    for part in range(SPLIT):
        h_wait(1, part)
        forward(2, part)
    for xs in (0, 1):
        twin_copy(xs, False).wait_recv()
    for part in range(SPLIT):
        decode(0, part)
    for part in range(SPLIT):
        h_wait(2, part)
        forward(3, part)
    for part in range(SPLIT):
        decode(1, part)
    hx_out = pltpu.make_async_copy(hx.at[pl.ds(0, STEPS)], hx_o, out_sem.at[0])
    hx_out.start()
    for part in range(SPLIT):
        decode(2, part)

    emb[...] = jnp.zeros_like(emb)
    gdec_o[...] = jnp.zeros_like(gdec_o)
    dcn[...] = jnp.zeros_like(dcn)

    def b_copy(t, part, d):
        rows = pl.ds(part * PART, PART)
        return remote(
            pbuf.at[t - 1, d - 1, rows],
            rbuf.at[t - 1, d - 1, rows],
            b_send.at[t - 1, part, d - 1],
            b_recv.at[t - 1, part, d - 1],
            peers[d]["dev"],
        )

    def backward(t, part):
        rows = pl.ds(part * PART, PART)
        if t < STEPS - 1:
            for d in (1, 2, 3):
                b_copy(t + 1, part, d).wait_recv()
        for xb in (0, 1):
            dh = dot_nt(dlog[t, rows], wo[mine[xb]].reshape(ROWS, CHARS))
            wide = pl.ds(xb * ROWS, ROWS)
            if t < STEPS - 1:
                dh = dh + ownp[rows, wide]
                for d in (1, 2, 3):
                    dh = dh + rbuf[t, d - 1, rows, wide].astype(F32)
            gate_i = act[t, xb, rows]
            gate_f = act[t, 2 + xb, rows]
            gate_g = act[t, 4 + xb, rows]
            gate_o = act[t, 6 + xb, rows]
            shown = jnp.tanh(call[t + 1, xb, rows])
            dc = dcn[xb, rows] + dh * gate_o * (1.0 - shown * shown)
            dcn[xb, rows] = dc * gate_f
            dg[t, rows, pl.ds(xb * ROWS, ROWS)] = (dc * gate_g * gate_i * (1.0 - gate_i)).astype(BF16)
            dg[t, rows, pl.ds((2 + xb) * ROWS, ROWS)] = (
                dc * call[t, xb, rows] * gate_f * (1.0 - gate_f)
            ).astype(BF16)
            dg[t, rows, pl.ds((4 + xb) * ROWS, ROWS)] = (dc * gate_i * (1.0 - gate_g * gate_g)).astype(BF16)
            dg[t, rows, pl.ds((6 + xb) * ROWS, ROWS)] = (dh * shown * gate_o * (1.0 - gate_o)).astype(BF16)
        if t > 0:
            for d in (3, 1, 2):
                there = peers[d]
                for xb in (0, 1):
                    pbuf[t - 1, d - 1, rows, pl.ds(xb * ROWS, ROWS)] = dot(
                        dg[t, rows, :], w2[:, cols(stripe(there["y"], there["zi"], xb))]
                    ).astype(BF16)
                b_copy(t, part, d).start()
            for xb in (0, 1):
                ownp[rows, pl.ds(xb * ROWS, ROWS)] = dot(dg[t, rows, :], w2[:, cols(mine[xb])])
        else:

            def unit(j, carry):
                dh0_o[rows, cols(j)] = dot(dg[0, rows, :], w2[:, cols(j)])
                return carry

            lax.fori_loop(0, HID // ROWS, unit, 0)

    def extras(t):
        dx = dot(dg[t], w2[:, pl.ds(HID, WIDE - HID)])
        high = dx.astype(BF16)
        rest = (dx - high.astype(F32)).astype(BF16)
        one = jnp.where(metas[:, t : t + 1] == lanes, 1.0, 0.0).astype(BF16)
        emb[...] += dot_tn(one, high) + dot_tn(one, rest)
        for xb in (0, 1):
            gdec_o[pl.ds(xb * ROWS, ROWS), :] += dot_tn(hx[t + 1, :, cols(mine[xb])], dlog[t])

    for part in range(SPLIT):
        h_wait(STEPS - 1, part)
        decode(STEPS - 1, part)
        backward(STEPS - 1, part)
    extras(STEPS - 1)
    dg_out = [pltpu.make_async_copy(dg.at[t], dg_o.at[t], out_sem.at[1 + t]) for t in range(STEPS)]
    dg_out[STEPS - 1].start()
    for t in reversed(range(STEPS - 1)):
        for part in range(SPLIT):
            backward(t, part)
        dg_out[t].start()
        extras(t)

    for xb in (0, 1):
        dc0_o[:, pl.ds(xb * ROWS, ROWS)] = dcn[xb]
    at_row = lax.broadcasted_iota(jnp.int32, (288, 128), 0)
    at_col = lax.broadcasted_iota(jnp.int32, (288, 128), 1)
    block = jnp.where((at_row < 275) & (at_col < INPUTS), emb[pl.ds(0, 288), :], 0.0)
    for n in range(3):
        block = jnp.where(at_row == 276 + n, totals["bias"][:, n * 128 : n * 128 + 128], block)
    block = jnp.where((at_row == 279) & (at_col == 0), totals["loss"], block)
    emb_o[...] = block

    for q in range(SLICES):
        for target in (0, 1):

            @pl.when(c + 2 * target != z)
            def _():
                z_copy(target, q).wait_send()

        for i in (0, 1):
            x_copy(i, q).wait_send()
            c_copy(i, q, False).wait_send()
            c_copy(i, q, True).wait_send()
    for copy in group:
        copy.wait_send()
    far_copy().wait_send()
    over_copy().wait_send()
    for xs in (0, 1):
        twin_copy(xs).wait_send()
    for t in range(STEPS):
        for part in range(SPLIT):
            for d in (1, 2, 3):
                for xb in (0, 1):
                    h_copy(t, part, xb, d).wait_send()
                if t > 0:
                    b_copy(t, part, d).wait_send()
    hx_out.wait()
    for t in range(STEPS):
        dg_out[t].wait()


def sum_kernel(
    dg,
    hx,
    dh0,
    dc0,
    emb,
    gdec,
    grad_o,
    gdec_o,
    emb_o,
    norm_o,
    gh_o,
    gc_o,
    c_out,
    c_in,
    kept,
    x_out,
    x_in,
    z_out,
    z_in,
    gh_out,
    gh_in,
    gc_out,
    gc_in,
    d_out,
    d_in,
    f_out,
    f_in,
    e_in,
    n_out,
    n_in,
    c_send,
    c_recv,
    x_send,
    x_recv,
    z_send,
    z_recv,
    g_send,
    g_recv,
    d_send,
    d_recv,
    f_send,
    f_recv,
    e_send,
    e_recv,
    n_send,
    n_recv,
):
    s = spots()
    z, y, x, c, k, zi, p = s["z"], s["y"], s["x"], s["c"], s["k"], s["zi"], s["p"]
    dp, shard = s["dp"], s["shard"]
    across = device(s, x=1 - x)
    twin = device(s, c=1 - c)
    far = device(s, z=2 * (1 - p) + zi)
    peers = {d: peer(s, d) for d in (1, 2, 3)}
    core = z % 2
    column = [(dz, dc) for dz in range(4) for dc in range(2) if (dz, dc) != (0, 0)]
    plane = [(dy, dx) for dy in range(2) for dx in range(2) if (dy, dx) != (0, 0)]
    quad = [(dx, dc) for dx in range(2) for dc in range(2) if (dx, dc) != (0, 0)]

    def flip(value, by):
        return 1 - value if by else value

    def column_to(dz, dc):
        return device(s, z=(z + dz) % 4, c=flip(c, dc))

    def column_from(dz, dc):
        return device(s, z=(z + 4 - dz) % 4, c=flip(c, dc))

    def plane_to(dy, dx):
        return device(s, y=flip(y, dy), x=flip(x, dx))

    def quad_to(dx, dc):
        return device(s, x=flip(x, dx), c=flip(c, dc))

    def final_to(xb):
        return 4 * y + 2 * xb + zi

    def final_from(half):
        return 4 * half + 2 * y + p

    for dz, dc in column:
        signal(column_from(dz, dc))
    for dy, dx in plane:
        signal(plane_to(dy, dx))
    signal(quad_to(1, 1))
    signal(peers[3]["dev"])
    away = 0
    for n in (0, 1):

        @pl.when(final_from(n) != dp)
        def _():
            signal((final_from(n), shard))

        away = away + jnp.where(final_to(n) != dp, 1, 0)
    pl.semaphore_wait(pltpu.get_barrier_semaphore(), 12 + away)

    def state_copies(d, sender=True):
        there = peers[d]
        rows = aligned(there["k"] * 64, 64)
        result = [
            remote(gh_out.at[d - 1], gh_in.at[d - 1], g_send.at[d - 1, 0], g_recv.at[d - 1, 0], there["dev"]),
            remote(gc_out.at[d - 1], gc_in.at[d - 1], g_send.at[d - 1, 1], g_recv.at[d - 1, 1], there["dev"]),
        ]
        return result

    def d_copy(n, sender=True):
        dx, dc = quad[n]
        return remote(d_out.at[n], d_in.at[n], d_send.at[n], d_recv.at[n], quad_to(dx, dc))

    def early():
        for d in (3, 1, 2):
            rows = aligned(peers[d]["k"] * 64, 64)
            gh_out[d - 1] = dh0[rows, :].astype(BF16)
            gc_out[d - 1] = dc0[rows, :]
            for copy in state_copies(d):
                copy.start()
        for n, (dx, dc) in enumerate(quad):
            theirs = 2 * flip(x, dx) + flip(c, dc)
            for xb in (0, 1):
                d_out[n, xb] = gdec[aligned(xb * ROWS + theirs * 64, 64), :].astype(BF16)
            d_copy(n).start()

    tiles = ((0, 512), (512, 512), (1024, 512), (1536, 640))

    def block_of(b, store):
        for start, size in tiles:
            at = pl.ds(start, size)
            store(at, dot_tn(dg[:, cols(b)], hx[:, at]))

    def c_copy(n, q):
        rows = pl.ds(q * SLICE, SLICE)
        return remote(c_out.at[n, rows], c_in.at[n, rows], c_send.at[n, q], c_recv.at[n, q], twin)

    def x_copy(i, q):
        rows = pl.ds(q * SLICE, SLICE)
        return remote(x_out.at[i, rows], x_in.at[i, rows], x_send.at[i, q], x_recv.at[i, q], across)

    def z_copy(i, q):
        rows = pl.ds(q * SLICE, SLICE)
        return remote(
            z_out.at[i, rows],
            z_in.at[p, rows],
            z_send.at[i, q],
            z_recv.at[p, q],
            device(s, z=c + 2 * i, c=core),
        )

    def z_wait(n, q):
        rows = pl.ds(q * SLICE, SLICE)
        remote(z_out.at[n, rows], z_in.at[n, rows], z_send.at[n, q], z_recv.at[n, q], across).wait_recv()

    def for_twin(n, b):
        def store(at, value):
            c_out[n, :, at] = value.astype(BF16)

        block_of(b, store)
        for q in range(SLICES):
            c_copy(n, q).start()

    def keep(i, b):
        def store(at, value):
            kept[i, :, at] = value

        block_of(b, store)

    def add_twin(i, n, q):
        rows = pl.ds(q * SLICE, SLICE)
        c_copy(n, q).wait_recv()
        return kept[i, rows] + c_in[n, rows].astype(F32)

    for i in (0, 1):
        for_twin(i, 2 * (1 - c + 2 * i) + 1 - x)
        keep(0, 2 * (c + 2 * i) + 1 - x)
        for q in range(SLICES):
            x_out[i, pl.ds(q * SLICE, SLICE)] = add_twin(0, i, q).astype(BF16)
            x_copy(i, q).start()
        if i == 0:
            early()
    for i in (0, 1):
        for_twin(2 + i, 2 * (1 - c + 2 * i) + x)
        keep(i, 2 * (c + 2 * i) + x)

    half = aligned(c * 144, 144)
    rest = aligned((1 - c) * 144, 144)
    hops = (twin, across, peers[1]["dev"], peers[2]["dev"], far, twin)

    def e_copy(n):
        if n == 0:
            return remote(emb_o.at[rest], e_in.at[0], e_send.at[0], e_recv.at[0], hops[0])
        if n == 5:
            return remote(emb_o.at[half], e_in.at[5], e_send.at[5], e_recv.at[5], hops[5])
        return remote(e_out_of(n), e_in.at[n], e_send.at[n], e_recv.at[n], hops[n])

    def e_out_of(n):
        return e_in.at[5 + n]

    def e_start(n):
        if n in (1, 2, 3, 4):
            e_in[5 + n] = emb_o[half, :]
        e_copy(n).start()

    def e_finish(n):
        if n == 5:
            e_copy(5).wait()
            emb_o[rest, :] = e_in[5]
            return
        e_copy(n).wait()
        emb_o[half, :] = emb_o[half, :] + e_in[n]

    emb_o[...] = emb[...]
    e_start(0)

    def f_copy(xb):
        return remote(f_out.at[xb], f_in.at[p], f_send.at[xb], f_recv.at[p], (final_to(xb), shard))

    def f_wait(n):
        remote(f_out.at[n], f_in.at[n], f_send.at[n], f_recv.at[n], across).wait_recv()

    def decoder_middle():
        for n in range(3):
            d_copy(n).wait_recv()
        for xb in (0, 1):
            part = gdec[aligned(xb * ROWS + shard * 64, 64), :]
            for n in range(3):
                part = part + d_in[n, xb].astype(F32)
            f_out[xb] = part.astype(BF16)

            @pl.when(final_to(xb) != dp)
            def _():
                f_copy(xb).start()

            @pl.when(final_to(xb) == dp)
            def _():
                f_in[p] = part.astype(BF16)

    for i in (0, 1):
        for q in range(SLICES):
            rows = pl.ds(q * SLICE, SLICE)
            x_copy(i, q).wait_recv()
            total = add_twin(i, 2 + i, q) + x_in[i, rows].astype(F32)
            z_out[i, rows] = total.astype(BF16)

            @pl.when(c + 2 * i != z)
            def _():
                z_copy(i, q).start()

            @pl.when(c + 2 * i == z)
            def _():
                z_in[p, rows] = z_out[i, rows]

            stage = i * SLICES + q
            if stage == 0:
                decoder_middle()
            if 1 <= stage <= 6:
                e_finish(stage - 1)
                if stage < 6:
                    e_start(stage)

    squares = jnp.zeros((1, 1), F32)

    def square_sum(value):
        return jnp.sum(jnp.sum(value * value, axis=1, keepdims=True), axis=0, keepdims=True)

    for n in (0, 1):

        @pl.when(final_from(n) != dp)
        def _():
            f_wait(n)

    final = f_in[0].astype(F32) + f_in[1].astype(F32)
    gdec_o[...] = final
    squares = squares + square_sum(final)
    for q in range(SLICES):
        rows = pl.ds(q * SLICE, SLICE)
        for n in (0, 1):

            @pl.when(jnp.logical_or(core != c, p != n))
            def _():
                z_wait(n, q)

        final = z_in[0, rows].astype(F32) + z_in[1, rows].astype(F32)
        grad_o[rows, :] = final
        squares = squares + square_sum(final)

    def n_copy(n):
        if n < 7:
            return remote(n_out.at[0], n_in.at[n], n_send.at[n], n_recv.at[n], column_to(*column[n]))
        return remote(n_out.at[1], n_in.at[n], n_send.at[n], n_recv.at[n], plane_to(*plane[n - 7]))

    n_out[0] = jnp.broadcast_to(squares, (8, 128))
    for n in range(7):
        n_copy(n).start()
    own = aligned(k * 64, 64)
    total = dh0[own, :]
    for d in (1, 2, 3):
        for copy in state_copies(d):
            copy.wait_recv()
        total = total + gh_in[d - 1].astype(F32)
    gh_o[...] = total
    for xb in (0, 1):
        gc_o[:, cols(stripe(y, zi, xb))] = dc0[own, pl.ds(xb * ROWS, ROWS)]
        for d in (1, 2, 3):
            there = peers[d]
            gc_o[:, cols(stripe(there["y"], there["zi"], xb))] = gc_in[d - 1, :, pl.ds(xb * ROWS, ROWS)]
    total = n_out[0]
    for n in range(7):
        n_copy(n).wait_recv()
        total = total + n_in[n]
    n_out[1] = total
    for n in range(7, 10):
        n_copy(n).start()
    at_row = lax.broadcasted_iota(jnp.int32, (288, 128), 0)
    shared = square_sum(jnp.where(at_row == 279, 0.0, emb_o[...]))
    for n in range(7, 10):
        n_copy(n).wait_recv()
        total = total + n_in[n]
    norm_o[...] = total + shared

    for n in range(4):
        for q in range(SLICES):
            c_copy(n, q).wait_send()
    for i in (0, 1):
        for q in range(SLICES):
            x_copy(i, q).wait_send()

            @pl.when(c + 2 * i != z)
            def _():
                z_copy(i, q).wait_send()

        @pl.when(final_to(i) != dp)
        def _():
            f_copy(i).wait_send()

    for d in (1, 2, 3):
        for copy in state_copies(d):
            copy.wait_send()
        d_copy(d - 1).wait_send()
    for n in range(10):
        n_copy(n).wait_send()


def split_local(
    char_ids,
    targets,
    hidden_start,
    cell_start,
    embedding,
    input_weight,
    hidden_weight,
    gate_bias,
    decoder_weight,
    decoder_bias,
    momentum_embed,
    momentum_input,
    momentum_hidden,
    momentum_gate,
    momentum_decoder,
    momentum_outbias,
):
    streams = char_ids.shape[0]
    vocab = embedding.shape[0]
    shape = jax.ShapeDtypeStruct
    wext = jnp.concatenate(
        [
            hidden_weight.astype(BF16),
            input_weight.astype(BF16),
            gate_bias.astype(BF16)[:, None],
            jnp.zeros((ROWS, WIDE - HID - INPUTS - 1), BF16),
        ],
        axis=1,
    )
    meta = jnp.pad(jnp.concatenate([char_ids, targets], axis=1), ((0, 0), (0, 120)))
    wout = jnp.pad(decoder_weight.astype(BF16), ((0, 0), (0, CHARS - vocab)))
    table = jnp.concatenate(
        [embedding.astype(BF16), jnp.ones((vocab, 1), BF16), jnp.zeros((vocab, WIDE - HID - INPUTS - 1), BF16)],
        axis=1,
    )
    table = jnp.pad(table, ((0, CHARS - vocab), (0, 0)))
    dbias = jnp.broadcast_to(
        jnp.pad(decoder_bias, (0, CHARS - vocab), constant_values=-1e30)[None, :], (8, CHARS)
    )
    vm = pl.BlockSpec(memory_space=pltpu.VMEM)
    hbm = pl.BlockSpec(memory_space=pl.ANY)
    dma = pltpu.SemaphoreType.DMA
    hx, dg, dh0, dc0, emb, gdec = pl.pallas_call(
        step_kernel,
        out_shape=(
            shape((STEPS, ROWS, WIDE), BF16),
            shape((STEPS, ROWS, HID), BF16),
            shape((ROWS, HID), F32),
            shape((ROWS, 512), F32),
            shape((288, 128), F32),
            shape((512, CHARS), F32),
        ),
        in_specs=[vm] * 7,
        out_specs=(hbm, hbm, vm, vm, vm, vm),
        scratch_shapes=[
            pltpu.VMEM((HID, WIDE), BF16),
            pltpu.VMEM((8, WIDE, ROWS), BF16),
            pltpu.VMEM((STEPS + 1, ROWS, WIDE), BF16),
            pltpu.VMEM((STEPS, 8, ROWS, ROWS), F32),
            pltpu.VMEM((STEPS + 1, 2, ROWS, ROWS), F32),
            pltpu.VMEM((STEPS, ROWS, HID), BF16),
            pltpu.VMEM((STEPS - 1, 3, ROWS, 512), BF16),
            pltpu.VMEM((STEPS - 1, 3, ROWS, 512), BF16),
            pltpu.VMEM((ROWS, 512), F32),
            pltpu.VMEM((2, ROWS, ROWS), F32),
            pltpu.VMEM((8, 4, 64, CHARS), BF16),
            pltpu.VMEM((STEPS, ROWS, CHARS), BF16),
            pltpu.VMEM((ROWS, 128), jnp.int32),
            pltpu.VMEM((CHARS, 128), F32),
            dma((3, 5)),
            dma((3, 5)),
            dma((2, SLICES)),
            dma((2, SLICES)),
            dma((2, SLICES)),
            dma((2, SLICES)),
            dma((2, 2, SLICES)),
            dma((2, 2, SLICES)),
            dma((4,)),
            dma((4,)),
            dma((STEPS, SPLIT, 2, 3)),
            dma((STEPS, SPLIT, 2, 3)),
            dma((STEPS - 1, SPLIT, 3)),
            dma((STEPS - 1, SPLIT, 3)),
            dma((1 + STEPS,)),
        ],
        compiler_params=pltpu.CompilerParams(
            collective_id=0, has_side_effects=True, vmem_limit_bytes=60 * 2**20
        ),
    )(wext, hidden_start.astype(BF16), cell_start, meta, wout, table, dbias)
    grad, gdec_own, emb, norm, grad_hidden_start, grad_cell_start = pl.pallas_call(
        sum_kernel,
        out_shape=(
            shape((ROWS, WIDE), F32),
            shape((64, CHARS), F32),
            shape((288, 128), F32),
            shape((8, 128), F32),
            shape((64, HID), F32),
            shape((64, HID), F32),
        ),
        in_specs=[vm] * 6,
        out_specs=(vm,) * 6,
        scratch_shapes=[
            pltpu.VMEM((4, ROWS, WIDE), BF16),
            pltpu.VMEM((4, ROWS, WIDE), BF16),
            pltpu.VMEM((2, ROWS, WIDE), F32),
            pltpu.VMEM((2, ROWS, WIDE), BF16),
            pltpu.VMEM((2, ROWS, WIDE), BF16),
            pltpu.VMEM((2, ROWS, WIDE), BF16),
            pltpu.VMEM((2, ROWS, WIDE), BF16),
            pltpu.VMEM((3, 64, HID), BF16),
            pltpu.VMEM((3, 64, HID), BF16),
            pltpu.VMEM((3, 64, 512), F32),
            pltpu.VMEM((3, 64, 512), F32),
            pltpu.VMEM((3, 2, 64, CHARS), BF16),
            pltpu.VMEM((3, 2, 64, CHARS), BF16),
            pltpu.VMEM((2, 64, CHARS), BF16),
            pltpu.VMEM((2, 64, CHARS), BF16),
            pltpu.VMEM((10, 144, 128), F32),
            pltpu.VMEM((2, 8, 128), F32),
            pltpu.VMEM((10, 8, 128), F32),
            dma((4, SLICES)),
            dma((4, SLICES)),
            dma((2, SLICES)),
            dma((2, SLICES)),
            dma((2, SLICES)),
            dma((2, SLICES)),
            dma((3, 2)),
            dma((3, 2)),
            dma((3,)),
            dma((3,)),
            dma((2,)),
            dma((2,)),
            dma((6,)),
            dma((6,)),
            dma((10,)),
            dma((10,)),
        ],
        compiler_params=pltpu.CompilerParams(
            collective_id=1, has_side_effects=True, vmem_limit_bytes=60 * 2**20
        ),
    )(dg.reshape(STEPS * ROWS, HID), hx.reshape(STEPS * ROWS, WIDE), dh0, dc0, emb, gdec)
    grad_norm = jnp.sqrt(norm[0:1, 0])
    factor = CLIP / jnp.maximum(grad_norm[0], CLIP)
    streams_all = streams * lax.axis_size("dp") * lax.axis_size("shard")
    loss = emb[279, 0:1] / streams_all
    grads = (
        emb[:vocab, :INPUTS],
        grad[:, HID : HID + INPUTS],
        grad[:, :HID],
        grad[:, HID + INPUTS],
        gdec_own[:, :vocab],
        emb[276:279].reshape(-1)[:vocab],
    )
    momenta = (
        momentum_embed,
        momentum_input,
        momentum_hidden,
        momentum_gate,
        momentum_decoder,
        momentum_outbias,
    )
    updated = tuple(MOMENTUM * momenta[n] + factor * grads[n] for n in range(6))
    return (loss, grad_norm, grad_hidden_start, grad_cell_start) + grads + updated


def solution(mesh):
    fits = mesh.shape["dp"] == 8 and mesh.shape["shard"] == 4
    placed = (
        P(("dp", "shard"), None),
        P(("dp", "shard"), None),
        P(("dp", "shard"), None),
        P(("dp", "shard"), None),
        P(),
        P(("dp", "shard"), None),
        P(("dp", "shard"), None),
        P(("dp", "shard")),
        P(("dp", "shard"), None),
        P(),
        P(),
        P(("dp", "shard"), None),
        P(("dp", "shard"), None),
        P(("dp", "shard")),
        P(("dp", "shard"), None),
        P(),
    )
    return jax.shard_map(
        split_local if fits else local,
        mesh=mesh,
        in_specs=placed,
        out_specs=(
            P(),
            P(),
            P(("dp", "shard"), None),
            P(("dp", "shard"), None),
            P(),
            P(("dp", "shard"), None),
            P(("dp", "shard"), None),
            P(("dp", "shard")),
            P(("dp", "shard"), None),
            P(),
            P(),
            P(("dp", "shard"), None),
            P(("dp", "shard"), None),
            P(("dp", "shard")),
            P(("dp", "shard"), None),
            P(),
        ),
        check_vma=False,
    )
```

```python
import functools

import jax
import jax.numpy as jnp
from jax import lax
from jax.experimental import pallas as pl
from jax.experimental.pallas import tpu as pltpu
from jax.sharding import PartitionSpec as P

MESH = pl.DeviceIdType.MESH
F32 = jnp.float32
BF16 = jnp.bfloat16

MICRO = 2


CLIP = 0.25
MOMENTUM = 0.5


def contract_rows(left, right):
    return lax.dot_general(
        left, right, (((0,), (0,)), ((), ())), preferred_element_type=jnp.float32
    )


def contract_last(left, right):
    return lax.dot_general(
        left, right, (((1,), (1,)), ((), ())), preferred_element_type=jnp.float32
    )


def local(
    char_ids,
    targets,
    hidden_start,
    cell_start,
    embedding,
    input_weight,
    hidden_weight,
    gate_bias,
    decoder_weight,
    decoder_bias,
    momentum_embed,
    momentum_input,
    momentum_hidden,
    momentum_gate,
    momentum_decoder,
    momentum_outbias,
):
    streams, seq_len = char_ids.shape
    micro_rows = streams // MICRO
    vocab_size = embedding.shape[0]
    hidden_size = hidden_start.shape[1]
    low_input = input_weight.astype(jnp.bfloat16)
    low_hidden = hidden_weight.astype(jnp.bfloat16)
    low_bias = gate_bias.astype(jnp.bfloat16)
    low_decoder = decoder_weight.astype(jnp.bfloat16)
    inner_rows = (
        lax.all_gather(low_input, "shard", axis=0, tiled=True),
        lax.all_gather(low_hidden, "shard", axis=0, tiled=True),
        lax.all_gather(low_bias, "shard", axis=0, tiled=True),
        lax.all_gather(low_decoder, "shard", axis=0, tiled=True),
    )
    weight_in, weight_rec, bias_low, weight_out = (
        lax.all_gather(inner_rows[0], "dp", axis=0, tiled=True),
        lax.all_gather(inner_rows[1], "dp", axis=0, tiled=True),
        lax.all_gather(inner_rows[2], "dp", axis=0, tiled=True),
        lax.all_gather(inner_rows[3], "dp", axis=0, tiled=True),
    )
    columns = jnp.arange(vocab_size, dtype=jnp.int32)
    table = embedding.astype(jnp.bfloat16)
    bias_row = bias_low.astype(jnp.float32)[None, :]

    def forward_step(carried, input_now):
        hidden_low, cell = carried
        preact = input_now + contract_last(hidden_low, weight_rec)
        input_gate = jax.nn.sigmoid(preact[:, :hidden_size])
        forget_gate = jax.nn.sigmoid(preact[:, hidden_size : 2 * hidden_size])
        candidate = jnp.tanh(preact[:, 2 * hidden_size : 3 * hidden_size])
        output_gate = jax.nn.sigmoid(preact[:, 3 * hidden_size :])
        cell_next = forget_gate * cell + input_gate * candidate
        hidden_next = (output_gate * jnp.tanh(cell_next)).astype(jnp.bfloat16)
        activations = jnp.concatenate([input_gate, forget_gate, candidate, output_gate], axis=1)
        return ((hidden_next, cell_next), (hidden_low, cell, activations, cell_next, hidden_next))

    def backward_step(carried, inputs):
        hidden_grad_next, cell_grad_next = carried
        out_grad, cell_before, gate_values, cell_now = inputs
        hidden_grad = out_grad + hidden_grad_next
        input_gate = gate_values[:, :hidden_size]
        forget_gate = gate_values[:, hidden_size : 2 * hidden_size]
        candidate = gate_values[:, 2 * hidden_size : 3 * hidden_size]
        output_gate = gate_values[:, 3 * hidden_size :]
        cell_tanh = jnp.tanh(cell_now)
        cell_grad = cell_grad_next + hidden_grad * output_gate * (1.0 - cell_tanh * cell_tanh)
        input_term = cell_grad * candidate * input_gate * (1.0 - input_gate)
        forget_term = cell_grad * cell_before * forget_gate * (1.0 - forget_gate)
        candidate_term = cell_grad * input_gate * (1.0 - candidate * candidate)
        output_term = hidden_grad * cell_tanh * output_gate * (1.0 - output_gate)
        gate_grad = jnp.concatenate(
            [input_term, forget_term, candidate_term, output_term], axis=1
        ).astype(jnp.bfloat16)
        hidden_grad_prev = jnp.dot(gate_grad, weight_rec, preferred_element_type=jnp.float32)
        return ((hidden_grad_prev, cell_grad * forget_gate), gate_grad)

    def micro_pass(loss_total, inputs):
        ids_part, target_part, hidden_part, cell_part = inputs
        batch_rows = ids_part.shape[0]
        token_ids = ids_part.T.reshape(-1)
        token_targets = target_part.T.reshape(-1)
        one_input = (token_ids[:, None] == columns[None, :]).astype(jnp.bfloat16)
        one_target = (token_targets[:, None] == columns[None, :]).astype(jnp.float32)
        embedded = jnp.dot(one_input, table, preferred_element_type=jnp.float32).astype(
            jnp.bfloat16
        )
        input_part = contract_last(embedded, weight_in) + bias_row
        input_part = input_part.reshape(seq_len, batch_rows, 4 * hidden_size)
        start_pair = (hidden_part.astype(jnp.bfloat16), cell_part)
        final_pair, saved = lax.scan(forward_step, start_pair, input_part)
        hidden_prev, cell_prev, activations, cell_after, hidden_after = saved
        hidden_rows = hidden_after.reshape(seq_len * batch_rows, hidden_size)
        logits = (
            jnp.dot(hidden_rows, weight_out, preferred_element_type=jnp.float32)
            + decoder_bias[None, :]
        )
        log_total = jax.nn.logsumexp(logits, axis=1)
        local_loss = jnp.sum(log_total - jnp.sum(one_target * logits, axis=1)) / seq_len
        probs = jnp.exp(logits - log_total[:, None])
        logit_grad = ((probs - one_target) / seq_len).astype(jnp.bfloat16)
        hidden_from_out = contract_last(logit_grad, weight_out).reshape(
            seq_len, batch_rows, hidden_size
        )
        zero_state = jnp.zeros((batch_rows, hidden_size), jnp.float32)
        start_grads, gate_grads = lax.scan(
            backward_step,
            (zero_state, zero_state),
            (hidden_from_out, cell_prev, activations, cell_after),
            reverse=True,
        )
        gate_rows = gate_grads.reshape(seq_len * batch_rows, 4 * hidden_size)
        prev_rows = hidden_prev.reshape(seq_len * batch_rows, hidden_size)
        return (
            loss_total + local_loss,
            (
                token_ids,
                embedded,
                logit_grad,
                hidden_rows,
                gate_rows,
                prev_rows,
                start_grads[0],
                start_grads[1],
            ),
        )

    def by_micro(array):
        return array.reshape((MICRO, micro_rows) + array.shape[1:])

    local_loss, stacked = lax.scan(
        micro_pass,
        jnp.zeros((), jnp.float32),
        (by_micro(char_ids), by_micro(targets), by_micro(hidden_start), by_micro(cell_start)),
    )
    token_ids, embedded, logit_grad, hidden_rows, gate_rows, prev_rows, hidden_grads, cell_grads = (
        stacked
    )
    token_ids = token_ids.reshape(-1)
    embedded = embedded.reshape(-1, embedded.shape[-1])
    logit_grad = logit_grad.reshape(-1, vocab_size)
    hidden_rows = hidden_rows.reshape(-1, hidden_size)
    gate_rows = gate_rows.reshape(-1, 4 * hidden_size)
    prev_rows = prev_rows.reshape(-1, hidden_size)
    grad_hidden_start = hidden_grads.reshape(streams, hidden_size)
    grad_cell_start = cell_grads.reshape(streams, hidden_size)
    grad_outbias_local = jnp.sum(logit_grad.astype(jnp.float32), axis=0)
    grad_decoder_local = contract_rows(hidden_rows, logit_grad)
    grad_input_local = contract_rows(gate_rows, embedded)
    grad_hidden_local = contract_rows(gate_rows, prev_rows)
    grad_bias_local = jnp.sum(gate_rows.astype(jnp.float32), axis=0)
    embed_rows_grad = jnp.dot(gate_rows, weight_in, preferred_element_type=jnp.float32)
    one_all = (token_ids[:, None] == columns[None, :]).astype(jnp.float32)
    grad_embed_local = lax.dot_general(
        one_all,
        embed_rows_grad,
        (((0,), (0,)), ((), ())),
        precision=lax.Precision.HIGHEST,
        preferred_element_type=jnp.float32,
    )
    grad_embedding, grad_decoder_bias, loss_sum = lax.psum(
        (grad_embed_local, grad_outbias_local, local_loss), ("dp", "shard")
    )
    outer_sums = (
        lax.psum_scatter(
            grad_input_local.astype(jnp.bfloat16), "dp", scatter_dimension=0, tiled=True
        ).astype(jnp.float32),
        lax.psum_scatter(
            grad_hidden_local.astype(jnp.bfloat16), "dp", scatter_dimension=0, tiled=True
        ).astype(jnp.float32),
        lax.psum_scatter(
            grad_bias_local.astype(jnp.bfloat16), "dp", scatter_dimension=0, tiled=True
        ).astype(jnp.float32),
        lax.psum_scatter(
            grad_decoder_local.astype(jnp.bfloat16), "dp", scatter_dimension=0, tiled=True
        ).astype(jnp.float32),
    )
    grad_input_weight, grad_hidden_weight, grad_gate_bias, grad_decoder_weight = (
        lax.psum_scatter(
            outer_sums[0].astype(jnp.bfloat16), "shard", scatter_dimension=0, tiled=True
        ).astype(jnp.float32),
        lax.psum_scatter(
            outer_sums[1].astype(jnp.bfloat16), "shard", scatter_dimension=0, tiled=True
        ).astype(jnp.float32),
        lax.psum_scatter(
            outer_sums[2].astype(jnp.bfloat16), "shard", scatter_dimension=0, tiled=True
        ).astype(jnp.float32),
        lax.psum_scatter(
            outer_sums[3].astype(jnp.bfloat16), "shard", scatter_dimension=0, tiled=True
        ).astype(jnp.float32),
    )
    shard_squares = jnp.sum(grad_input_weight * grad_input_weight) + jnp.sum(
        grad_hidden_weight * grad_hidden_weight
    )
    shard_squares = (
        shard_squares
        + jnp.sum(grad_gate_bias * grad_gate_bias)
        + jnp.sum(grad_decoder_weight * grad_decoder_weight)
    )
    square_total = lax.psum(shard_squares, ("dp", "shard"))
    square_total = (
        square_total
        + jnp.sum(grad_embedding * grad_embedding)
        + jnp.sum(grad_decoder_bias * grad_decoder_bias)
    )
    grad_norm = jnp.sqrt(square_total)
    factor = CLIP / jnp.maximum(grad_norm, CLIP)
    streams_all = streams * lax.axis_size("dp") * lax.axis_size("shard")
    loss = loss_sum / streams_all
    momenta = (
        momentum_embed,
        momentum_input,
        momentum_hidden,
        momentum_gate,
        momentum_decoder,
        momentum_outbias,
    )
    weight_grads = (
        grad_embedding,
        grad_input_weight,
        grad_hidden_weight,
        grad_gate_bias,
        grad_decoder_weight,
        grad_decoder_bias,
    )
    new_momenta = [MOMENTUM * momenta[index] + factor * weight_grads[index] for index in range(6)]
    return (
        loss.reshape(1),
        grad_norm.reshape(1),
        grad_hidden_start,
        grad_cell_start,
        grad_embedding,
        grad_input_weight,
        grad_hidden_weight,
        grad_gate_bias,
        grad_decoder_weight,
        grad_decoder_bias,
        new_momenta[0],
        new_momenta[1],
        new_momenta[2],
        new_momenta[3],
        new_momenta[4],
        new_momenta[5],
    )


ROWS = 256
HID = 2048
WIDE = 2176
INPUTS = 100
CHARS = 384
SPLIT = 2
PART = ROWS // SPLIT
SLICES = 8
SLICE = ROWS // SLICES
STEPS = 4


def spots():
    dp = lax.axis_index("dp")
    shard = lax.axis_index("shard")
    return dict(
        p=dp // 4,
        zi=(dp // 2) % 2,
        z=dp // 2,
        y=dp % 2,
        k=dp % 4,
        x=shard // 2,
        c=shard % 2,
        dp=dp,
        shard=shard,
    )


def device(s, z=None, y=None, x=None, c=None):
    z = s["z"] if z is None else z
    y = s["y"] if y is None else y
    x = s["x"] if x is None else x
    c = s["c"] if c is None else c
    return (z * 2 + y, x * 2 + c)


def peer(s, d):
    y = 1 - s["y"] if d % 2 else s["y"]
    zi = 1 - s["zi"] if d // 2 else s["zi"]
    z = 2 * s["p"] + zi
    return dict(y=y, zi=zi, k=2 * zi + y, dev=(z * 2 + y, s["shard"]))


def stripe(y, zi, xb):
    return 4 * y + 2 * xb + zi


def cols(index):
    return pl.ds(pl.multiple_of(index * ROWS, ROWS), ROWS)


def aligned(start, size):
    return pl.ds(pl.multiple_of(start, size), size)


def remote(src, dst, send, recv, dev):
    return pltpu.make_async_remote_copy(
        src_ref=src, dst_ref=dst, send_sem=send, recv_sem=recv, device_id=dev, device_id_type=MESH
    )


def dot(left, right):
    return jnp.dot(left, right, preferred_element_type=F32)


def dot_nt(left, right):
    return lax.dot_general(left, right, (((1,), (1,)), ((), ())), preferred_element_type=F32)


def dot_tn(left, right):
    return lax.dot_general(left, right, (((0,), (0,)), ((), ())), preferred_element_type=F32)


def signal(dev):
    pl.semaphore_signal(
        pltpu.get_barrier_semaphore(), inc=1, device_id=dev, device_id_type=MESH
    )


def step_kernel(
    wext,
    h_own,
    cell_own,
    meta_own,
    wout_own,
    table,
    dbias,
    hx_o,
    dg_o,
    dh0_o,
    dc0_o,
    emb_o,
    gdec_o,
    w2,
    wt,
    hx,
    act,
    call,
    dg,
    pbuf,
    rbuf,
    ownp,
    dcn,
    wo,
    dlog,
    metas,
    emb,
    cells,
    dpart,
    d_out,
    d_in,
    f_out,
    f_in,
    g_send,
    g_recv,
    wz_send,
    wz_recv,
    wx_send,
    wx_recv,
    wc_send,
    wc_recv,
    o_send,
    o_recv,
    h_send,
    h_recv,
    b_send,
    b_recv,
    d_send,
    d_recv,
    f_send,
    f_recv,
    out_sem,
):
    s = spots()
    z, y, x, c, k, zi, p = s["z"], s["y"], s["x"], s["c"], s["k"], s["zi"], s["p"]
    dp, shard = s["dp"], s["shard"]
    across = device(s, x=1 - x)
    twin = device(s, c=1 - c)
    far = device(s, z=2 * (1 - p) + zi)
    peers = {d: peer(s, d) for d in (1, 2, 3)}
    mine = [stripe(y, zi, xb) for xb in (0, 1)]
    core = z % 2
    off_core = jnp.where(core == c, 0, 1)
    quad = [(dx, dc) for dx in range(2) for dc in range(2) if (dx, dc) != (0, 0)]

    def flip(value, by):
        return 1 - value if by else value

    def quad_to(dx, dc):
        return device(s, x=flip(x, dx), c=flip(c, dc))

    def final_to(xb):
        return 4 * y + 2 * xb + zi

    def final_from(half):
        return 4 * half + 2 * y + p

    for d in (1, 2, 3):
        signal(peers[d]["dev"])
    signal(across)
    signal(twin)
    signal(far)

    signal(device(s, x=1 - x, c=1 - c))

    @pl.when(core != c)
    def _():
        for i in (0, 1):
            signal(device(s, z=c + 2 * i, c=core))

    away = 0
    for n in (0, 1):

        @pl.when(final_from(n) != dp)
        def _():
            signal((final_from(n), shard))

        away = away + jnp.where(final_to(n) != dp, 1, 0)
    pl.semaphore_wait(pltpu.get_barrier_semaphore(), 7 + 2 * off_core + away)

    def z_copy(target, q):
        rows = pl.ds(q * SLICE, SLICE)
        slot = aligned((2 * z + x) * ROWS + q * SLICE, SLICE)
        return remote(
            wext.at[rows],
            w2.at[slot],
            wz_send.at[target, q],
            wz_recv.at[z // 2, q],
            device(s, z=c + 2 * target, c=core),
        )

    def z_wait(i, q):
        slot = aligned((2 * (c + 2 * i) + x) * ROWS + q * SLICE, SLICE)
        remote(wext.at[pl.ds(q * SLICE, SLICE)], w2.at[slot], wz_send.at[0, q], wz_recv.at[i, q], across).wait_recv()

    def x_copy(i, q, sender=True):
        xs = x if sender else 1 - x
        slot = aligned((2 * (c + 2 * i) + xs) * ROWS + q * SLICE, SLICE)
        return remote(w2.at[slot], w2.at[slot], wx_send.at[i, q], wx_recv.at[i, q], across)

    def c_copy(i, q, n, other, sender=True):
        xs = 1 - x if other else x
        cs = c if sender else 1 - c
        slot = aligned((2 * (cs + 2 * i) + xs) * ROWS + q * SLICE, SLICE)
        return remote(
            w2.at[slot], w2.at[slot], wc_send.at[n, int(other), q], wc_recv.at[n, int(other), q], twin
        )

    near = p
    beyond = 1 - p

    def start_beyond():
        for q in range(SLICES):

            @pl.when(c + 2 * beyond != z)
            def _():
                z_copy(beyond, q).start()

    pl.when(zi != p)(start_beyond)
    own = aligned(k * 64, 64)

    def group_copy(d, n):
        dev = peers[d]["dev"]
        send, recv = g_send.at[d - 1, n], g_recv.at[d - 1, n]
        if n == 0:
            return remote(meta_own, metas.at[own], send, recv, dev)
        if n == 1:
            return remote(h_own, hx.at[0, own, pl.ds(0, HID)], send, recv, dev)
        if n == 2:
            return remote(wout_own, wo.at[dp, shard], send, recv, dev)
        theirs = stripe(peers[d]["y"], peers[d]["zi"], n - 3)
        return remote(cell_own.at[:, cols(theirs)], cells.at[n - 3, own], send, recv, dev)

    def corner_copy(n, sender=True):
        there = peers[2 if sender else 3]
        rows = aligned(there["k"] * 64, 64)
        send, recv = g_send.at[2, n], g_recv.at[2, n]
        dev = peers[1]["dev"]
        if n == 0:
            part = metas.at[rows]
        elif n == 1:
            part = hx.at[0, rows, pl.ds(0, HID)]
        else:
            part = wo.at[there["dev"][0], shard]
        return remote(part, part, send, recv, dev)

    @pl.when(c + 2 * near == z)
    def _():
        w2[aligned((2 * z + x) * ROWS, ROWS), :] = wext[...]

    for q in range(SLICES):

        @pl.when(c + 2 * near != z)
        def _():
            z_copy(near, q).start()

        if q == 0:
            for n in (0, 2, 1):
                for d in (2, 1):
                    group_copy(d, n).start()
    for n in (3, 4):
        for d in (3, 2, 1):
            group_copy(d, n).start()
    pl.when(zi == p)(start_beyond)
    metas[own, :] = meta_own[...]
    hx[0, own, pl.ds(0, HID)] = h_own[...]
    wo[dp, shard] = wout_own[...]
    for xb in (0, 1):
        cells[xb, own] = cell_own[:, cols(mine[xb])]

    def group_wait(d, n):
        there = peers[d]
        rows = aligned(there["k"] * 64, 64)
        send, recv = g_send.at[d - 1, n], g_recv.at[d - 1, n]
        if n == 0:
            copy = remote(meta_own, metas.at[rows], send, recv, there["dev"])
        elif n == 1:
            copy = remote(h_own, hx.at[0, rows, pl.ds(0, HID)], send, recv, there["dev"])
        elif n == 2:
            copy = remote(wout_own, wo.at[there["dev"][0], shard], send, recv, there["dev"])
        else:
            copy = remote(cell_own.at[:, cols(mine[n - 3])], cells.at[n - 3, rows], send, recv, there["dev"])
        copy.wait_recv()

    lanes = lax.broadcasted_iota(jnp.int32, (ROWS, CHARS), 1)

    def turn(b):
        wt[b] = w2[cols(b), :].T

    order = [(n, q) for n in (0, 1) for q in range(SLICES)]
    gates = (p, 1 - p)
    for at, (n, q) in enumerate(order):
        i = gates[n]

        @pl.when(c + 2 * i != z)
        def _():
            z_wait(i, q)

        x_copy(i, q).start()
        c_copy(i, q, n, False).start()
        if at > 0:
            before, slot = order[at - 1]
            x_copy(gates[before], slot, False).wait_recv()
            c_copy(gates[before], slot, before, True).start()
        if n == 0 and q == SLICES - 1:
            for m in (0, 2, 1):
                group_wait(2, m)
                corner_copy(m).start()
        if n == 1 and q < 2:
            turn(2 * (c + 2 * p) + q)
        if n == 1 and q == 2:
            for other in (False, True):
                for slot in range(SLICES):
                    c_copy(p, slot, 0, other, False).wait_recv()
            for xs in (0, 1):
                turn(2 * (1 - c + 2 * p) + xs)
    x_copy(1 - p, SLICES - 1, False).wait_recv()
    c_copy(1 - p, SLICES - 1, 1, True).start()
    for xs in (0, 1):
        turn(2 * (c + 2 * (1 - p)) + xs)
    for other in (False, True):
        for q in range(SLICES):
            c_copy(1 - p, q, 1, other, False).wait_recv()
    for xs in (0, 1):
        turn(2 * (1 - c + 2 * (1 - p)) + xs)
    for n in (0, 1, 2):
        group_wait(1, n)
        corner_copy(n, False).wait_recv()
    for n in (3, 4):
        for d in (1, 2, 3):
            group_wait(d, n)
        call[0, n - 3] = cells[n - 3].astype(F32)
    for t in range(STEPS):
        one = jnp.where(metas[:, t : t + 1] == lanes, 1.0, 0.0).astype(BF16)
        hx[t, :, pl.ds(HID, WIDE - HID)] = dot(one, table[...]).astype(BF16)

    def far_copy(sender=True):
        first = 4 * p if sender else 4 * (1 - p)
        part = wo.at[pl.ds(first, 4), shard]
        return remote(part, part, o_send.at[0], o_recv.at[0], far)

    def over_copy(sender=True):
        part = wo.at[:, 2 * x + c if sender else 2 * (1 - x) + c]
        return remote(part, part, o_send.at[1], o_recv.at[1], across)

    def twin_copy(xs, sender=True):
        part = wo.at[:, 2 * xs + (c if sender else 1 - c)]
        return remote(part, part, o_send.at[2 + xs], o_recv.at[2 + xs], twin)

    def h_copy(t, part, xb, d, sender=True):
        there = peers[d]
        rows = pl.ds(part * PART, PART)
        at = mine[xb] if sender else stripe(there["y"], there["zi"], xb)
        block = hx.at[t + 1, rows, cols(at)]
        return remote(block, block, h_send.at[t, part, xb, d - 1], h_recv.at[t, part, xb, d - 1], there["dev"])

    def forward(t, part):
        rows = pl.ds(part * PART, PART)
        for xb in (0, 1):

            def pre(g):
                return dot(hx[t, rows, :], wt[2 * g + xb])

            gate_i = jax.nn.sigmoid(pre(0))
            act[t, xb, rows] = gate_i
            gate_f = jax.nn.sigmoid(pre(1))
            act[t, 2 + xb, rows] = gate_f
            gate_g = jnp.tanh(pre(2))
            act[t, 4 + xb, rows] = gate_g
            gate_o = jax.nn.sigmoid(pre(3))
            act[t, 6 + xb, rows] = gate_o
            cell = gate_f * call[t, xb, rows] + gate_i * gate_g
            call[t + 1, xb, rows] = cell
            hx[t + 1, rows, cols(mine[xb])] = (gate_o * jnp.tanh(cell)).astype(BF16)
            for d in (3, 1, 2):
                h_copy(t, part, xb, d).start()

    def h_wait(t, part):
        for xb in (0, 1):
            for d in (1, 2, 3):
                h_copy(t, part, xb, d, False).wait_recv()

    part_lanes = lax.broadcasted_iota(jnp.int32, (PART, CHARS), 1)
    part_rows = lax.broadcasted_iota(jnp.int32, (PART, 1), 0)
    totals = dict(loss=jnp.zeros((1, 1), F32), bias=jnp.zeros((1, CHARS), F32))

    def decode(t, part):
        rows = pl.ds(part * PART, PART)
        logits = dot(hx[t + 1, rows, pl.ds(0, HID)], wo[...].reshape(HID, CHARS)) + dbias[0:1, :]
        top = jnp.max(logits, axis=1, keepdims=True)
        grown = jnp.exp(logits - top)
        total = jnp.sum(grown, axis=1, keepdims=True)
        hit = metas[rows, STEPS + t : STEPS + t + 1] == part_lanes
        picked = jnp.sum(jnp.where(hit, logits, 0.0), axis=1, keepdims=True)
        low = ((grown / total - jnp.where(hit, 1.0, 0.0)) / STEPS).astype(BF16)
        dlog[t, rows] = low
        at = part_rows + part * PART
        ours = (at >= k * 64) & (at < k * 64 + 64)
        term = jnp.where(ours, (top + jnp.log(total) - picked) / STEPS, 0.0)
        totals["loss"] = totals["loss"] + jnp.sum(term, axis=0, keepdims=True)
        totals["bias"] = totals["bias"] + jnp.sum(jnp.where(ours, low.astype(F32), 0.0), axis=0, keepdims=True)

    far_copy().start()
    for part in range(SPLIT):
        forward(0, part)
    far_copy(False).wait_recv()
    over_copy().start()
    for part in range(SPLIT):
        h_wait(0, part)
        forward(1, part)
    over_copy(False).wait_recv()
    for xs in (0, 1):
        twin_copy(xs).start()
    for part in range(SPLIT):
        h_wait(1, part)
        forward(2, part)
    for xs in (0, 1):
        twin_copy(xs, False).wait_recv()
    for part in range(SPLIT):
        decode(0, part)
    for part in range(SPLIT):
        h_wait(2, part)
        forward(3, part)
    for part in range(SPLIT):
        decode(1, part)
    hx_out = pltpu.make_async_copy(hx.at[pl.ds(0, STEPS)], hx_o, out_sem.at[0])
    hx_out.start()
    for part in range(SPLIT):
        decode(2, part)

    emb[...] = jnp.zeros_like(emb)
    dcn[...] = jnp.zeros_like(dcn)

    def b_copy(t, part, d):
        rows = pl.ds(part * PART, PART)
        return remote(
            pbuf.at[t - 1, d - 1, rows],
            rbuf.at[t - 1, d - 1, rows],
            b_send.at[t - 1, part, d - 1],
            b_recv.at[t - 1, part, d - 1],
            peers[d]["dev"],
        )

    def backward(t, part):
        rows = pl.ds(part * PART, PART)
        if t < STEPS - 1:
            for d in (1, 2, 3):
                b_copy(t + 1, part, d).wait_recv()
        for xb in (0, 1):
            dh = dot_nt(dlog[t, rows], wo[mine[xb]].reshape(ROWS, CHARS))
            wide = pl.ds(xb * ROWS, ROWS)
            if t < STEPS - 1:
                dh = dh + ownp[rows, wide]
                for d in (1, 2, 3):
                    dh = dh + rbuf[t, d - 1, rows, wide].astype(F32)
            gate_i = act[t, xb, rows]
            gate_f = act[t, 2 + xb, rows]
            gate_g = act[t, 4 + xb, rows]
            gate_o = act[t, 6 + xb, rows]
            shown = jnp.tanh(call[t + 1, xb, rows])
            dc = dcn[xb, rows] + dh * gate_o * (1.0 - shown * shown)
            dcn[xb, rows] = dc * gate_f
            dg[t, rows, pl.ds(xb * ROWS, ROWS)] = (dc * gate_g * gate_i * (1.0 - gate_i)).astype(BF16)
            dg[t, rows, pl.ds((2 + xb) * ROWS, ROWS)] = (
                dc * call[t, xb, rows] * gate_f * (1.0 - gate_f)
            ).astype(BF16)
            dg[t, rows, pl.ds((4 + xb) * ROWS, ROWS)] = (dc * gate_i * (1.0 - gate_g * gate_g)).astype(BF16)
            dg[t, rows, pl.ds((6 + xb) * ROWS, ROWS)] = (dh * shown * gate_o * (1.0 - gate_o)).astype(BF16)
        if t > 0:
            for d in (3, 1, 2):
                there = peers[d]
                for xb in (0, 1):
                    pbuf[t - 1, d - 1, rows, pl.ds(xb * ROWS, ROWS)] = dot(
                        dg[t, rows, :], w2[:, cols(stripe(there["y"], there["zi"], xb))]
                    ).astype(BF16)
                b_copy(t, part, d).start()
            for xb in (0, 1):
                ownp[rows, pl.ds(xb * ROWS, ROWS)] = dot(dg[t, rows, :], w2[:, cols(mine[xb])])
        else:

            def unit(j, carry):
                dh0_o[rows, cols(j)] = dot(dg[0, rows, :], w2[:, cols(j)])
                return carry

            lax.fori_loop(0, HID // ROWS, unit, 0)

    def extras(t):
        dx = dot(dg[t], w2[:, pl.ds(HID, WIDE - HID)])
        high = dx.astype(BF16)
        rest = (dx - high.astype(F32)).astype(BF16)
        one = jnp.where(metas[:, t : t + 1] == lanes, 1.0, 0.0).astype(BF16)
        emb[...] += dot_tn(one, high) + dot_tn(one, rest)

    def d_copy(n):
        return remote(d_out.at[n], d_in.at[n], d_send.at[n], d_recv.at[n], quad_to(*quad[n]))

    def f_copy(xb):
        return remote(f_out.at[xb], f_in.at[p], f_send.at[xb], f_recv.at[p], (final_to(xb), shard))

    def f_wait(n):
        remote(f_out.at[n], f_in.at[n], f_send.at[n], f_recv.at[n], across).wait_recv()

    def decoder_start():
        for xb in (0, 1):
            total = dot_tn(hx[1, :, cols(mine[xb])], dlog[0])
            for t in range(1, STEPS):
                total = total + dot_tn(hx[t + 1, :, cols(mine[xb])], dlog[t])
            dpart[xb] = total
        for n, (dx, dc) in enumerate(quad):
            theirs = 2 * flip(x, dx) + flip(c, dc)
            for xb in (0, 1):
                d_out[n, xb] = dpart[xb, aligned(theirs * 64, 64), :].astype(BF16)
            d_copy(n).start()

    def decoder_middle():
        for n in range(3):
            d_copy(n).wait_recv()
        for xb in (0, 1):
            part = dpart[xb, aligned(shard * 64, 64), :]
            for n in range(3):
                part = part + d_in[n, xb].astype(F32)
            f_out[xb] = part.astype(BF16)

            @pl.when(final_to(xb) != dp)
            def _():
                f_copy(xb).start()

            @pl.when(final_to(xb) == dp)
            def _():
                f_in[p] = f_out[xb]

    def decoder_end():
        for n in (0, 1):

            @pl.when(final_from(n) != dp)
            def _():
                f_wait(n)

        gdec_o[...] = f_in[0].astype(F32) + f_in[1].astype(F32)

    for part in range(SPLIT):
        h_wait(STEPS - 1, part)
        decode(STEPS - 1, part)
        backward(STEPS - 1, part)
    decoder_start()
    extras(STEPS - 1)
    dg_out = [pltpu.make_async_copy(dg.at[t], dg_o.at[t], out_sem.at[1 + t]) for t in range(STEPS)]
    dg_out[STEPS - 1].start()
    for t in reversed(range(STEPS - 1)):
        for part in range(SPLIT):
            backward(t, part)
        dg_out[t].start()
        if t == STEPS - 2:
            decoder_middle()
        extras(t)
    decoder_end()

    for xb in (0, 1):
        dc0_o[:, pl.ds(xb * ROWS, ROWS)] = dcn[xb]
    at_row = lax.broadcasted_iota(jnp.int32, (288, 128), 0)
    at_col = lax.broadcasted_iota(jnp.int32, (288, 128), 1)
    block = jnp.where((at_row < 275) & (at_col < INPUTS), emb[pl.ds(0, 288), :], 0.0)
    for n in range(3):
        block = jnp.where(at_row == 276 + n, totals["bias"][:, n * 128 : n * 128 + 128], block)
    block = jnp.where((at_row == 279) & (at_col == 0), totals["loss"], block)
    emb_o[...] = block

    for q in range(SLICES):
        for target in (0, 1):

            @pl.when(c + 2 * target != z)
            def _():
                z_copy(target, q).wait_send()

        for n in (0, 1):
            x_copy(gates[n], q).wait_send()
            c_copy(gates[n], q, n, False).wait_send()
            c_copy(gates[n], q, n, True).wait_send()
    for n in range(5):
        for d in (1, 2):
            group_copy(d, n).wait_send()
        if n < 3:
            corner_copy(n).wait_send()
        else:
            group_copy(3, n).wait_send()
    for n in range(3):
        d_copy(n).wait_send()
    for xb in (0, 1):

        @pl.when(final_to(xb) != dp)
        def _():
            f_copy(xb).wait_send()

    far_copy().wait_send()
    over_copy().wait_send()
    for xs in (0, 1):
        twin_copy(xs).wait_send()
    for t in range(STEPS):
        for part in range(SPLIT):
            for d in (1, 2, 3):
                for xb in (0, 1):
                    h_copy(t, part, xb, d).wait_send()
                if t > 0:
                    b_copy(t, part, d).wait_send()
    hx_out.wait()
    for t in range(STEPS):
        dg_out[t].wait()


def sum_kernel(
    dg,
    hx,
    dh0,
    dc0,
    emb,
    gdec_own,
    grad_o,
    emb_o,
    norm_o,
    gh_o,
    gc_o,
    c_out,
    c_in,
    kept,
    x_out,
    x_in,
    z_out,
    z_in,
    gh_out,
    gh_in,
    gc_out,
    gc_in,
    e_in,
    n_out,
    n_in,
    c_send,
    c_recv,
    x_send,
    x_recv,
    z_send,
    z_recv,
    g_send,
    g_recv,
    e_send,
    e_recv,
    n_send,
    n_recv,
):
    s = spots()
    z, y, x, c, k, zi, p = s["z"], s["y"], s["x"], s["c"], s["k"], s["zi"], s["p"]
    dp, shard = s["dp"], s["shard"]
    across = device(s, x=1 - x)
    twin = device(s, c=1 - c)
    far = device(s, z=2 * (1 - p) + zi)
    peers = {d: peer(s, d) for d in (1, 2, 3)}
    core = z % 2
    column = [(dz, dc) for dz in range(4) for dc in range(2) if (dz, dc) != (0, 0)]
    plane = [(dy, dx) for dy in range(2) for dx in range(2) if (dy, dx) != (0, 0)]

    def flip(value, by):
        return 1 - value if by else value

    def column_to(dz, dc):
        return device(s, z=(z + dz) % 4, c=flip(c, dc))

    def column_from(dz, dc):
        return device(s, z=(z + 4 - dz) % 4, c=flip(c, dc))

    def plane_to(dy, dx):
        return device(s, y=flip(y, dy), x=flip(x, dx))

    for dz, dc in column:
        signal(column_from(dz, dc))
    for dy, dx in plane:
        signal(plane_to(dy, dx))
    signal(peers[3]["dev"])
    pl.semaphore_wait(pltpu.get_barrier_semaphore(), 11)

    def state_copies(d, sender=True):
        there = peers[d]
        rows = aligned(there["k"] * 64, 64)
        result = [
            remote(gh_out.at[d - 1], gh_in.at[d - 1], g_send.at[d - 1, 0], g_recv.at[d - 1, 0], there["dev"]),
            remote(gc_out.at[d - 1], gc_in.at[d - 1], g_send.at[d - 1, 1], g_recv.at[d - 1, 1], there["dev"]),
        ]
        return result

    def early():
        for d in (3, 1, 2):
            rows = aligned(peers[d]["k"] * 64, 64)
            gh_out[d - 1] = dh0[rows, :].astype(BF16)
            gc_out[d - 1] = dc0[rows, :].astype(BF16)
            for copy in state_copies(d):
                copy.start()

    tiles = ((0, 512), (512, 512), (1024, 512), (1536, 640))

    def block_of(b, store):
        for start, size in tiles:
            at = pl.ds(start, size)
            store(at, dot_tn(dg[:, cols(b)], hx[:, at]))

    def c_copy(n, q):
        rows = pl.ds(q * SLICE, SLICE)
        return remote(c_out.at[n, rows], c_in.at[n, rows], c_send.at[n, q], c_recv.at[n, q], twin)

    def x_copy(i, q):
        rows = pl.ds(q * SLICE, SLICE)
        return remote(x_out.at[i, rows], x_in.at[i, rows], x_send.at[i, q], x_recv.at[i, q], across)

    def z_copy(i, q):
        rows = pl.ds(q * SLICE, SLICE)
        return remote(
            z_out.at[i, rows],
            z_in.at[p, rows],
            z_send.at[i, q],
            z_recv.at[p, q],
            device(s, z=c + 2 * gates[i], c=core),
        )

    def z_wait(n, q):
        rows = pl.ds(q * SLICE, SLICE)
        remote(z_out.at[n, rows], z_in.at[n, rows], z_send.at[n, q], z_recv.at[n, q], across).wait_recv()

    def for_twin(n, b):
        def store(at, value):
            c_out[n, :, at] = value.astype(BF16)

        block_of(b, store)
        for q in range(SLICES):
            c_copy(n, q).start()

    def keep(i, b):
        def store(at, value):
            kept[i, :, at] = value

        block_of(b, store)

    def add_twin(i, n, q):
        rows = pl.ds(q * SLICE, SLICE)
        c_copy(n, q).wait_recv()
        return kept[i, rows] + c_in[n, rows].astype(F32)

    half = aligned(c * 144, 144)
    rest = aligned((1 - c) * 144, 144)
    hops = (twin, across, far, peers[2]["dev"], peers[1]["dev"], twin)

    def e_copy(n):
        if n == 0:
            return remote(emb_o.at[rest], e_in.at[0], e_send.at[0], e_recv.at[0], hops[0])
        if n == 5:
            return remote(emb_o.at[half], e_in.at[5], e_send.at[5], e_recv.at[5], hops[5])
        return remote(e_out_of(n), e_in.at[n], e_send.at[n], e_recv.at[n], hops[n])

    def e_out_of(n):
        return e_in.at[5 + n]

    def e_start(n):
        if n in (1, 2, 3, 4):
            e_in[5 + n] = emb_o[half, :]
        e_copy(n).start()

    def e_finish(n):
        if n == 5:
            e_copy(5).wait()
            emb_o[rest, :] = e_in[5]
            return
        e_copy(n).wait()
        emb_o[half, :] = emb_o[half, :] + e_in[n]

    gates = (1 - p, p)

    def pass_on(n, q):
        i = gates[n]
        rows = pl.ds(q * SLICE, SLICE)
        x_copy(n, q).wait_recv()
        total = add_twin(n, 2 + n, q) + x_in[n, rows].astype(F32)
        z_out[n, rows] = total.astype(BF16)

        @pl.when(c + 2 * i != z)
        def _():
            z_copy(n, q).start()

        @pl.when(c + 2 * i == z)
        def _():
            z_in[p, rows] = z_out[n, rows]

    def to_across(n):
        for q in range(SLICES):
            x_out[n, pl.ds(q * SLICE, SLICE)] = add_twin(2, n, q).astype(BF16)
            x_copy(n, q).start()

    emb_o[...] = emb[...]
    e_start(0)
    for_twin(0, 2 * (1 - c + 2 * gates[0]) + 1 - x)
    e_finish(0)
    e_start(1)
    keep(2, 2 * (c + 2 * gates[0]) + 1 - x)
    to_across(0)
    e_finish(1)
    e_start(2)
    for_twin(2, 2 * (1 - c + 2 * gates[0]) + x)
    keep(0, 2 * (c + 2 * gates[0]) + x)
    e_finish(2)
    e_start(3)
    for_twin(1, 2 * (1 - c + 2 * gates[1]) + 1 - x)
    keep(2, 2 * (c + 2 * gates[1]) + 1 - x)
    e_finish(3)
    e_start(4)
    for q in range(SLICES):
        pass_on(0, q)
        if q == 0:
            to_across(1)
            early()
        if q == 1:
            for_twin(3, 2 * (1 - c + 2 * gates[1]) + x)
        if q == 2:
            keep(1, 2 * (c + 2 * gates[1]) + x)
        if q == 3:
            e_finish(4)
            e_start(5)
    for q in range(SLICES):
        pass_on(1, q)
    e_finish(5)

    squares = jnp.zeros((1, 1), F32)

    def square_sum(value):
        return jnp.sum(jnp.sum(value * value, axis=1, keepdims=True), axis=0, keepdims=True)

    squares = squares + square_sum(gdec_own[...])
    for q in range(SLICES):
        rows = pl.ds(q * SLICE, SLICE)
        for n in (0, 1):

            @pl.when(jnp.logical_or(core != c, p != n))
            def _():
                z_wait(n, q)

        final = z_in[0, rows].astype(F32) + z_in[1, rows].astype(F32)
        grad_o[rows, :] = final
        squares = squares + square_sum(final)

    def n_copy(n):
        if n < 7:
            return remote(n_out.at[0], n_in.at[n], n_send.at[n], n_recv.at[n], column_to(*column[n]))
        return remote(n_out.at[1], n_in.at[n], n_send.at[n], n_recv.at[n], plane_to(*plane[n - 7]))

    n_out[0] = jnp.broadcast_to(squares, (8, 128))
    for n in range(7):
        n_copy(n).start()
    own = aligned(k * 64, 64)
    total = dh0[own, :]
    for d in (1, 2, 3):
        for copy in state_copies(d):
            copy.wait_recv()
        total = total + gh_in[d - 1].astype(F32)
    gh_o[...] = total
    for xb in (0, 1):
        gc_o[:, cols(stripe(y, zi, xb))] = dc0[own, pl.ds(xb * ROWS, ROWS)]
        for d in (1, 2, 3):
            there = peers[d]
            gc_o[:, cols(stripe(there["y"], there["zi"], xb))] = gc_in[d - 1, :, pl.ds(xb * ROWS, ROWS)].astype(F32)
    total = n_out[0]
    for n in range(7):
        n_copy(n).wait_recv()
        total = total + n_in[n]
    n_out[1] = total
    for n in range(7, 10):
        n_copy(n).start()
    at_row = lax.broadcasted_iota(jnp.int32, (288, 128), 0)
    shared = square_sum(jnp.where(at_row == 279, 0.0, emb_o[...]))
    for n in range(7, 10):
        n_copy(n).wait_recv()
        total = total + n_in[n]
    norm_o[...] = total + shared

    for n in range(4):
        for q in range(SLICES):
            c_copy(n, q).wait_send()
    for i in (0, 1):
        for q in range(SLICES):
            x_copy(i, q).wait_send()

            @pl.when(c + 2 * gates[i] != z)
            def _():
                z_copy(i, q).wait_send()

    for d in (1, 2, 3):
        for copy in state_copies(d):
            copy.wait_send()
    for n in range(10):
        n_copy(n).wait_send()


def split_local(
    char_ids,
    targets,
    hidden_start,
    cell_start,
    embedding,
    input_weight,
    hidden_weight,
    gate_bias,
    decoder_weight,
    decoder_bias,
    momentum_embed,
    momentum_input,
    momentum_hidden,
    momentum_gate,
    momentum_decoder,
    momentum_outbias,
):
    streams = char_ids.shape[0]
    vocab = embedding.shape[0]
    shape = jax.ShapeDtypeStruct
    wext = jnp.concatenate(
        [
            hidden_weight.astype(BF16),
            input_weight.astype(BF16),
            gate_bias.astype(BF16)[:, None],
            jnp.zeros((ROWS, WIDE - HID - INPUTS - 1), BF16),
        ],
        axis=1,
    )
    meta = jnp.pad(jnp.concatenate([char_ids, targets], axis=1), ((0, 0), (0, 120)))
    wout = jnp.pad(decoder_weight.astype(BF16), ((0, 0), (0, CHARS - vocab)))
    table = jnp.concatenate(
        [embedding.astype(BF16), jnp.ones((vocab, 1), BF16), jnp.zeros((vocab, WIDE - HID - INPUTS - 1), BF16)],
        axis=1,
    )
    table = jnp.pad(table, ((0, CHARS - vocab), (0, 0)))
    dbias = jnp.broadcast_to(
        jnp.pad(decoder_bias, (0, CHARS - vocab), constant_values=-1e30)[None, :], (8, CHARS)
    )
    vm = pl.BlockSpec(memory_space=pltpu.VMEM)
    hbm = pl.BlockSpec(memory_space=pl.ANY)
    dma = pltpu.SemaphoreType.DMA
    hx, dg, dh0, dc0, emb, gdec_own = pl.pallas_call(
        step_kernel,
        out_shape=(
            shape((STEPS, ROWS, WIDE), BF16),
            shape((STEPS, ROWS, HID), BF16),
            shape((ROWS, HID), F32),
            shape((ROWS, 512), F32),
            shape((288, 128), F32),
            shape((64, CHARS), F32),
        ),
        in_specs=[vm] * 7,
        out_specs=(hbm, hbm, vm, vm, vm, vm),
        scratch_shapes=[
            pltpu.VMEM((HID, WIDE), BF16),
            pltpu.VMEM((8, WIDE, ROWS), BF16),
            pltpu.VMEM((STEPS + 1, ROWS, WIDE), BF16),
            pltpu.VMEM((STEPS, 8, ROWS, ROWS), F32),
            pltpu.VMEM((STEPS + 1, 2, ROWS, ROWS), F32),
            pltpu.VMEM((STEPS, ROWS, HID), BF16),
            pltpu.VMEM((STEPS - 1, 3, ROWS, 512), BF16),
            pltpu.VMEM((STEPS - 1, 3, ROWS, 512), BF16),
            pltpu.VMEM((ROWS, 512), F32),
            pltpu.VMEM((2, ROWS, ROWS), F32),
            pltpu.VMEM((8, 4, 64, CHARS), BF16),
            pltpu.VMEM((STEPS, ROWS, CHARS), BF16),
            pltpu.VMEM((ROWS, 128), jnp.int32),
            pltpu.VMEM((CHARS, 128), F32),
            pltpu.VMEM((2, ROWS, ROWS), BF16),
            pltpu.VMEM((2, ROWS, CHARS), F32),
            pltpu.VMEM((3, 2, 64, CHARS), BF16),
            pltpu.VMEM((3, 2, 64, CHARS), BF16),
            pltpu.VMEM((2, 64, CHARS), BF16),
            pltpu.VMEM((2, 64, CHARS), BF16),
            dma((3, 5)),
            dma((3, 5)),
            dma((2, SLICES)),
            dma((2, SLICES)),
            dma((2, SLICES)),
            dma((2, SLICES)),
            dma((2, 2, SLICES)),
            dma((2, 2, SLICES)),
            dma((4,)),
            dma((4,)),
            dma((STEPS, SPLIT, 2, 3)),
            dma((STEPS, SPLIT, 2, 3)),
            dma((STEPS - 1, SPLIT, 3)),
            dma((STEPS - 1, SPLIT, 3)),
            dma((3,)),
            dma((3,)),
            dma((2,)),
            dma((2,)),
            dma((1 + STEPS,)),
        ],
        compiler_params=pltpu.CompilerParams(
            collective_id=0, has_side_effects=True, vmem_limit_bytes=60 * 2**20
        ),
    )(wext, hidden_start.astype(BF16), cell_start.astype(BF16), meta, wout, table, dbias)
    grad, emb, norm, grad_hidden_start, grad_cell_start = pl.pallas_call(
        sum_kernel,
        out_shape=(
            shape((ROWS, WIDE), F32),
            shape((288, 128), F32),
            shape((8, 128), F32),
            shape((64, HID), F32),
            shape((64, HID), F32),
        ),
        in_specs=[vm] * 6,
        out_specs=(vm,) * 5,
        scratch_shapes=[
            pltpu.VMEM((4, ROWS, WIDE), BF16),
            pltpu.VMEM((4, ROWS, WIDE), BF16),
            pltpu.VMEM((3, ROWS, WIDE), F32),
            pltpu.VMEM((2, ROWS, WIDE), BF16),
            pltpu.VMEM((2, ROWS, WIDE), BF16),
            pltpu.VMEM((2, ROWS, WIDE), BF16),
            pltpu.VMEM((2, ROWS, WIDE), BF16),
            pltpu.VMEM((3, 64, HID), BF16),
            pltpu.VMEM((3, 64, HID), BF16),
            pltpu.VMEM((3, 64, 512), BF16),
            pltpu.VMEM((3, 64, 512), BF16),
            pltpu.VMEM((10, 144, 128), F32),
            pltpu.VMEM((2, 8, 128), F32),
            pltpu.VMEM((10, 8, 128), F32),
            dma((4, SLICES)),
            dma((4, SLICES)),
            dma((2, SLICES)),
            dma((2, SLICES)),
            dma((2, SLICES)),
            dma((2, SLICES)),
            dma((3, 2)),
            dma((3, 2)),
            dma((6,)),
            dma((6,)),
            dma((10,)),
            dma((10,)),
        ],
        compiler_params=pltpu.CompilerParams(
            collective_id=1, has_side_effects=True, vmem_limit_bytes=60 * 2**20
        ),
    )(dg.reshape(STEPS * ROWS, HID), hx.reshape(STEPS * ROWS, WIDE), dh0, dc0, emb, gdec_own)
    grad_norm = jnp.sqrt(norm[0:1, 0])
    factor = CLIP / jnp.maximum(grad_norm[0], CLIP)
    streams_all = streams * lax.axis_size("dp") * lax.axis_size("shard")
    loss = emb[279, 0:1] / streams_all
    grads = (
        emb[:vocab, :INPUTS],
        grad[:, HID : HID + INPUTS],
        grad[:, :HID],
        grad[:, HID + INPUTS],
        gdec_own[:, :vocab],
        emb[276:279].reshape(-1)[:vocab],
    )
    momenta = (
        momentum_embed,
        momentum_input,
        momentum_hidden,
        momentum_gate,
        momentum_decoder,
        momentum_outbias,
    )
    updated = tuple(MOMENTUM * momenta[n] + factor * grads[n] for n in range(6))
    return (loss, grad_norm, grad_hidden_start, grad_cell_start) + grads + updated


def solution(mesh):
    fits = mesh.shape["dp"] == 8 and mesh.shape["shard"] == 4
    placed = (
        P(("dp", "shard"), None),
        P(("dp", "shard"), None),
        P(("dp", "shard"), None),
        P(("dp", "shard"), None),
        P(),
        P(("dp", "shard"), None),
        P(("dp", "shard"), None),
        P(("dp", "shard")),
        P(("dp", "shard"), None),
        P(),
        P(),
        P(("dp", "shard"), None),
        P(("dp", "shard"), None),
        P(("dp", "shard")),
        P(("dp", "shard"), None),
        P(),
    )
    return jax.shard_map(
        split_local if fits else local,
        mesh=mesh,
        in_specs=placed,
        out_specs=(
            P(),
            P(),
            P(("dp", "shard"), None),
            P(("dp", "shard"), None),
            P(),
            P(("dp", "shard"), None),
            P(("dp", "shard"), None),
            P(("dp", "shard")),
            P(("dp", "shard"), None),
            P(),
            P(),
            P(("dp", "shard"), None),
            P(("dp", "shard"), None),
            P(("dp", "shard")),
            P(("dp", "shard"), None),
            P(),
        ),
        check_vma=False,
    )
```

```python
import functools

import jax
import jax.numpy as jnp
from jax import lax
from jax.experimental import pallas as pl
from jax.experimental.pallas import tpu as pltpu
from jax.sharding import PartitionSpec as P

MESH = pl.DeviceIdType.MESH
F32 = jnp.float32
BF16 = jnp.bfloat16

MICRO = 2


CLIP = 0.25
MOMENTUM = 0.5


def contract_rows(left, right):
    return lax.dot_general(
        left, right, (((0,), (0,)), ((), ())), preferred_element_type=jnp.float32
    )


def contract_last(left, right):
    return lax.dot_general(
        left, right, (((1,), (1,)), ((), ())), preferred_element_type=jnp.float32
    )


def local(
    char_ids,
    targets,
    hidden_start,
    cell_start,
    embedding,
    input_weight,
    hidden_weight,
    gate_bias,
    decoder_weight,
    decoder_bias,
    momentum_embed,
    momentum_input,
    momentum_hidden,
    momentum_gate,
    momentum_decoder,
    momentum_outbias,
):
    streams, seq_len = char_ids.shape
    micro_rows = streams // MICRO
    vocab_size = embedding.shape[0]
    hidden_size = hidden_start.shape[1]
    low_input = input_weight.astype(jnp.bfloat16)
    low_hidden = hidden_weight.astype(jnp.bfloat16)
    low_bias = gate_bias.astype(jnp.bfloat16)
    low_decoder = decoder_weight.astype(jnp.bfloat16)
    inner_rows = (
        lax.all_gather(low_input, "shard", axis=0, tiled=True),
        lax.all_gather(low_hidden, "shard", axis=0, tiled=True),
        lax.all_gather(low_bias, "shard", axis=0, tiled=True),
        lax.all_gather(low_decoder, "shard", axis=0, tiled=True),
    )
    weight_in, weight_rec, bias_low, weight_out = (
        lax.all_gather(inner_rows[0], "dp", axis=0, tiled=True),
        lax.all_gather(inner_rows[1], "dp", axis=0, tiled=True),
        lax.all_gather(inner_rows[2], "dp", axis=0, tiled=True),
        lax.all_gather(inner_rows[3], "dp", axis=0, tiled=True),
    )
    columns = jnp.arange(vocab_size, dtype=jnp.int32)
    table = embedding.astype(jnp.bfloat16)
    bias_row = bias_low.astype(jnp.float32)[None, :]

    def forward_step(carried, input_now):
        hidden_low, cell = carried
        preact = input_now + contract_last(hidden_low, weight_rec)
        input_gate = jax.nn.sigmoid(preact[:, :hidden_size])
        forget_gate = jax.nn.sigmoid(preact[:, hidden_size : 2 * hidden_size])
        candidate = jnp.tanh(preact[:, 2 * hidden_size : 3 * hidden_size])
        output_gate = jax.nn.sigmoid(preact[:, 3 * hidden_size :])
        cell_next = forget_gate * cell + input_gate * candidate
        hidden_next = (output_gate * jnp.tanh(cell_next)).astype(jnp.bfloat16)
        activations = jnp.concatenate([input_gate, forget_gate, candidate, output_gate], axis=1)
        return ((hidden_next, cell_next), (hidden_low, cell, activations, cell_next, hidden_next))

    def backward_step(carried, inputs):
        hidden_grad_next, cell_grad_next = carried
        out_grad, cell_before, gate_values, cell_now = inputs
        hidden_grad = out_grad + hidden_grad_next
        input_gate = gate_values[:, :hidden_size]
        forget_gate = gate_values[:, hidden_size : 2 * hidden_size]
        candidate = gate_values[:, 2 * hidden_size : 3 * hidden_size]
        output_gate = gate_values[:, 3 * hidden_size :]
        cell_tanh = jnp.tanh(cell_now)
        cell_grad = cell_grad_next + hidden_grad * output_gate * (1.0 - cell_tanh * cell_tanh)
        input_term = cell_grad * candidate * input_gate * (1.0 - input_gate)
        forget_term = cell_grad * cell_before * forget_gate * (1.0 - forget_gate)
        candidate_term = cell_grad * input_gate * (1.0 - candidate * candidate)
        output_term = hidden_grad * cell_tanh * output_gate * (1.0 - output_gate)
        gate_grad = jnp.concatenate(
            [input_term, forget_term, candidate_term, output_term], axis=1
        ).astype(jnp.bfloat16)
        hidden_grad_prev = jnp.dot(gate_grad, weight_rec, preferred_element_type=jnp.float32)
        return ((hidden_grad_prev, cell_grad * forget_gate), gate_grad)

    def micro_pass(loss_total, inputs):
        ids_part, target_part, hidden_part, cell_part = inputs
        batch_rows = ids_part.shape[0]
        token_ids = ids_part.T.reshape(-1)
        token_targets = target_part.T.reshape(-1)
        one_input = (token_ids[:, None] == columns[None, :]).astype(jnp.bfloat16)
        one_target = (token_targets[:, None] == columns[None, :]).astype(jnp.float32)
        embedded = jnp.dot(one_input, table, preferred_element_type=jnp.float32).astype(
            jnp.bfloat16
        )
        input_part = contract_last(embedded, weight_in) + bias_row
        input_part = input_part.reshape(seq_len, batch_rows, 4 * hidden_size)
        start_pair = (hidden_part.astype(jnp.bfloat16), cell_part)
        final_pair, saved = lax.scan(forward_step, start_pair, input_part)
        hidden_prev, cell_prev, activations, cell_after, hidden_after = saved
        hidden_rows = hidden_after.reshape(seq_len * batch_rows, hidden_size)
        logits = (
            jnp.dot(hidden_rows, weight_out, preferred_element_type=jnp.float32)
            + decoder_bias[None, :]
        )
        log_total = jax.nn.logsumexp(logits, axis=1)
        local_loss = jnp.sum(log_total - jnp.sum(one_target * logits, axis=1)) / seq_len
        probs = jnp.exp(logits - log_total[:, None])
        logit_grad = ((probs - one_target) / seq_len).astype(jnp.bfloat16)
        hidden_from_out = contract_last(logit_grad, weight_out).reshape(
            seq_len, batch_rows, hidden_size
        )
        zero_state = jnp.zeros((batch_rows, hidden_size), jnp.float32)
        start_grads, gate_grads = lax.scan(
            backward_step,
            (zero_state, zero_state),
            (hidden_from_out, cell_prev, activations, cell_after),
            reverse=True,
        )
        gate_rows = gate_grads.reshape(seq_len * batch_rows, 4 * hidden_size)
        prev_rows = hidden_prev.reshape(seq_len * batch_rows, hidden_size)
        return (
            loss_total + local_loss,
            (
                token_ids,
                embedded,
                logit_grad,
                hidden_rows,
                gate_rows,
                prev_rows,
                start_grads[0],
                start_grads[1],
            ),
        )

    def by_micro(array):
        return array.reshape((MICRO, micro_rows) + array.shape[1:])

    local_loss, stacked = lax.scan(
        micro_pass,
        jnp.zeros((), jnp.float32),
        (by_micro(char_ids), by_micro(targets), by_micro(hidden_start), by_micro(cell_start)),
    )
    token_ids, embedded, logit_grad, hidden_rows, gate_rows, prev_rows, hidden_grads, cell_grads = (
        stacked
    )
    token_ids = token_ids.reshape(-1)
    embedded = embedded.reshape(-1, embedded.shape[-1])
    logit_grad = logit_grad.reshape(-1, vocab_size)
    hidden_rows = hidden_rows.reshape(-1, hidden_size)
    gate_rows = gate_rows.reshape(-1, 4 * hidden_size)
    prev_rows = prev_rows.reshape(-1, hidden_size)
    grad_hidden_start = hidden_grads.reshape(streams, hidden_size)
    grad_cell_start = cell_grads.reshape(streams, hidden_size)
    grad_outbias_local = jnp.sum(logit_grad.astype(jnp.float32), axis=0)
    grad_decoder_local = contract_rows(hidden_rows, logit_grad)
    grad_input_local = contract_rows(gate_rows, embedded)
    grad_hidden_local = contract_rows(gate_rows, prev_rows)
    grad_bias_local = jnp.sum(gate_rows.astype(jnp.float32), axis=0)
    embed_rows_grad = jnp.dot(gate_rows, weight_in, preferred_element_type=jnp.float32)
    one_all = (token_ids[:, None] == columns[None, :]).astype(jnp.float32)
    grad_embed_local = lax.dot_general(
        one_all,
        embed_rows_grad,
        (((0,), (0,)), ((), ())),
        precision=lax.Precision.HIGHEST,
        preferred_element_type=jnp.float32,
    )
    grad_embedding, grad_decoder_bias, loss_sum = lax.psum(
        (grad_embed_local, grad_outbias_local, local_loss), ("dp", "shard")
    )
    outer_sums = (
        lax.psum_scatter(
            grad_input_local.astype(jnp.bfloat16), "dp", scatter_dimension=0, tiled=True
        ).astype(jnp.float32),
        lax.psum_scatter(
            grad_hidden_local.astype(jnp.bfloat16), "dp", scatter_dimension=0, tiled=True
        ).astype(jnp.float32),
        lax.psum_scatter(
            grad_bias_local.astype(jnp.bfloat16), "dp", scatter_dimension=0, tiled=True
        ).astype(jnp.float32),
        lax.psum_scatter(
            grad_decoder_local.astype(jnp.bfloat16), "dp", scatter_dimension=0, tiled=True
        ).astype(jnp.float32),
    )
    grad_input_weight, grad_hidden_weight, grad_gate_bias, grad_decoder_weight = (
        lax.psum_scatter(
            outer_sums[0].astype(jnp.bfloat16), "shard", scatter_dimension=0, tiled=True
        ).astype(jnp.float32),
        lax.psum_scatter(
            outer_sums[1].astype(jnp.bfloat16), "shard", scatter_dimension=0, tiled=True
        ).astype(jnp.float32),
        lax.psum_scatter(
            outer_sums[2].astype(jnp.bfloat16), "shard", scatter_dimension=0, tiled=True
        ).astype(jnp.float32),
        lax.psum_scatter(
            outer_sums[3].astype(jnp.bfloat16), "shard", scatter_dimension=0, tiled=True
        ).astype(jnp.float32),
    )
    shard_squares = jnp.sum(grad_input_weight * grad_input_weight) + jnp.sum(
        grad_hidden_weight * grad_hidden_weight
    )
    shard_squares = (
        shard_squares
        + jnp.sum(grad_gate_bias * grad_gate_bias)
        + jnp.sum(grad_decoder_weight * grad_decoder_weight)
    )
    square_total = lax.psum(shard_squares, ("dp", "shard"))
    square_total = (
        square_total
        + jnp.sum(grad_embedding * grad_embedding)
        + jnp.sum(grad_decoder_bias * grad_decoder_bias)
    )
    grad_norm = jnp.sqrt(square_total)
    factor = CLIP / jnp.maximum(grad_norm, CLIP)
    streams_all = streams * lax.axis_size("dp") * lax.axis_size("shard")
    loss = loss_sum / streams_all
    momenta = (
        momentum_embed,
        momentum_input,
        momentum_hidden,
        momentum_gate,
        momentum_decoder,
        momentum_outbias,
    )
    weight_grads = (
        grad_embedding,
        grad_input_weight,
        grad_hidden_weight,
        grad_gate_bias,
        grad_decoder_weight,
        grad_decoder_bias,
    )
    new_momenta = [MOMENTUM * momenta[index] + factor * weight_grads[index] for index in range(6)]
    return (
        loss.reshape(1),
        grad_norm.reshape(1),
        grad_hidden_start,
        grad_cell_start,
        grad_embedding,
        grad_input_weight,
        grad_hidden_weight,
        grad_gate_bias,
        grad_decoder_weight,
        grad_decoder_bias,
        new_momenta[0],
        new_momenta[1],
        new_momenta[2],
        new_momenta[3],
        new_momenta[4],
        new_momenta[5],
    )


ROWS = 256
HID = 2048
WIDE = 2176
INPUTS = 100
CHARS = 384
SPLIT = 2
PART = ROWS // SPLIT
SLICES = 8
SLICE = ROWS // SLICES
STEPS = 4


def spots():
    dp = lax.axis_index("dp")
    shard = lax.axis_index("shard")
    return dict(
        p=dp // 4,
        zi=(dp // 2) % 2,
        z=dp // 2,
        y=dp % 2,
        k=dp % 4,
        x=shard // 2,
        c=shard % 2,
        dp=dp,
        shard=shard,
    )


def device(s, z=None, y=None, x=None, c=None):
    z = s["z"] if z is None else z
    y = s["y"] if y is None else y
    x = s["x"] if x is None else x
    c = s["c"] if c is None else c
    return (z * 2 + y, x * 2 + c)


def peer(s, d):
    y = 1 - s["y"] if d % 2 else s["y"]
    zi = 1 - s["zi"] if d // 2 else s["zi"]
    z = 2 * s["p"] + zi
    return dict(y=y, zi=zi, k=2 * zi + y, dev=(z * 2 + y, s["shard"]))


def stripe(y, zi, xb):
    return 4 * y + 2 * xb + zi


def cols(index):
    return pl.ds(pl.multiple_of(index * ROWS, ROWS), ROWS)


def aligned(start, size):
    return pl.ds(pl.multiple_of(start, size), size)


def remote(src, dst, send, recv, dev):
    return pltpu.make_async_remote_copy(
        src_ref=src, dst_ref=dst, send_sem=send, recv_sem=recv, device_id=dev, device_id_type=MESH
    )


def dot(left, right):
    return jnp.dot(left, right, preferred_element_type=F32)


def dot_nt(left, right):
    return lax.dot_general(left, right, (((1,), (1,)), ((), ())), preferred_element_type=F32)


def dot_tn(left, right):
    return lax.dot_general(left, right, (((0,), (0,)), ((), ())), preferred_element_type=F32)


def signal(dev):
    pl.semaphore_signal(
        pltpu.get_barrier_semaphore(), inc=1, device_id=dev, device_id_type=MESH
    )


def step_kernel(
    ids_in,
    targets_in,
    hidden_in,
    cell_in,
    embedding_in,
    input_in,
    weight_in,
    gate_in,
    decoder_in,
    outbias_in,
    hx_o,
    dg_o,
    dh0_o,
    dc0_o,
    emb_o,
    gdec_o,
    w2,
    wt,
    hx,
    act,
    call,
    dg,
    pbuf,
    rbuf,
    ownp,
    dcn,
    wo,
    dlog,
    metas,
    emb,
    cells,
    dpart,
    d_out,
    d_in,
    f_out,
    f_in,
    wext,
    h_own,
    cell_own,
    meta_own,
    wout_own,
    table,
    dbias,
    narrow,
    ids_wide,
    g_send,
    g_recv,
    wz_send,
    wz_recv,
    wx_send,
    wx_recv,
    wc_send,
    wc_recv,
    o_send,
    o_recv,
    h_send,
    h_recv,
    b_send,
    b_recv,
    d_send,
    d_recv,
    f_send,
    f_recv,
    out_sem,
):
    s = spots()
    z, y, x, c, k, zi, p = s["z"], s["y"], s["x"], s["c"], s["k"], s["zi"], s["p"]
    dp, shard = s["dp"], s["shard"]
    across = device(s, x=1 - x)
    twin = device(s, c=1 - c)
    far = device(s, z=2 * (1 - p) + zi)
    peers = {d: peer(s, d) for d in (1, 2, 3)}
    mine = [stripe(y, zi, xb) for xb in (0, 1)]
    core = z % 2
    off_core = jnp.where(core == c, 0, 1)
    quad = [(dx, dc) for dx in range(2) for dc in range(2) if (dx, dc) != (0, 0)]

    def flip(value, by):
        return 1 - value if by else value

    def quad_to(dx, dc):
        return device(s, x=flip(x, dx), c=flip(c, dc))

    def final_to(xb):
        return 4 * y + 2 * xb + zi

    def final_from(half):
        return 4 * half + 2 * y + p

    for d in (1, 2, 3):
        signal(peers[d]["dev"])
    signal(across)
    signal(twin)
    signal(far)

    signal(device(s, x=1 - x, c=1 - c))

    @pl.when(core != c)
    def _():
        for i in (0, 1):
            signal(device(s, z=c + 2 * i, c=core))

    away = 0
    for n in (0, 1):

        @pl.when(final_from(n) != dp)
        def _():
            signal((final_from(n), shard))

        away = away + jnp.where(final_to(n) != dp, 1, 0)

    narrow[...] = jnp.zeros_like(narrow)
    narrow[pl.ds(0, INPUTS), :] = input_in[...]
    narrow[pl.ds(INPUTS, 1), :] = gate_in[...]
    wext[:, pl.ds(HID, WIDE - HID)] = narrow[...].T.astype(BF16)
    wext[:, pl.ds(0, HID)] = weight_in[...].astype(BF16)
    ids_wide[...] = jnp.zeros_like(ids_wide)
    ids_wide[pl.ds(0, STEPS), pl.ds(0, 64)] = ids_in[...]
    ids_wide[pl.ds(STEPS, STEPS), pl.ds(0, 64)] = targets_in[...]
    meta_own[...] = ids_wide[...].T[0:64, :]
    h_own[...] = hidden_in[...].astype(BF16)
    vocab = decoder_in.shape[1]
    wout_own[...] = jnp.zeros_like(wout_own)
    wout_own[:, pl.ds(0, vocab)] = decoder_in[...].astype(BF16)
    cell_own[...] = cell_in[...].astype(BF16)
    pl.semaphore_wait(pltpu.get_barrier_semaphore(), 7 + 2 * off_core + away)

    def z_copy(target, q):
        rows = pl.ds(q * SLICE, SLICE)
        slot = aligned((2 * z + x) * ROWS + q * SLICE, SLICE)
        return remote(
            wext.at[rows],
            w2.at[slot],
            wz_send.at[target, q],
            wz_recv.at[z // 2, q],
            device(s, z=c + 2 * target, c=core),
        )

    def z_wait(i, q):
        slot = aligned((2 * (c + 2 * i) + x) * ROWS + q * SLICE, SLICE)
        remote(wext.at[pl.ds(q * SLICE, SLICE)], w2.at[slot], wz_send.at[0, q], wz_recv.at[i, q], across).wait_recv()

    def x_copy(i, q, sender=True):
        xs = x if sender else 1 - x
        slot = aligned((2 * (c + 2 * i) + xs) * ROWS + q * SLICE, SLICE)
        return remote(w2.at[slot], w2.at[slot], wx_send.at[i, q], wx_recv.at[i, q], across)

    def c_copy(i, q, n, other, sender=True):
        xs = 1 - x if other else x
        cs = c if sender else 1 - c
        slot = aligned((2 * (cs + 2 * i) + xs) * ROWS + q * SLICE, SLICE)
        return remote(
            w2.at[slot], w2.at[slot], wc_send.at[n, int(other), q], wc_recv.at[n, int(other), q], twin
        )

    near = p
    beyond = 1 - p

    def start_beyond():
        for q in range(SLICES):

            @pl.when(c + 2 * beyond != z)
            def _():
                z_copy(beyond, q).start()

    pl.when(zi != p)(start_beyond)
    own = aligned(k * 64, 64)

    def group_copy(d, n):
        dev = peers[d]["dev"]
        send, recv = g_send.at[d - 1, n], g_recv.at[d - 1, n]
        if n == 0:
            return remote(meta_own, metas.at[own], send, recv, dev)
        if n == 1:
            return remote(h_own, hx.at[0, own, pl.ds(0, HID)], send, recv, dev)
        if n == 2:
            return remote(wout_own, wo.at[dp, shard], send, recv, dev)
        theirs = stripe(peers[d]["y"], peers[d]["zi"], n - 3)
        return remote(cell_own.at[:, cols(theirs)], cells.at[n - 3, own], send, recv, dev)

    def corner_copy(n, sender=True):
        there = peers[2 if sender else 3]
        rows = aligned(there["k"] * 64, 64)
        send, recv = g_send.at[2, n], g_recv.at[2, n]
        dev = peers[1]["dev"]
        if n == 0:
            part = metas.at[rows]
        elif n == 1:
            part = hx.at[0, rows, pl.ds(0, HID)]
        else:
            part = wo.at[there["dev"][0], shard]
        return remote(part, part, send, recv, dev)

    @pl.when(c + 2 * near == z)
    def _():
        w2[aligned((2 * z + x) * ROWS, ROWS), :] = wext[...]

    for q in range(SLICES):

        @pl.when(c + 2 * near != z)
        def _():
            z_copy(near, q).start()

        if q == 0:
            for n in (0, 2, 1):
                for d in (2, 1):
                    group_copy(d, n).start()
    for n in (3, 4):
        for d in (3, 2, 1):
            group_copy(d, n).start()
    pl.when(zi == p)(start_beyond)
    metas[own, :] = meta_own[...]
    hx[0, own, pl.ds(0, HID)] = h_own[...]
    wo[dp, shard] = wout_own[...]
    for xb in (0, 1):
        cells[xb, own] = cell_own[:, cols(mine[xb])]

    dbias[...] = jnp.full(dbias.shape, -1e30, F32)
    dbias[pl.ds(0, 1), pl.ds(0, vocab)] = outbias_in[...]
    table[...] = jnp.where(lax.broadcasted_iota(jnp.int32, table.shape, 1) == INPUTS, 1.0, 0.0)
    table[pl.ds(0, vocab), pl.ds(0, INPUTS)] = embedding_in[...].astype(BF16).astype(F32)

    def group_wait(d, n):
        there = peers[d]
        rows = aligned(there["k"] * 64, 64)
        send, recv = g_send.at[d - 1, n], g_recv.at[d - 1, n]
        if n == 0:
            copy = remote(meta_own, metas.at[rows], send, recv, there["dev"])
        elif n == 1:
            copy = remote(h_own, hx.at[0, rows, pl.ds(0, HID)], send, recv, there["dev"])
        elif n == 2:
            copy = remote(wout_own, wo.at[there["dev"][0], shard], send, recv, there["dev"])
        else:
            copy = remote(cell_own.at[:, cols(mine[n - 3])], cells.at[n - 3, rows], send, recv, there["dev"])
        copy.wait_recv()

    lanes = lax.broadcasted_iota(jnp.int32, (ROWS, CHARS), 1)

    def embed_inputs():
        for t in range(STEPS):
            one = jnp.where(metas[:, t : t + 1] == lanes, 1.0, 0.0).astype(BF16)
            hx[t, :, pl.ds(HID, WIDE - HID)] = dot(one, table[...].astype(BF16)).astype(BF16)

    def turn(b):
        wt[b] = w2[cols(b), :].T

    order = [(n, q) for n in (0, 1) for q in range(SLICES)]
    gates = (p, 1 - p)
    for at, (n, q) in enumerate(order):
        i = gates[n]

        @pl.when(c + 2 * i != z)
        def _():
            z_wait(i, q)

        x_copy(i, q).start()
        c_copy(i, q, n, False).start()
        if at > 0:
            before, slot = order[at - 1]
            x_copy(gates[before], slot, False).wait_recv()
            c_copy(gates[before], slot, before, True).start()
        if n == 0 and q == SLICES - 1:
            for m in (0, 2, 1):
                group_wait(2, m)
                corner_copy(m).start()
        if n == 1 and q < 2:
            turn(2 * (c + 2 * p) + q)
        if n == 1 and q == 3:
            group_wait(1, 0)
            corner_copy(0, False).wait_recv()
            embed_inputs()
        if n == 1 and q == 2:
            for other in (False, True):
                for slot in range(SLICES):
                    c_copy(p, slot, 0, other, False).wait_recv()
            for xs in (0, 1):
                turn(2 * (1 - c + 2 * p) + xs)
    x_copy(1 - p, SLICES - 1, False).wait_recv()
    c_copy(1 - p, SLICES - 1, 1, True).start()
    for xs in (0, 1):
        turn(2 * (c + 2 * (1 - p)) + xs)
    for other in (False, True):
        for q in range(SLICES):
            c_copy(1 - p, q, 1, other, False).wait_recv()
    for xs in (0, 1):
        turn(2 * (1 - c + 2 * (1 - p)) + xs)
    for n in (1, 2):
        group_wait(1, n)
        corner_copy(n, False).wait_recv()
    for n in (3, 4):
        for d in (1, 2, 3):
            group_wait(d, n)
        call[0, n - 3] = cells[n - 3].astype(F32)

    def far_copy(sender=True):
        first = 4 * p if sender else 4 * (1 - p)
        part = wo.at[pl.ds(first, 4), shard]
        return remote(part, part, o_send.at[0], o_recv.at[0], far)

    def over_copy(sender=True):
        part = wo.at[:, 2 * x + c if sender else 2 * (1 - x) + c]
        return remote(part, part, o_send.at[1], o_recv.at[1], across)

    def twin_copy(xs, sender=True):
        part = wo.at[:, 2 * xs + (c if sender else 1 - c)]
        return remote(part, part, o_send.at[2 + xs], o_recv.at[2 + xs], twin)

    def h_copy(t, part, xb, d, sender=True):
        there = peers[d]
        rows = pl.ds(part * PART, PART)
        at = mine[xb] if sender else stripe(there["y"], there["zi"], xb)
        block = hx.at[t + 1, rows, cols(at)]
        return remote(block, block, h_send.at[t, part, xb, d - 1], h_recv.at[t, part, xb, d - 1], there["dev"])

    def forward(t, part):
        rows = pl.ds(part * PART, PART)
        for xb in (0, 1):

            def pre(g):
                return dot(hx[t, rows, :], wt[2 * g + xb])

            gate_i = jax.nn.sigmoid(pre(0))
            act[t, xb, rows] = gate_i
            gate_f = jax.nn.sigmoid(pre(1))
            act[t, 2 + xb, rows] = gate_f
            gate_g = jnp.tanh(pre(2))
            act[t, 4 + xb, rows] = gate_g
            gate_o = jax.nn.sigmoid(pre(3))
            act[t, 6 + xb, rows] = gate_o
            cell = gate_f * call[t, xb, rows] + gate_i * gate_g
            call[t + 1, xb, rows] = cell
            hx[t + 1, rows, cols(mine[xb])] = (gate_o * jnp.tanh(cell)).astype(BF16)
            for d in (3, 1, 2):
                h_copy(t, part, xb, d).start()

    def h_wait(t, part):
        for xb in (0, 1):
            for d in (1, 2, 3):
                h_copy(t, part, xb, d, False).wait_recv()

    part_lanes = lax.broadcasted_iota(jnp.int32, (PART, CHARS), 1)
    part_rows = lax.broadcasted_iota(jnp.int32, (PART, 1), 0)
    totals = dict(loss=jnp.zeros((1, 1), F32), bias=jnp.zeros((1, CHARS), F32))

    def decode(t, part):
        rows = pl.ds(part * PART, PART)
        logits = dot(hx[t + 1, rows, pl.ds(0, HID)], wo[...].reshape(HID, CHARS)) + dbias[0:1, :]
        top = jnp.max(logits, axis=1, keepdims=True)
        grown = jnp.exp(logits - top)
        total = jnp.sum(grown, axis=1, keepdims=True)
        hit = metas[rows, STEPS + t : STEPS + t + 1] == part_lanes
        picked = jnp.sum(jnp.where(hit, logits, 0.0), axis=1, keepdims=True)
        low = ((grown / total - jnp.where(hit, 1.0, 0.0)) / STEPS).astype(BF16)
        dlog[t, rows] = low
        at = part_rows + part * PART
        ours = (at >= k * 64) & (at < k * 64 + 64)
        term = jnp.where(ours, (top + jnp.log(total) - picked) / STEPS, 0.0)
        totals["loss"] = totals["loss"] + jnp.sum(term, axis=0, keepdims=True)
        totals["bias"] = totals["bias"] + jnp.sum(jnp.where(ours, low.astype(F32), 0.0), axis=0, keepdims=True)

    far_copy().start()
    for part in range(SPLIT):
        forward(0, part)
    far_copy(False).wait_recv()
    over_copy().start()
    for part in range(SPLIT):
        h_wait(0, part)
        forward(1, part)
    over_copy(False).wait_recv()
    for xs in (0, 1):
        twin_copy(xs).start()
    for part in range(SPLIT):
        h_wait(1, part)
        forward(2, part)
    for xs in (0, 1):
        twin_copy(xs, False).wait_recv()
    for part in range(SPLIT):
        decode(0, part)
    for part in range(SPLIT):
        h_wait(2, part)
        forward(3, part)
    for part in range(SPLIT):
        decode(1, part)
    hx_out = pltpu.make_async_copy(hx.at[pl.ds(0, STEPS)], hx_o, out_sem.at[0])
    hx_out.start()
    for part in range(SPLIT):
        decode(2, part)

    emb[...] = jnp.zeros_like(emb)
    dcn[...] = jnp.zeros_like(dcn)

    def b_copy(t, part, d):
        rows = pl.ds(part * PART, PART)
        return remote(
            pbuf.at[t - 1, d - 1, rows],
            rbuf.at[t - 1, d - 1, rows],
            b_send.at[t - 1, part, d - 1],
            b_recv.at[t - 1, part, d - 1],
            peers[d]["dev"],
        )

    def backward(t, part):
        rows = pl.ds(part * PART, PART)
        if t < STEPS - 1:
            for d in (1, 2, 3):
                b_copy(t + 1, part, d).wait_recv()
        for xb in (0, 1):
            dh = dot_nt(dlog[t, rows], wo[mine[xb]].reshape(ROWS, CHARS))
            wide = pl.ds(xb * ROWS, ROWS)
            if t < STEPS - 1:
                dh = dh + ownp[rows, wide]
                for d in (1, 2, 3):
                    dh = dh + rbuf[t, d - 1, rows, wide].astype(F32)
            gate_i = act[t, xb, rows]
            gate_f = act[t, 2 + xb, rows]
            gate_g = act[t, 4 + xb, rows]
            gate_o = act[t, 6 + xb, rows]
            shown = jnp.tanh(call[t + 1, xb, rows])
            dc = dcn[xb, rows] + dh * gate_o * (1.0 - shown * shown)
            dcn[xb, rows] = dc * gate_f
            dg[t, rows, pl.ds(xb * ROWS, ROWS)] = (dc * gate_g * gate_i * (1.0 - gate_i)).astype(BF16)
            dg[t, rows, pl.ds((2 + xb) * ROWS, ROWS)] = (
                dc * call[t, xb, rows] * gate_f * (1.0 - gate_f)
            ).astype(BF16)
            dg[t, rows, pl.ds((4 + xb) * ROWS, ROWS)] = (dc * gate_i * (1.0 - gate_g * gate_g)).astype(BF16)
            dg[t, rows, pl.ds((6 + xb) * ROWS, ROWS)] = (dh * shown * gate_o * (1.0 - gate_o)).astype(BF16)
        if t > 0:
            for d in (3, 1, 2):
                there = peers[d]
                for xb in (0, 1):
                    pbuf[t - 1, d - 1, rows, pl.ds(xb * ROWS, ROWS)] = dot(
                        dg[t, rows, :], w2[:, cols(stripe(there["y"], there["zi"], xb))]
                    ).astype(BF16)
                b_copy(t, part, d).start()
            for xb in (0, 1):
                ownp[rows, pl.ds(xb * ROWS, ROWS)] = dot(dg[t, rows, :], w2[:, cols(mine[xb])])
        else:

            def unit(j, carry):
                dh0_o[rows, cols(j)] = dot(dg[0, rows, :], w2[:, cols(j)])
                return carry

            lax.fori_loop(0, HID // ROWS, unit, 0)

    def extras(t):
        dx = dot(dg[t], w2[:, pl.ds(HID, WIDE - HID)])
        high = dx.astype(BF16)
        rest = (dx - high.astype(F32)).astype(BF16)
        one = jnp.where(metas[:, t : t + 1] == lanes, 1.0, 0.0).astype(BF16)
        emb[...] += dot_tn(one, high) + dot_tn(one, rest)

    def d_copy(n):
        return remote(d_out.at[n], d_in.at[n], d_send.at[n], d_recv.at[n], quad_to(*quad[n]))

    def f_copy(xb):
        return remote(f_out.at[xb], f_in.at[p], f_send.at[xb], f_recv.at[p], (final_to(xb), shard))

    def f_wait(n):
        remote(f_out.at[n], f_in.at[n], f_send.at[n], f_recv.at[n], across).wait_recv()

    def decoder_start():
        for xb in (0, 1):
            total = dot_tn(hx[1, :, cols(mine[xb])], dlog[0])
            for t in range(1, STEPS):
                total = total + dot_tn(hx[t + 1, :, cols(mine[xb])], dlog[t])
            dpart[xb] = total
        for n, (dx, dc) in enumerate(quad):
            theirs = 2 * flip(x, dx) + flip(c, dc)
            for xb in (0, 1):
                d_out[n, xb] = dpart[xb, aligned(theirs * 64, 64), :].astype(BF16)
            d_copy(n).start()

    def decoder_middle():
        for n in range(3):
            d_copy(n).wait_recv()
        for xb in (0, 1):
            part = dpart[xb, aligned(shard * 64, 64), :]
            for n in range(3):
                part = part + d_in[n, xb].astype(F32)
            f_out[xb] = part.astype(BF16)

            @pl.when(final_to(xb) != dp)
            def _():
                f_copy(xb).start()

            @pl.when(final_to(xb) == dp)
            def _():
                f_in[p] = f_out[xb]

    def decoder_end():
        for n in (0, 1):

            @pl.when(final_from(n) != dp)
            def _():
                f_wait(n)

        gdec_o[...] = f_in[0].astype(F32) + f_in[1].astype(F32)

    for part in range(SPLIT):
        h_wait(STEPS - 1, part)
        decode(STEPS - 1, part)
        backward(STEPS - 1, part)
    decoder_start()
    extras(STEPS - 1)
    dg_out = [pltpu.make_async_copy(dg.at[t], dg_o.at[t], out_sem.at[1 + t]) for t in range(STEPS)]
    dg_out[STEPS - 1].start()
    for t in reversed(range(STEPS - 1)):
        for part in range(SPLIT):
            backward(t, part)
        dg_out[t].start()
        if t == STEPS - 2:
            decoder_middle()
        extras(t)
    decoder_end()

    for xb in (0, 1):
        dc0_o[:, pl.ds(xb * ROWS, ROWS)] = dcn[xb]
    at_row = lax.broadcasted_iota(jnp.int32, (288, 128), 0)
    at_col = lax.broadcasted_iota(jnp.int32, (288, 128), 1)
    block = jnp.where((at_row < 275) & (at_col < INPUTS), emb[pl.ds(0, 288), :], 0.0)
    for n in range(3):
        block = jnp.where(at_row == 276 + n, totals["bias"][:, n * 128 : n * 128 + 128], block)
    block = jnp.where((at_row == 279) & (at_col == 0), totals["loss"], block)
    emb_o[...] = block

    for q in range(SLICES):
        for target in (0, 1):

            @pl.when(c + 2 * target != z)
            def _():
                z_copy(target, q).wait_send()

        for n in (0, 1):
            x_copy(gates[n], q).wait_send()
            c_copy(gates[n], q, n, False).wait_send()
            c_copy(gates[n], q, n, True).wait_send()
    for n in range(5):
        for d in (1, 2):
            group_copy(d, n).wait_send()
        if n < 3:
            corner_copy(n).wait_send()
        else:
            group_copy(3, n).wait_send()
    for n in range(3):
        d_copy(n).wait_send()
    for xb in (0, 1):

        @pl.when(final_to(xb) != dp)
        def _():
            f_copy(xb).wait_send()

    far_copy().wait_send()
    over_copy().wait_send()
    for xs in (0, 1):
        twin_copy(xs).wait_send()
    for t in range(STEPS):
        for part in range(SPLIT):
            for d in (1, 2, 3):
                for xb in (0, 1):
                    h_copy(t, part, xb, d).wait_send()
                if t > 0:
                    b_copy(t, part, d).wait_send()
    hx_out.wait()
    for t in range(STEPS):
        dg_out[t].wait()


def sum_kernel(
    dg,
    hx,
    dh0,
    dc0,
    emb,
    gdec_own,
    grad_o,
    emb_o,
    norm_o,
    gh_o,
    gc_o,
    c_out,
    c_in,
    kept,
    x_out,
    x_in,
    z_out,
    z_in,
    gh_out,
    gh_in,
    gc_out,
    gc_in,
    e_in,
    n_out,
    n_in,
    c_send,
    c_recv,
    x_send,
    x_recv,
    z_send,
    z_recv,
    g_send,
    g_recv,
    e_send,
    e_recv,
    n_send,
    n_recv,
):
    s = spots()
    z, y, x, c, k, zi, p = s["z"], s["y"], s["x"], s["c"], s["k"], s["zi"], s["p"]
    dp, shard = s["dp"], s["shard"]
    across = device(s, x=1 - x)
    twin = device(s, c=1 - c)
    far = device(s, z=2 * (1 - p) + zi)
    peers = {d: peer(s, d) for d in (1, 2, 3)}
    core = z % 2
    column = [(dz, dc) for dz in range(4) for dc in range(2) if (dz, dc) != (0, 0)]
    plane = [(dy, dx) for dy in range(2) for dx in range(2) if (dy, dx) != (0, 0)]

    def flip(value, by):
        return 1 - value if by else value

    def column_to(dz, dc):
        return device(s, z=(z + dz) % 4, c=flip(c, dc))

    def column_from(dz, dc):
        return device(s, z=(z + 4 - dz) % 4, c=flip(c, dc))

    def plane_to(dy, dx):
        return device(s, y=flip(y, dy), x=flip(x, dx))

    for dz, dc in column:
        signal(column_from(dz, dc))
    for dy, dx in plane:
        signal(plane_to(dy, dx))
    signal(peers[3]["dev"])
    pl.semaphore_wait(pltpu.get_barrier_semaphore(), 11)

    def state_copies(d, sender=True):
        there = peers[d]
        rows = aligned(there["k"] * 64, 64)
        result = [
            remote(gh_out.at[d - 1], gh_in.at[d - 1], g_send.at[d - 1, 0], g_recv.at[d - 1, 0], there["dev"]),
            remote(gc_out.at[d - 1], gc_in.at[d - 1], g_send.at[d - 1, 1], g_recv.at[d - 1, 1], there["dev"]),
        ]
        return result

    def early():
        for d in (3, 1, 2):
            rows = aligned(peers[d]["k"] * 64, 64)
            gh_out[d - 1] = dh0[rows, :].astype(BF16)
            gc_out[d - 1] = dc0[rows, :].astype(BF16)
            for copy in state_copies(d):
                copy.start()

    tiles = ((0, 512), (512, 512), (1024, 512), (1536, 640))

    def block_of(b, store):
        for start, size in tiles:
            at = pl.ds(start, size)
            store(at, dot_tn(dg[:, cols(b)], hx[:, at]))

    def c_copy(n, q):
        rows = pl.ds(q * SLICE, SLICE)
        return remote(c_out.at[n, rows], c_in.at[n, rows], c_send.at[n, q], c_recv.at[n, q], twin)

    def x_copy(i, q):
        rows = pl.ds(q * SLICE, SLICE)
        return remote(x_out.at[i, rows], x_in.at[i, rows], x_send.at[i, q], x_recv.at[i, q], across)

    def z_copy(i, q):
        rows = pl.ds(q * SLICE, SLICE)
        return remote(
            z_out.at[i, rows],
            z_in.at[p, rows],
            z_send.at[i, q],
            z_recv.at[p, q],
            device(s, z=c + 2 * gates[i], c=core),
        )

    def z_wait(n, q):
        rows = pl.ds(q * SLICE, SLICE)
        remote(z_out.at[n, rows], z_in.at[n, rows], z_send.at[n, q], z_recv.at[n, q], across).wait_recv()

    def for_twin(n, b):
        def store(at, value):
            c_out[n, :, at] = value.astype(BF16)

        block_of(b, store)
        for q in range(SLICES):
            c_copy(n, q).start()

    def keep(i, b):
        def store(at, value):
            kept[i, :, at] = value

        block_of(b, store)

    def add_twin(i, n, q):
        rows = pl.ds(q * SLICE, SLICE)
        c_copy(n, q).wait_recv()
        return kept[i, rows] + c_in[n, rows].astype(F32)

    half = aligned(c * 144, 144)
    rest = aligned((1 - c) * 144, 144)
    hops = (twin, across, far, peers[2]["dev"], peers[1]["dev"], twin)

    def e_copy(n):
        if n == 0:
            return remote(emb_o.at[rest], e_in.at[0], e_send.at[0], e_recv.at[0], hops[0])
        if n == 5:
            return remote(emb_o.at[half], e_in.at[5], e_send.at[5], e_recv.at[5], hops[5])
        return remote(e_out_of(n), e_in.at[n], e_send.at[n], e_recv.at[n], hops[n])

    def e_out_of(n):
        return e_in.at[5 + n]

    def e_start(n):
        if n in (1, 2, 3, 4):
            e_in[5 + n] = emb_o[half, :]
        e_copy(n).start()

    def e_finish(n):
        if n == 5:
            e_copy(5).wait()
            emb_o[rest, :] = e_in[5]
            return
        e_copy(n).wait()
        emb_o[half, :] = emb_o[half, :] + e_in[n]

    gates = (1 - p, p)

    def pass_on(n, q):
        i = gates[n]
        rows = pl.ds(q * SLICE, SLICE)
        x_copy(n, q).wait_recv()
        total = add_twin(n, 2 + n, q) + x_in[n, rows].astype(F32)
        z_out[n, rows] = total.astype(BF16)

        @pl.when(c + 2 * i != z)
        def _():
            z_copy(n, q).start()

        @pl.when(c + 2 * i == z)
        def _():
            z_in[p, rows] = z_out[n, rows]

    def to_across(n):
        for q in range(SLICES):
            x_out[n, pl.ds(q * SLICE, SLICE)] = add_twin(2, n, q).astype(BF16)
            x_copy(n, q).start()

    emb_o[...] = emb[...]
    e_start(0)
    for_twin(0, 2 * (1 - c + 2 * gates[0]) + 1 - x)
    e_finish(0)
    e_start(1)
    keep(2, 2 * (c + 2 * gates[0]) + 1 - x)
    to_across(0)
    e_finish(1)
    e_start(2)
    for_twin(2, 2 * (1 - c + 2 * gates[0]) + x)
    keep(0, 2 * (c + 2 * gates[0]) + x)
    e_finish(2)
    e_start(3)
    for_twin(1, 2 * (1 - c + 2 * gates[1]) + 1 - x)
    keep(2, 2 * (c + 2 * gates[1]) + 1 - x)
    e_finish(3)
    e_start(4)
    for q in range(SLICES):
        pass_on(0, q)
        if q == 0:
            to_across(1)
            early()
        if q == 1:
            for_twin(3, 2 * (1 - c + 2 * gates[1]) + x)
        if q == 2:
            keep(1, 2 * (c + 2 * gates[1]) + x)
        if q == 3:
            e_finish(4)
            e_start(5)
    for q in range(SLICES):
        pass_on(1, q)
    e_finish(5)

    squares = jnp.zeros((1, 1), F32)

    def square_sum(value):
        return jnp.sum(jnp.sum(value * value, axis=1, keepdims=True), axis=0, keepdims=True)

    squares = squares + square_sum(gdec_own[...])
    for q in range(SLICES):
        rows = pl.ds(q * SLICE, SLICE)
        for n in (0, 1):

            @pl.when(jnp.logical_or(core != c, p != n))
            def _():
                z_wait(n, q)

        final = z_in[0, rows].astype(F32) + z_in[1, rows].astype(F32)
        grad_o[rows, :] = final
        squares = squares + square_sum(final)

    def n_copy(n):
        if n < 7:
            return remote(n_out.at[0], n_in.at[n], n_send.at[n], n_recv.at[n], column_to(*column[n]))
        return remote(n_out.at[1], n_in.at[n], n_send.at[n], n_recv.at[n], plane_to(*plane[n - 7]))

    n_out[0] = jnp.broadcast_to(squares, (8, 128))
    for n in range(7):
        n_copy(n).start()
    own = aligned(k * 64, 64)
    total = dh0[own, :]
    for d in (1, 2, 3):
        for copy in state_copies(d):
            copy.wait_recv()
        total = total + gh_in[d - 1].astype(F32)
    gh_o[...] = total
    for xb in (0, 1):
        gc_o[:, cols(stripe(y, zi, xb))] = dc0[own, pl.ds(xb * ROWS, ROWS)]
        for d in (1, 2, 3):
            there = peers[d]
            gc_o[:, cols(stripe(there["y"], there["zi"], xb))] = gc_in[d - 1, :, pl.ds(xb * ROWS, ROWS)].astype(F32)
    total = n_out[0]
    for n in range(7):
        n_copy(n).wait_recv()
        total = total + n_in[n]
    n_out[1] = total
    for n in range(7, 10):
        n_copy(n).start()
    at_row = lax.broadcasted_iota(jnp.int32, (288, 128), 0)
    shared = square_sum(jnp.where(at_row == 279, 0.0, emb_o[...]))
    for n in range(7, 10):
        n_copy(n).wait_recv()
        total = total + n_in[n]
    norm_o[...] = total + shared

    for n in range(4):
        for q in range(SLICES):
            c_copy(n, q).wait_send()
    for i in (0, 1):
        for q in range(SLICES):
            x_copy(i, q).wait_send()

            @pl.when(c + 2 * gates[i] != z)
            def _():
                z_copy(i, q).wait_send()

    for d in (1, 2, 3):
        for copy in state_copies(d):
            copy.wait_send()
    for n in range(10):
        n_copy(n).wait_send()


def finish_kernel(
    streams_all,
    grad,
    emb,
    squares,
    gdec,
    gh,
    gc,
    m_embed,
    m_input,
    m_hidden,
    m_gate,
    m_decoder,
    m_outbias,
    loss_o,
    norm_o,
    gh_o,
    gc_o,
    g_embed,
    g_input,
    g_hidden,
    g_gate,
    g_decoder,
    g_outbias,
    n_embed,
    n_input,
    n_hidden,
    n_gate,
    n_decoder,
    n_outbias,
):
    norm = jnp.sqrt(squares[0:1, 0:1])
    norm_o[0] = norm[0, 0]
    factor = CLIP / jnp.maximum(norm, CLIP)
    loss_o[0] = emb[279, 0] / streams_all
    gh_o[...] = gh[...]
    gc_o[...] = gc[...]

    def out(value, momentum, grad_ref, new_ref):
        grad_ref[...] = value
        new_ref[...] = MOMENTUM * momentum[...] + factor * value

    vocab = m_outbias.shape[1]
    out(emb[pl.ds(0, vocab), pl.ds(0, INPUTS)], m_embed, g_embed, n_embed)
    turned = grad[:, pl.ds(HID, WIDE - HID)].T
    out(turned[0:INPUTS, :], m_input, g_input, n_input)
    out(turned[INPUTS : INPUTS + 1, :], m_gate, g_gate, n_gate)
    out(grad[:, pl.ds(0, HID)], m_hidden, g_hidden, n_hidden)
    out(gdec[:, pl.ds(0, vocab)], m_decoder, g_decoder, n_decoder)
    row = jnp.concatenate([emb[276 + n : 277 + n, :] for n in range(3)], axis=1)
    out(row[:, 0:vocab], m_outbias, g_outbias, n_outbias)


def split_local(
    char_ids,
    targets,
    hidden_start,
    cell_start,
    embedding,
    input_weight,
    hidden_weight,
    gate_bias,
    decoder_weight,
    decoder_bias,
    momentum_embed,
    momentum_input,
    momentum_hidden,
    momentum_gate,
    momentum_decoder,
    momentum_outbias,
):
    streams = char_ids.shape[0]
    vocab = embedding.shape[0]
    shape = jax.ShapeDtypeStruct
    vm = pl.BlockSpec(memory_space=pltpu.VMEM)
    hbm = pl.BlockSpec(memory_space=pl.ANY)
    dma = pltpu.SemaphoreType.DMA
    hx, dg, dh0, dc0, emb, gdec_own = pl.pallas_call(
        step_kernel,
        out_shape=(
            shape((STEPS, ROWS, WIDE), BF16),
            shape((STEPS, ROWS, HID), BF16),
            shape((ROWS, HID), F32),
            shape((ROWS, 512), F32),
            shape((288, 128), F32),
            shape((64, CHARS), F32),
        ),
        in_specs=[vm] * 10,
        out_specs=(hbm, hbm, vm, vm, vm, vm),
        scratch_shapes=[
            pltpu.VMEM((HID, WIDE), BF16),
            pltpu.VMEM((8, WIDE, ROWS), BF16),
            pltpu.VMEM((STEPS + 1, ROWS, WIDE), BF16),
            pltpu.VMEM((STEPS, 8, ROWS, ROWS), F32),
            pltpu.VMEM((STEPS + 1, 2, ROWS, ROWS), F32),
            pltpu.VMEM((STEPS, ROWS, HID), BF16),
            pltpu.VMEM((STEPS - 1, 3, ROWS, 512), BF16),
            pltpu.VMEM((STEPS - 1, 3, ROWS, 512), BF16),
            pltpu.VMEM((ROWS, 512), F32),
            pltpu.VMEM((2, ROWS, ROWS), F32),
            pltpu.VMEM((8, 4, 64, CHARS), BF16),
            pltpu.VMEM((STEPS, ROWS, CHARS), BF16),
            pltpu.VMEM((ROWS, 128), jnp.int32),
            pltpu.VMEM((CHARS, 128), F32),
            pltpu.VMEM((2, ROWS, ROWS), BF16),
            pltpu.VMEM((2, ROWS, CHARS), F32),
            pltpu.VMEM((3, 2, 64, CHARS), BF16),
            pltpu.VMEM((3, 2, 64, CHARS), BF16),
            pltpu.VMEM((2, 64, CHARS), BF16),
            pltpu.VMEM((2, 64, CHARS), BF16),
            pltpu.VMEM((ROWS, WIDE), BF16),
            pltpu.VMEM((64, HID), BF16),
            pltpu.VMEM((64, HID), BF16),
            pltpu.VMEM((64, 128), jnp.int32),
            pltpu.VMEM((64, CHARS), BF16),
            pltpu.VMEM((CHARS, 128), F32),
            pltpu.VMEM((8, CHARS), F32),
            pltpu.VMEM((128, ROWS), F32),
            pltpu.VMEM((128, 128), jnp.int32),
            dma((3, 5)),
            dma((3, 5)),
            dma((2, SLICES)),
            dma((2, SLICES)),
            dma((2, SLICES)),
            dma((2, SLICES)),
            dma((2, 2, SLICES)),
            dma((2, 2, SLICES)),
            dma((4,)),
            dma((4,)),
            dma((STEPS, SPLIT, 2, 3)),
            dma((STEPS, SPLIT, 2, 3)),
            dma((STEPS - 1, SPLIT, 3)),
            dma((STEPS - 1, SPLIT, 3)),
            dma((3,)),
            dma((3,)),
            dma((2,)),
            dma((2,)),
            dma((1 + STEPS,)),
        ],
        compiler_params=pltpu.CompilerParams(
            collective_id=0, has_side_effects=True, vmem_limit_bytes=60 * 2**20
        ),
    )(
        char_ids.T,
        targets.T,
        hidden_start,
        cell_start,
        embedding,
        input_weight.T,
        hidden_weight,
        gate_bias[None, :],
        decoder_weight,
        decoder_bias[None, :],
    )
    grad, emb, norm, grad_hidden_start, grad_cell_start = pl.pallas_call(
        sum_kernel,
        out_shape=(
            shape((ROWS, WIDE), F32),
            shape((288, 128), F32),
            shape((8, 128), F32),
            shape((64, HID), F32),
            shape((64, HID), F32),
        ),
        in_specs=[vm] * 6,
        out_specs=(vm,) * 5,
        scratch_shapes=[
            pltpu.VMEM((4, ROWS, WIDE), BF16),
            pltpu.VMEM((4, ROWS, WIDE), BF16),
            pltpu.VMEM((3, ROWS, WIDE), F32),
            pltpu.VMEM((2, ROWS, WIDE), BF16),
            pltpu.VMEM((2, ROWS, WIDE), BF16),
            pltpu.VMEM((2, ROWS, WIDE), BF16),
            pltpu.VMEM((2, ROWS, WIDE), BF16),
            pltpu.VMEM((3, 64, HID), BF16),
            pltpu.VMEM((3, 64, HID), BF16),
            pltpu.VMEM((3, 64, 512), BF16),
            pltpu.VMEM((3, 64, 512), BF16),
            pltpu.VMEM((10, 144, 128), F32),
            pltpu.VMEM((2, 8, 128), F32),
            pltpu.VMEM((10, 8, 128), F32),
            dma((4, SLICES)),
            dma((4, SLICES)),
            dma((2, SLICES)),
            dma((2, SLICES)),
            dma((2, SLICES)),
            dma((2, SLICES)),
            dma((3, 2)),
            dma((3, 2)),
            dma((6,)),
            dma((6,)),
            dma((10,)),
            dma((10,)),
        ],
        compiler_params=pltpu.CompilerParams(
            collective_id=1, has_side_effects=True, vmem_limit_bytes=60 * 2**20
        ),
    )(dg.reshape(STEPS * ROWS, HID), hx.reshape(STEPS * ROWS, WIDE), dh0, dc0, emb, gdec_own)
    streams_all = streams * lax.axis_size("dp") * lax.axis_size("shard")
    whole = lambda a: pl.BlockSpec(a, lambda n: (0, 0))
    rows = lambda r, w: pl.BlockSpec((r, w), lambda n: (n, 0))
    lanes = lambda r: pl.BlockSpec((r, ROWS // 2), lambda n: (0, n))
    weights = [
        (whole((vocab, INPUTS)), (vocab, INPUTS)),
        (lanes(INPUTS), (INPUTS, ROWS)),
        (rows(ROWS // 2, HID), (ROWS, HID)),
        (lanes(1), (1, ROWS)),
        (whole((64, vocab)), (64, vocab)),
        (whole((1, vocab)), (1, vocab)),
    ]
    state = (rows(32, HID), (64, HID))
    scalar = (pl.BlockSpec(memory_space=pltpu.SMEM), (1,))
    results = [scalar, scalar, state, state] + weights + weights
    loss, norm, gh, gc, *rest = pl.pallas_call(
        functools.partial(finish_kernel, float(streams_all)),
        grid=(2,),
        out_shape=[shape(dims, F32) for _, dims in results],
        in_specs=[
            rows(ROWS // 2, WIDE),
            whole((288, 128)),
            whole((8, 128)),
            whole((64, CHARS)),
            state[0],
            state[0],
        ]
        + [spec for spec, _ in weights],
        out_specs=[spec for spec, _ in results],
        compiler_params=pltpu.CompilerParams(vmem_limit_bytes=60 * 2**20),
    )(
        grad,
        emb,
        norm,
        gdec_own,
        grad_hidden_start,
        grad_cell_start,
        momentum_embed,
        momentum_input.T,
        momentum_hidden,
        momentum_gate[None, :],
        momentum_decoder,
        momentum_outbias[None, :],
    )
    for n in (0, 6):
        rest[n + 1] = rest[n + 1].T
        rest[n + 3] = rest[n + 3].reshape(-1)
        rest[n + 5] = rest[n + 5].reshape(-1)
    return (loss, norm, gh, gc, *rest)


def solution(mesh):
    fits = mesh.shape["dp"] == 8 and mesh.shape["shard"] == 4
    placed = (
        P(("dp", "shard"), None),
        P(("dp", "shard"), None),
        P(("dp", "shard"), None),
        P(("dp", "shard"), None),
        P(),
        P(("dp", "shard"), None),
        P(("dp", "shard"), None),
        P(("dp", "shard")),
        P(("dp", "shard"), None),
        P(),
        P(),
        P(("dp", "shard"), None),
        P(("dp", "shard"), None),
        P(("dp", "shard")),
        P(("dp", "shard"), None),
        P(),
    )
    return jax.shard_map(
        split_local if fits else local,
        mesh=mesh,
        in_specs=placed,
        out_specs=(
            P(),
            P(),
            P(("dp", "shard"), None),
            P(("dp", "shard"), None),
            P(),
            P(("dp", "shard"), None),
            P(("dp", "shard"), None),
            P(("dp", "shard")),
            P(("dp", "shard"), None),
            P(),
            P(),
            P(("dp", "shard"), None),
            P(("dp", "shard"), None),
            P(("dp", "shard")),
            P(("dp", "shard"), None),
            P(),
        ),
        check_vma=False,
    )
```

```python
import functools

import jax
import jax.numpy as jnp
from jax import lax
from jax.experimental import pallas as pl
from jax.experimental.pallas import tpu as pltpu
from jax.sharding import PartitionSpec as P

MESH = pl.DeviceIdType.MESH
F32 = jnp.float32
BF16 = jnp.bfloat16

MICRO = 2


CLIP = 0.25
MOMENTUM = 0.5


def contract_rows(left, right):
    return lax.dot_general(
        left, right, (((0,), (0,)), ((), ())), preferred_element_type=jnp.float32
    )


def contract_last(left, right):
    return lax.dot_general(
        left, right, (((1,), (1,)), ((), ())), preferred_element_type=jnp.float32
    )


def local(
    char_ids,
    targets,
    hidden_start,
    cell_start,
    embedding,
    input_weight,
    hidden_weight,
    gate_bias,
    decoder_weight,
    decoder_bias,
    momentum_embed,
    momentum_input,
    momentum_hidden,
    momentum_gate,
    momentum_decoder,
    momentum_outbias,
):
    streams, seq_len = char_ids.shape
    micro_rows = streams // MICRO
    vocab_size = embedding.shape[0]
    hidden_size = hidden_start.shape[1]
    low_input = input_weight.astype(jnp.bfloat16)
    low_hidden = hidden_weight.astype(jnp.bfloat16)
    low_bias = gate_bias.astype(jnp.bfloat16)
    low_decoder = decoder_weight.astype(jnp.bfloat16)
    inner_rows = (
        lax.all_gather(low_input, "shard", axis=0, tiled=True),
        lax.all_gather(low_hidden, "shard", axis=0, tiled=True),
        lax.all_gather(low_bias, "shard", axis=0, tiled=True),
        lax.all_gather(low_decoder, "shard", axis=0, tiled=True),
    )
    weight_in, weight_rec, bias_low, weight_out = (
        lax.all_gather(inner_rows[0], "dp", axis=0, tiled=True),
        lax.all_gather(inner_rows[1], "dp", axis=0, tiled=True),
        lax.all_gather(inner_rows[2], "dp", axis=0, tiled=True),
        lax.all_gather(inner_rows[3], "dp", axis=0, tiled=True),
    )
    columns = jnp.arange(vocab_size, dtype=jnp.int32)
    table = embedding.astype(jnp.bfloat16)
    bias_row = bias_low.astype(jnp.float32)[None, :]

    def forward_step(carried, input_now):
        hidden_low, cell = carried
        preact = input_now + contract_last(hidden_low, weight_rec)
        input_gate = jax.nn.sigmoid(preact[:, :hidden_size])
        forget_gate = jax.nn.sigmoid(preact[:, hidden_size : 2 * hidden_size])
        candidate = jnp.tanh(preact[:, 2 * hidden_size : 3 * hidden_size])
        output_gate = jax.nn.sigmoid(preact[:, 3 * hidden_size :])
        cell_next = forget_gate * cell + input_gate * candidate
        hidden_next = (output_gate * jnp.tanh(cell_next)).astype(jnp.bfloat16)
        activations = jnp.concatenate([input_gate, forget_gate, candidate, output_gate], axis=1)
        return ((hidden_next, cell_next), (hidden_low, cell, activations, cell_next, hidden_next))

    def backward_step(carried, inputs):
        hidden_grad_next, cell_grad_next = carried
        out_grad, cell_before, gate_values, cell_now = inputs
        hidden_grad = out_grad + hidden_grad_next
        input_gate = gate_values[:, :hidden_size]
        forget_gate = gate_values[:, hidden_size : 2 * hidden_size]
        candidate = gate_values[:, 2 * hidden_size : 3 * hidden_size]
        output_gate = gate_values[:, 3 * hidden_size :]
        cell_tanh = jnp.tanh(cell_now)
        cell_grad = cell_grad_next + hidden_grad * output_gate * (1.0 - cell_tanh * cell_tanh)
        input_term = cell_grad * candidate * input_gate * (1.0 - input_gate)
        forget_term = cell_grad * cell_before * forget_gate * (1.0 - forget_gate)
        candidate_term = cell_grad * input_gate * (1.0 - candidate * candidate)
        output_term = hidden_grad * cell_tanh * output_gate * (1.0 - output_gate)
        gate_grad = jnp.concatenate(
            [input_term, forget_term, candidate_term, output_term], axis=1
        ).astype(jnp.bfloat16)
        hidden_grad_prev = jnp.dot(gate_grad, weight_rec, preferred_element_type=jnp.float32)
        return ((hidden_grad_prev, cell_grad * forget_gate), gate_grad)

    def micro_pass(loss_total, inputs):
        ids_part, target_part, hidden_part, cell_part = inputs
        batch_rows = ids_part.shape[0]
        token_ids = ids_part.T.reshape(-1)
        token_targets = target_part.T.reshape(-1)
        one_input = (token_ids[:, None] == columns[None, :]).astype(jnp.bfloat16)
        one_target = (token_targets[:, None] == columns[None, :]).astype(jnp.float32)
        embedded = jnp.dot(one_input, table, preferred_element_type=jnp.float32).astype(
            jnp.bfloat16
        )
        input_part = contract_last(embedded, weight_in) + bias_row
        input_part = input_part.reshape(seq_len, batch_rows, 4 * hidden_size)
        start_pair = (hidden_part.astype(jnp.bfloat16), cell_part)
        final_pair, saved = lax.scan(forward_step, start_pair, input_part)
        hidden_prev, cell_prev, activations, cell_after, hidden_after = saved
        hidden_rows = hidden_after.reshape(seq_len * batch_rows, hidden_size)
        logits = (
            jnp.dot(hidden_rows, weight_out, preferred_element_type=jnp.float32)
            + decoder_bias[None, :]
        )
        log_total = jax.nn.logsumexp(logits, axis=1)
        local_loss = jnp.sum(log_total - jnp.sum(one_target * logits, axis=1)) / seq_len
        probs = jnp.exp(logits - log_total[:, None])
        logit_grad = ((probs - one_target) / seq_len).astype(jnp.bfloat16)
        hidden_from_out = contract_last(logit_grad, weight_out).reshape(
            seq_len, batch_rows, hidden_size
        )
        zero_state = jnp.zeros((batch_rows, hidden_size), jnp.float32)
        start_grads, gate_grads = lax.scan(
            backward_step,
            (zero_state, zero_state),
            (hidden_from_out, cell_prev, activations, cell_after),
            reverse=True,
        )
        gate_rows = gate_grads.reshape(seq_len * batch_rows, 4 * hidden_size)
        prev_rows = hidden_prev.reshape(seq_len * batch_rows, hidden_size)
        return (
            loss_total + local_loss,
            (
                token_ids,
                embedded,
                logit_grad,
                hidden_rows,
                gate_rows,
                prev_rows,
                start_grads[0],
                start_grads[1],
            ),
        )

    def by_micro(array):
        return array.reshape((MICRO, micro_rows) + array.shape[1:])

    local_loss, stacked = lax.scan(
        micro_pass,
        jnp.zeros((), jnp.float32),
        (by_micro(char_ids), by_micro(targets), by_micro(hidden_start), by_micro(cell_start)),
    )
    token_ids, embedded, logit_grad, hidden_rows, gate_rows, prev_rows, hidden_grads, cell_grads = (
        stacked
    )
    token_ids = token_ids.reshape(-1)
    embedded = embedded.reshape(-1, embedded.shape[-1])
    logit_grad = logit_grad.reshape(-1, vocab_size)
    hidden_rows = hidden_rows.reshape(-1, hidden_size)
    gate_rows = gate_rows.reshape(-1, 4 * hidden_size)
    prev_rows = prev_rows.reshape(-1, hidden_size)
    grad_hidden_start = hidden_grads.reshape(streams, hidden_size)
    grad_cell_start = cell_grads.reshape(streams, hidden_size)
    grad_outbias_local = jnp.sum(logit_grad.astype(jnp.float32), axis=0)
    grad_decoder_local = contract_rows(hidden_rows, logit_grad)
    grad_input_local = contract_rows(gate_rows, embedded)
    grad_hidden_local = contract_rows(gate_rows, prev_rows)
    grad_bias_local = jnp.sum(gate_rows.astype(jnp.float32), axis=0)
    embed_rows_grad = jnp.dot(gate_rows, weight_in, preferred_element_type=jnp.float32)
    one_all = (token_ids[:, None] == columns[None, :]).astype(jnp.float32)
    grad_embed_local = lax.dot_general(
        one_all,
        embed_rows_grad,
        (((0,), (0,)), ((), ())),
        precision=lax.Precision.HIGHEST,
        preferred_element_type=jnp.float32,
    )
    grad_embedding, grad_decoder_bias, loss_sum = lax.psum(
        (grad_embed_local, grad_outbias_local, local_loss), ("dp", "shard")
    )
    outer_sums = (
        lax.psum_scatter(
            grad_input_local.astype(jnp.bfloat16), "dp", scatter_dimension=0, tiled=True
        ).astype(jnp.float32),
        lax.psum_scatter(
            grad_hidden_local.astype(jnp.bfloat16), "dp", scatter_dimension=0, tiled=True
        ).astype(jnp.float32),
        lax.psum_scatter(
            grad_bias_local.astype(jnp.bfloat16), "dp", scatter_dimension=0, tiled=True
        ).astype(jnp.float32),
        lax.psum_scatter(
            grad_decoder_local.astype(jnp.bfloat16), "dp", scatter_dimension=0, tiled=True
        ).astype(jnp.float32),
    )
    grad_input_weight, grad_hidden_weight, grad_gate_bias, grad_decoder_weight = (
        lax.psum_scatter(
            outer_sums[0].astype(jnp.bfloat16), "shard", scatter_dimension=0, tiled=True
        ).astype(jnp.float32),
        lax.psum_scatter(
            outer_sums[1].astype(jnp.bfloat16), "shard", scatter_dimension=0, tiled=True
        ).astype(jnp.float32),
        lax.psum_scatter(
            outer_sums[2].astype(jnp.bfloat16), "shard", scatter_dimension=0, tiled=True
        ).astype(jnp.float32),
        lax.psum_scatter(
            outer_sums[3].astype(jnp.bfloat16), "shard", scatter_dimension=0, tiled=True
        ).astype(jnp.float32),
    )
    shard_squares = jnp.sum(grad_input_weight * grad_input_weight) + jnp.sum(
        grad_hidden_weight * grad_hidden_weight
    )
    shard_squares = (
        shard_squares
        + jnp.sum(grad_gate_bias * grad_gate_bias)
        + jnp.sum(grad_decoder_weight * grad_decoder_weight)
    )
    square_total = lax.psum(shard_squares, ("dp", "shard"))
    square_total = (
        square_total
        + jnp.sum(grad_embedding * grad_embedding)
        + jnp.sum(grad_decoder_bias * grad_decoder_bias)
    )
    grad_norm = jnp.sqrt(square_total)
    factor = CLIP / jnp.maximum(grad_norm, CLIP)
    streams_all = streams * lax.axis_size("dp") * lax.axis_size("shard")
    loss = loss_sum / streams_all
    momenta = (
        momentum_embed,
        momentum_input,
        momentum_hidden,
        momentum_gate,
        momentum_decoder,
        momentum_outbias,
    )
    weight_grads = (
        grad_embedding,
        grad_input_weight,
        grad_hidden_weight,
        grad_gate_bias,
        grad_decoder_weight,
        grad_decoder_bias,
    )
    new_momenta = [MOMENTUM * momenta[index] + factor * weight_grads[index] for index in range(6)]
    return (
        loss.reshape(1),
        grad_norm.reshape(1),
        grad_hidden_start,
        grad_cell_start,
        grad_embedding,
        grad_input_weight,
        grad_hidden_weight,
        grad_gate_bias,
        grad_decoder_weight,
        grad_decoder_bias,
        new_momenta[0],
        new_momenta[1],
        new_momenta[2],
        new_momenta[3],
        new_momenta[4],
        new_momenta[5],
    )


ROWS = 256
HID = 2048
WIDE = 2176
INPUTS = 100
CHARS = 384
SPLIT = 2
PART = ROWS // SPLIT
SLICES = 8
SLICE = ROWS // SLICES
STEPS = 4


def spots():
    dp = lax.axis_index("dp")
    shard = lax.axis_index("shard")
    return dict(
        p=dp // 4,
        zi=(dp // 2) % 2,
        z=dp // 2,
        y=dp % 2,
        k=dp % 4,
        x=shard // 2,
        c=shard % 2,
        dp=dp,
        shard=shard,
    )


def device(s, z=None, y=None, x=None, c=None):
    z = s["z"] if z is None else z
    y = s["y"] if y is None else y
    x = s["x"] if x is None else x
    c = s["c"] if c is None else c
    return (z * 2 + y, x * 2 + c)


def peer(s, d):
    y = 1 - s["y"] if d % 2 else s["y"]
    zi = 1 - s["zi"] if d // 2 else s["zi"]
    z = 2 * s["p"] + zi
    return dict(y=y, zi=zi, k=2 * zi + y, dev=(z * 2 + y, s["shard"]))


def stripe(y, zi, xb):
    return 4 * y + 2 * xb + zi


def cols(index):
    return pl.ds(pl.multiple_of(index * ROWS, ROWS), ROWS)


def aligned(start, size):
    return pl.ds(pl.multiple_of(start, size), size)


def remote(src, dst, send, recv, dev):
    return pltpu.make_async_remote_copy(
        src_ref=src, dst_ref=dst, send_sem=send, recv_sem=recv, device_id=dev, device_id_type=MESH
    )


def dot(left, right):
    return jnp.dot(left, right, preferred_element_type=F32)


def dot_nt(left, right):
    return lax.dot_general(left, right, (((1,), (1,)), ((), ())), preferred_element_type=F32)


def dot_tn(left, right):
    return lax.dot_general(left, right, (((0,), (0,)), ((), ())), preferred_element_type=F32)


def signal(dev):
    pl.semaphore_signal(
        pltpu.get_barrier_semaphore(), inc=1, device_id=dev, device_id_type=MESH
    )


def step_kernel(
    ids_in,
    targets_in,
    hidden_in,
    cell_in,
    embedding_in,
    input_in,
    weight_in,
    gate_in,
    decoder_in,
    outbias_in,
    hx_o,
    dgt_o,
    dg_o,
    w2_o,
    dc0_o,
    emb_o,
    gdec_o,
    w2,
    wt,
    hx,
    act,
    call,
    dg,
    dgt,
    pbuf,
    rbuf,
    ownp,
    dcn,
    wo,
    dlog,
    metas,
    emb,
    cells,
    dpart,
    d_out,
    d_in,
    f_out,
    f_in,
    wext,
    h_own,
    cell_own,
    meta_own,
    wout_own,
    table,
    dbias,
    narrow,
    ids_wide,
    g_send,
    g_recv,
    wz_send,
    wz_recv,
    wx_send,
    wx_recv,
    wc_send,
    wc_recv,
    o_send,
    o_recv,
    h_send,
    h_recv,
    b_send,
    b_recv,
    d_send,
    d_recv,
    f_send,
    f_recv,
    out_sem,
):
    s = spots()
    z, y, x, c, k, zi, p = s["z"], s["y"], s["x"], s["c"], s["k"], s["zi"], s["p"]
    dp, shard = s["dp"], s["shard"]
    across = device(s, x=1 - x)
    twin = device(s, c=1 - c)
    far = device(s, z=2 * (1 - p) + zi)
    peers = {d: peer(s, d) for d in (1, 2, 3)}
    mine = [stripe(y, zi, xb) for xb in (0, 1)]
    core = z % 2
    off_core = jnp.where(core == c, 0, 1)
    quad = [(dx, dc) for dx in range(2) for dc in range(2) if (dx, dc) != (0, 0)]

    def flip(value, by):
        return 1 - value if by else value

    def quad_to(dx, dc):
        return device(s, x=flip(x, dx), c=flip(c, dc))

    def final_to(xb):
        return 4 * y + 2 * xb + zi

    def final_from(half):
        return 4 * half + 2 * y + p

    for d in (1, 2, 3):
        signal(peers[d]["dev"])
    signal(across)
    signal(twin)
    signal(far)

    signal(device(s, x=1 - x, c=1 - c))

    @pl.when(core != c)
    def _():
        for i in (0, 1):
            signal(device(s, z=c + 2 * i, c=core))

    away = 0
    for n in (0, 1):

        @pl.when(final_from(n) != dp)
        def _():
            signal((final_from(n), shard))

        away = away + jnp.where(final_to(n) != dp, 1, 0)

    narrow[...] = jnp.zeros_like(narrow)
    narrow[pl.ds(0, INPUTS), :] = input_in[...]
    narrow[pl.ds(INPUTS, 1), :] = gate_in[...]
    wext[:, pl.ds(HID, WIDE - HID)] = narrow[...].T.astype(BF16)
    wext[:, pl.ds(0, HID)] = weight_in[...].astype(BF16)
    ids_wide[...] = jnp.zeros_like(ids_wide)
    ids_wide[pl.ds(0, STEPS), pl.ds(0, 64)] = ids_in[...]
    ids_wide[pl.ds(STEPS, STEPS), pl.ds(0, 64)] = targets_in[...]
    meta_own[...] = ids_wide[...].T[0:64, :]
    h_own[...] = hidden_in[...].astype(BF16)
    vocab = decoder_in.shape[1]
    wout_own[...] = jnp.zeros_like(wout_own)
    wout_own[:, pl.ds(0, vocab)] = decoder_in[...].astype(BF16)
    cell_own[...] = cell_in[...].astype(BF16)
    pl.semaphore_wait(pltpu.get_barrier_semaphore(), 7 + 2 * off_core + away)

    def z_copy(target, q):
        rows = pl.ds(q * SLICE, SLICE)
        slot = aligned((2 * z + x) * ROWS + q * SLICE, SLICE)
        return remote(
            wext.at[rows],
            w2.at[slot],
            wz_send.at[target, q],
            wz_recv.at[z // 2, q],
            device(s, z=c + 2 * target, c=core),
        )

    def z_wait(i, q):
        slot = aligned((2 * (c + 2 * i) + x) * ROWS + q * SLICE, SLICE)
        remote(wext.at[pl.ds(q * SLICE, SLICE)], w2.at[slot], wz_send.at[0, q], wz_recv.at[i, q], across).wait_recv()

    def x_copy(i, q, sender=True):
        xs = x if sender else 1 - x
        slot = aligned((2 * (c + 2 * i) + xs) * ROWS + q * SLICE, SLICE)
        return remote(w2.at[slot], w2.at[slot], wx_send.at[i, q], wx_recv.at[i, q], across)

    def c_copy(i, q, n, other, sender=True):
        xs = 1 - x if other else x
        cs = c if sender else 1 - c
        slot = aligned((2 * (cs + 2 * i) + xs) * ROWS + q * SLICE, SLICE)
        return remote(
            w2.at[slot], w2.at[slot], wc_send.at[n, int(other), q], wc_recv.at[n, int(other), q], twin
        )

    near = p
    beyond = 1 - p

    def start_beyond():
        for q in range(SLICES):

            @pl.when(c + 2 * beyond != z)
            def _():
                z_copy(beyond, q).start()

    pl.when(zi != p)(start_beyond)
    own = aligned(k * 64, 64)

    def group_copy(d, n):
        dev = peers[d]["dev"]
        send, recv = g_send.at[d - 1, n], g_recv.at[d - 1, n]
        if n == 0:
            return remote(meta_own, metas.at[own], send, recv, dev)
        if n == 1:
            return remote(h_own, hx.at[0, own, pl.ds(0, HID)], send, recv, dev)
        if n == 2:
            return remote(wout_own, wo.at[dp, shard], send, recv, dev)
        theirs = stripe(peers[d]["y"], peers[d]["zi"], n - 3)
        return remote(cell_own.at[:, cols(theirs)], cells.at[n - 3, own], send, recv, dev)

    def corner_copy(n, sender=True):
        there = peers[2 if sender else 3]
        rows = aligned(there["k"] * 64, 64)
        send, recv = g_send.at[2, n], g_recv.at[2, n]
        dev = peers[1]["dev"]
        if n == 0:
            part = metas.at[rows]
        elif n == 1:
            part = hx.at[0, rows, pl.ds(0, HID)]
        else:
            part = wo.at[there["dev"][0], shard]
        return remote(part, part, send, recv, dev)

    @pl.when(c + 2 * near == z)
    def _():
        w2[aligned((2 * z + x) * ROWS, ROWS), :] = wext[...]

    for q in range(SLICES):

        @pl.when(c + 2 * near != z)
        def _():
            z_copy(near, q).start()

        if q == 0:
            for n in (0, 2, 1):
                for d in (2, 1):
                    group_copy(d, n).start()
    for n in (3, 4):
        for d in (3, 2, 1):
            group_copy(d, n).start()
    pl.when(zi == p)(start_beyond)
    metas[own, :] = meta_own[...]
    hx[0, own, pl.ds(0, HID)] = h_own[...]
    wo[dp, shard] = wout_own[...]
    for xb in (0, 1):
        cells[xb, own] = cell_own[:, cols(mine[xb])]

    dbias[...] = jnp.full(dbias.shape, -1e30, F32)
    dbias[pl.ds(0, 1), pl.ds(0, vocab)] = outbias_in[...]
    table[...] = jnp.where(lax.broadcasted_iota(jnp.int32, table.shape, 1) == INPUTS, 1.0, 0.0)
    table[pl.ds(0, vocab), pl.ds(0, INPUTS)] = embedding_in[...].astype(BF16).astype(F32)

    def group_wait(d, n):
        there = peers[d]
        rows = aligned(there["k"] * 64, 64)
        send, recv = g_send.at[d - 1, n], g_recv.at[d - 1, n]
        if n == 0:
            copy = remote(meta_own, metas.at[rows], send, recv, there["dev"])
        elif n == 1:
            copy = remote(h_own, hx.at[0, rows, pl.ds(0, HID)], send, recv, there["dev"])
        elif n == 2:
            copy = remote(wout_own, wo.at[there["dev"][0], shard], send, recv, there["dev"])
        else:
            copy = remote(cell_own.at[:, cols(mine[n - 3])], cells.at[n - 3, rows], send, recv, there["dev"])
        copy.wait_recv()

    lanes = lax.broadcasted_iota(jnp.int32, (ROWS, CHARS), 1)

    def first_step(g):
        for xb in (0, 1):
            act[0, 2 * g + xb] = dot(hx[0], wt[2 * g + xb])

    def embed_inputs():
        for t in range(STEPS):
            one = jnp.where(metas[:, t : t + 1] == lanes, 1.0, 0.0).astype(BF16)
            hx[t, :, pl.ds(HID, WIDE - HID)] = dot(one, table[...].astype(BF16)).astype(BF16)

    def turn(b):
        wt[b] = w2[cols(b), :].T

    order = [(n, q) for n in (0, 1) for q in range(SLICES)]
    gates = (p, 1 - p)
    for at, (n, q) in enumerate(order):
        i = gates[n]

        @pl.when(c + 2 * i != z)
        def _():
            z_wait(i, q)

        x_copy(i, q).start()
        c_copy(i, q, n, False).start()
        if at > 0:
            before, slot = order[at - 1]
            x_copy(gates[before], slot, False).wait_recv()
            c_copy(gates[before], slot, before, True).start()
        if n == 0 and q == SLICES - 1:
            for m in (0, 2, 1):
                group_wait(2, m)
                corner_copy(m).start()
        if n == 1 and q < 2:
            turn(2 * (c + 2 * p) + q)
        if n == 1 and q == 3:
            for m in (0, 1):
                group_wait(1, m)
                corner_copy(m, False).wait_recv()
            embed_inputs()
        if n == 1 and q in (4, 5):
            first_step(2 * p + q - 4)
        if n == 1 and q == 2:
            for other in (False, True):
                for slot in range(SLICES):
                    c_copy(p, slot, 0, other, False).wait_recv()
            for xs in (0, 1):
                turn(2 * (1 - c + 2 * p) + xs)
    x_copy(1 - p, SLICES - 1, False).wait_recv()
    c_copy(1 - p, SLICES - 1, 1, True).start()
    for xs in (0, 1):
        turn(2 * (c + 2 * (1 - p)) + xs)
    for other in (False, True):
        for q in range(SLICES):
            c_copy(1 - p, q, 1, other, False).wait_recv()
    for xs in (0, 1):
        turn(2 * (1 - c + 2 * (1 - p)) + xs)
    for a in (0, 1):
        first_step(2 * (1 - p) + a)
    w2_out = pltpu.make_async_copy(w2, w2_o, out_sem.at[6])
    w2_out.start()
    group_wait(1, 2)
    corner_copy(2, False).wait_recv()
    for n in (3, 4):
        for d in (1, 2, 3):
            group_wait(d, n)
        call[0, n - 3] = cells[n - 3].astype(F32)

    def far_copy(sender=True):
        first = 4 * p if sender else 4 * (1 - p)
        part = wo.at[pl.ds(first, 4), shard]
        return remote(part, part, o_send.at[0], o_recv.at[0], far)

    def over_copy(sender=True):
        part = wo.at[:, 2 * x + c if sender else 2 * (1 - x) + c]
        return remote(part, part, o_send.at[1], o_recv.at[1], across)

    def twin_copy(xs, sender=True):
        part = wo.at[:, 2 * xs + (c if sender else 1 - c)]
        return remote(part, part, o_send.at[2 + xs], o_recv.at[2 + xs], twin)

    def h_copy(t, part, xb, d, sender=True):
        there = peers[d]
        rows = pl.ds(part * PART, PART)
        at = mine[xb] if sender else stripe(there["y"], there["zi"], xb)
        block = hx.at[t + 1, rows, cols(at)]
        return remote(block, block, h_send.at[t, part, xb, d - 1], h_recv.at[t, part, xb, d - 1], there["dev"])

    def forward(t, part):
        rows = pl.ds(part * PART, PART)
        for xb in (0, 1):

            def pre(g):
                if t == 0:
                    return act[0, 2 * g + xb, rows]
                return dot(hx[t, rows, :], wt[2 * g + xb])

            gate_i = jax.nn.sigmoid(pre(0))
            act[t, xb, rows] = gate_i
            gate_f = jax.nn.sigmoid(pre(1))
            act[t, 2 + xb, rows] = gate_f
            gate_g = jnp.tanh(pre(2))
            act[t, 4 + xb, rows] = gate_g
            gate_o = jax.nn.sigmoid(pre(3))
            act[t, 6 + xb, rows] = gate_o
            cell = gate_f * call[t, xb, rows] + gate_i * gate_g
            call[t + 1, xb, rows] = cell
            hx[t + 1, rows, cols(mine[xb])] = (gate_o * jnp.tanh(cell)).astype(BF16)
            for d in (3, 1, 2):
                h_copy(t, part, xb, d).start()

    def h_wait(t, part):
        for xb in (0, 1):
            for d in (1, 2, 3):
                h_copy(t, part, xb, d, False).wait_recv()

    part_lanes = lax.broadcasted_iota(jnp.int32, (PART, CHARS), 1)
    part_rows = lax.broadcasted_iota(jnp.int32, (PART, 1), 0)
    totals = dict(loss=jnp.zeros((1, 1), F32), bias=jnp.zeros((1, CHARS), F32))

    def decode(t, part):
        rows = pl.ds(part * PART, PART)
        logits = dot(hx[t + 1, rows, pl.ds(0, HID)], wo[...].reshape(HID, CHARS)) + dbias[0:1, :]
        top = jnp.max(logits, axis=1, keepdims=True)
        grown = jnp.exp(logits - top)
        total = jnp.sum(grown, axis=1, keepdims=True)
        hit = metas[rows, STEPS + t : STEPS + t + 1] == part_lanes
        picked = jnp.sum(jnp.where(hit, logits, 0.0), axis=1, keepdims=True)
        low = ((grown / total - jnp.where(hit, 1.0, 0.0)) / STEPS).astype(BF16)
        dlog[t, rows] = low
        at = part_rows + part * PART
        ours = (at >= k * 64) & (at < k * 64 + 64)
        term = jnp.where(ours, (top + jnp.log(total) - picked) / STEPS, 0.0)
        totals["loss"] = totals["loss"] + jnp.sum(term, axis=0, keepdims=True)
        totals["bias"] = totals["bias"] + jnp.sum(jnp.where(ours, low.astype(F32), 0.0), axis=0, keepdims=True)

    far_copy().start()
    for part in range(SPLIT):
        forward(0, part)
    far_copy(False).wait_recv()
    over_copy().start()
    for part in range(SPLIT):
        h_wait(0, part)
        forward(1, part)
    over_copy(False).wait_recv()
    for xs in (0, 1):
        twin_copy(xs).start()
    for part in range(SPLIT):
        h_wait(1, part)
        forward(2, part)
    for xs in (0, 1):
        twin_copy(xs, False).wait_recv()
    for part in range(SPLIT):
        decode(0, part)
    for part in range(SPLIT):
        h_wait(2, part)
        forward(3, part)
    for part in range(SPLIT):
        decode(1, part)
    hx_out = pltpu.make_async_copy(hx.at[pl.ds(0, STEPS)], hx_o, out_sem.at[0])
    hx_out.start()
    for part in range(SPLIT):
        decode(2, part)

    emb[...] = jnp.zeros_like(emb)
    dcn[...] = jnp.zeros_like(dcn)

    def b_copy(t, part, d):
        rows = pl.ds(part * PART, PART)
        return remote(
            pbuf.at[t - 1, d - 1, rows],
            rbuf.at[t - 1, d - 1, rows],
            b_send.at[t - 1, part, d - 1],
            b_recv.at[t - 1, part, d - 1],
            peers[d]["dev"],
        )

    def backward(t, part):
        rows = pl.ds(part * PART, PART)
        if t < STEPS - 1:
            for d in (1, 2, 3):
                b_copy(t + 1, part, d).wait_recv()
        for xb in (0, 1):
            dh = dot_nt(dlog[t, rows], wo[mine[xb]].reshape(ROWS, CHARS))
            wide = pl.ds(xb * ROWS, ROWS)
            if t < STEPS - 1:
                dh = dh + ownp[rows, wide]
                for d in (1, 2, 3):
                    dh = dh + rbuf[t, d - 1, rows, wide].astype(F32)
            gate_i = act[t, xb, rows]
            gate_f = act[t, 2 + xb, rows]
            gate_g = act[t, 4 + xb, rows]
            gate_o = act[t, 6 + xb, rows]
            shown = jnp.tanh(call[t + 1, xb, rows])
            dc = dcn[xb, rows] + dh * gate_o * (1.0 - shown * shown)
            dcn[xb, rows] = dc * gate_f
            dg[t, rows, pl.ds(xb * ROWS, ROWS)] = (dc * gate_g * gate_i * (1.0 - gate_i)).astype(BF16)
            dg[t, rows, pl.ds((2 + xb) * ROWS, ROWS)] = (
                dc * call[t, xb, rows] * gate_f * (1.0 - gate_f)
            ).astype(BF16)
            dg[t, rows, pl.ds((4 + xb) * ROWS, ROWS)] = (dc * gate_i * (1.0 - gate_g * gate_g)).astype(BF16)
            dg[t, rows, pl.ds((6 + xb) * ROWS, ROWS)] = (dh * shown * gate_o * (1.0 - gate_o)).astype(BF16)
        if t > 0:
            for d in (3, 1, 2):
                there = peers[d]
                for xb in (0, 1):
                    pbuf[t - 1, d - 1, rows, pl.ds(xb * ROWS, ROWS)] = dot(
                        dg[t, rows, :], w2[:, cols(stripe(there["y"], there["zi"], xb))]
                    ).astype(BF16)
                b_copy(t, part, d).start()
            for xb in (0, 1):
                ownp[rows, pl.ds(xb * ROWS, ROWS)] = dot(dg[t, rows, :], w2[:, cols(mine[xb])])
        dgt[t, :, pl.ds(part * PART, PART)] = dg[t, rows, :].T

    def extras(t):
        dx = dot(dg[t], w2[:, pl.ds(HID, WIDE - HID)])
        high = dx.astype(BF16)
        rest = (dx - high.astype(F32)).astype(BF16)
        one = jnp.where(metas[:, t : t + 1] == lanes, 1.0, 0.0).astype(BF16)
        emb[...] += dot_tn(one, high) + dot_tn(one, rest)

    def d_copy(n):
        return remote(d_out.at[n], d_in.at[n], d_send.at[n], d_recv.at[n], quad_to(*quad[n]))

    def f_copy(xb):
        return remote(f_out.at[xb], f_in.at[p], f_send.at[xb], f_recv.at[p], (final_to(xb), shard))

    def f_wait(n):
        remote(f_out.at[n], f_in.at[n], f_send.at[n], f_recv.at[n], across).wait_recv()

    def decoder_start():
        for xb in (0, 1):
            total = dot_tn(hx[1, :, cols(mine[xb])], dlog[0])
            for t in range(1, STEPS):
                total = total + dot_tn(hx[t + 1, :, cols(mine[xb])], dlog[t])
            dpart[xb] = total
        for n, (dx, dc) in enumerate(quad):
            theirs = 2 * flip(x, dx) + flip(c, dc)
            for xb in (0, 1):
                d_out[n, xb] = dpart[xb, aligned(theirs * 64, 64), :].astype(BF16)
            d_copy(n).start()

    def decoder_middle():
        for n in range(3):
            d_copy(n).wait_recv()
        for xb in (0, 1):
            part = dpart[xb, aligned(shard * 64, 64), :]
            for n in range(3):
                part = part + d_in[n, xb].astype(F32)
            f_out[xb] = part.astype(BF16)

            @pl.when(final_to(xb) != dp)
            def _():
                f_copy(xb).start()

            @pl.when(final_to(xb) == dp)
            def _():
                f_in[p] = f_out[xb]

    def decoder_end():
        for n in (0, 1):

            @pl.when(final_from(n) != dp)
            def _():
                f_wait(n)

        gdec_o[...] = f_in[0].astype(F32) + f_in[1].astype(F32)

    for part in range(SPLIT):
        h_wait(STEPS - 1, part)
        decode(STEPS - 1, part)
        backward(STEPS - 1, part)
    decoder_start()
    extras(STEPS - 1)
    dg_out = [pltpu.make_async_copy(dgt.at[t], dgt_o.at[t], out_sem.at[1 + t]) for t in range(STEPS)]
    dg_last = pltpu.make_async_copy(dg.at[0], dg_o, out_sem.at[5])
    dg_out[STEPS - 1].start()
    for t in reversed(range(STEPS - 1)):
        for part in range(SPLIT):
            backward(t, part)
        dg_out[t].start()
        if t == 0:
            dg_last.start()
        if t == STEPS - 2:
            decoder_middle()
        extras(t)
    decoder_end()

    for xb in (0, 1):
        dc0_o[:, pl.ds(xb * ROWS, ROWS)] = dcn[xb]
    at_row = lax.broadcasted_iota(jnp.int32, (288, 128), 0)
    at_col = lax.broadcasted_iota(jnp.int32, (288, 128), 1)
    block = jnp.where((at_row < 275) & (at_col < INPUTS), emb[pl.ds(0, 288), :], 0.0)
    for n in range(3):
        block = jnp.where(at_row == 276 + n, totals["bias"][:, n * 128 : n * 128 + 128], block)
    block = jnp.where((at_row == 279) & (at_col == 0), totals["loss"], block)
    emb_o[...] = block

    for q in range(SLICES):
        for target in (0, 1):

            @pl.when(c + 2 * target != z)
            def _():
                z_copy(target, q).wait_send()

        for n in (0, 1):
            x_copy(gates[n], q).wait_send()
            c_copy(gates[n], q, n, False).wait_send()
            c_copy(gates[n], q, n, True).wait_send()
    for n in range(5):
        for d in (1, 2):
            group_copy(d, n).wait_send()
        if n < 3:
            corner_copy(n).wait_send()
        else:
            group_copy(3, n).wait_send()
    for n in range(3):
        d_copy(n).wait_send()
    for xb in (0, 1):

        @pl.when(final_to(xb) != dp)
        def _():
            f_copy(xb).wait_send()

    far_copy().wait_send()
    over_copy().wait_send()
    for xs in (0, 1):
        twin_copy(xs).wait_send()
    for t in range(STEPS):
        for part in range(SPLIT):
            for d in (1, 2, 3):
                for xb in (0, 1):
                    h_copy(t, part, xb, d).wait_send()
                if t > 0:
                    b_copy(t, part, d).wait_send()
    hx_out.wait()
    w2_out.wait()
    dg_last.wait()
    for t in range(STEPS):
        dg_out[t].wait()


def sum_kernel(
    dgt_in,
    hx_in,
    dg_in,
    w2_in,
    dc0,
    emb,
    gdec_own,
    grad_o,
    emb_o,
    norm_o,
    gh_o,
    gc_o,
    dgt,
    hx,
    dg,
    w2,
    dh0,
    c_out,
    c_in,
    kept,
    x_out,
    x_in,
    z_out,
    z_in,
    gh_out,
    gh_in,
    gc_out,
    gc_in,
    e_in,
    n_out,
    n_in,
    c_send,
    c_recv,
    x_send,
    x_recv,
    z_send,
    z_recv,
    g_send,
    g_recv,
    e_send,
    e_recv,
    n_send,
    n_recv,
    in_sem,
):
    s = spots()
    z, y, x, c, k, zi, p = s["z"], s["y"], s["x"], s["c"], s["k"], s["zi"], s["p"]
    dp, shard = s["dp"], s["shard"]
    across = device(s, x=1 - x)
    twin = device(s, c=1 - c)
    far = device(s, z=2 * (1 - p) + zi)
    peers = {d: peer(s, d) for d in (1, 2, 3)}
    core = z % 2
    column = [(dz, dc) for dz in range(4) for dc in range(2) if (dz, dc) != (0, 0)]
    plane = [(dy, dx) for dy in range(2) for dx in range(2) if (dy, dx) != (0, 0)]

    def flip(value, by):
        return 1 - value if by else value

    def column_to(dz, dc):
        return device(s, z=(z + dz) % 4, c=flip(c, dc))

    def column_from(dz, dc):
        return device(s, z=(z + 4 - dz) % 4, c=flip(c, dc))

    def plane_to(dy, dx):
        return device(s, y=flip(y, dy), x=flip(x, dx))

    loads = [
        pltpu.make_async_copy(source, target, in_sem.at[n])
        for n, (source, target) in enumerate(((hx_in, hx), (dgt_in, dgt), (dg_in, dg), (w2_in, w2)))
    ]
    for load in loads:
        load.start()
    for dz, dc in column:
        signal(column_from(dz, dc))
    for dy, dx in plane:
        signal(plane_to(dy, dx))
    signal(peers[3]["dev"])
    pl.semaphore_wait(pltpu.get_barrier_semaphore(), 11)

    def state_copies(d, sender=True):
        there = peers[d]
        rows = aligned(there["k"] * 64, 64)
        result = [
            remote(gh_out.at[d - 1], gh_in.at[d - 1], g_send.at[d - 1, 0], g_recv.at[d - 1, 0], there["dev"]),
            remote(gc_out.at[d - 1], gc_in.at[d - 1], g_send.at[d - 1, 1], g_recv.at[d - 1, 1], there["dev"]),
        ]
        return result

    def early():
        for d in (3, 1, 2):
            rows = aligned(peers[d]["k"] * 64, 64)
            gh_out[d - 1] = dh0[rows, :].astype(BF16)
            gc_out[d - 1] = dc0[rows, :].astype(BF16)
            for copy in state_copies(d):
                copy.start()

    tiles = ((0, 512), (512, 512), (1024, 512), (1536, 640))

    def block_of(b, store):
        for start, size in tiles:
            at = pl.ds(start, size)
            total = dot(dgt[0, cols(b), :], hx[0, :, at])
            for t in range(1, STEPS):
                total = total + dot(dgt[t, cols(b), :], hx[t, :, at])
            store(at, total)

    def c_copy(n, q):
        rows = pl.ds(q * SLICE, SLICE)
        return remote(c_out.at[n, rows], c_in.at[n, rows], c_send.at[n, q], c_recv.at[n, q], twin)

    def x_copy(i, q):
        rows = pl.ds(q * SLICE, SLICE)
        return remote(x_out.at[i, rows], x_in.at[i, rows], x_send.at[i, q], x_recv.at[i, q], across)

    def z_copy(i, q):
        rows = pl.ds(q * SLICE, SLICE)
        return remote(
            z_out.at[i, rows],
            z_in.at[p, rows],
            z_send.at[i, q],
            z_recv.at[p, q],
            device(s, z=c + 2 * gates[i], c=core),
        )

    def z_wait(n, q):
        rows = pl.ds(q * SLICE, SLICE)
        remote(z_out.at[n, rows], z_in.at[n, rows], z_send.at[n, q], z_recv.at[n, q], across).wait_recv()

    def for_twin(n, b):
        def store(at, value):
            c_out[n, :, at] = value.astype(BF16)

        block_of(b, store)
        for q in range(SLICES):
            c_copy(n, q).start()

    def keep(i, b):
        def store(at, value):
            kept[i, :, at] = value

        block_of(b, store)

    def add_twin(i, n, q):
        rows = pl.ds(q * SLICE, SLICE)
        c_copy(n, q).wait_recv()
        return kept[i, rows] + c_in[n, rows].astype(F32)

    half = aligned(c * 144, 144)
    rest = aligned((1 - c) * 144, 144)
    hops = (twin, across, far, peers[2]["dev"], peers[1]["dev"], twin)

    def e_copy(n):
        if n == 0:
            return remote(emb_o.at[rest], e_in.at[0], e_send.at[0], e_recv.at[0], hops[0])
        if n == 5:
            return remote(emb_o.at[half], e_in.at[5], e_send.at[5], e_recv.at[5], hops[5])
        return remote(e_out_of(n), e_in.at[n], e_send.at[n], e_recv.at[n], hops[n])

    def e_out_of(n):
        return e_in.at[5 + n]

    def e_start(n):
        if n in (1, 2, 3, 4):
            e_in[5 + n] = emb_o[half, :]
        e_copy(n).start()

    def e_finish(n):
        if n == 5:
            e_copy(5).wait()
            emb_o[rest, :] = e_in[5]
            return
        e_copy(n).wait()
        emb_o[half, :] = emb_o[half, :] + e_in[n]

    gates = (1 - p, p)

    def pass_on(n, q):
        i = gates[n]
        rows = pl.ds(q * SLICE, SLICE)
        x_copy(n, q).wait_recv()
        total = add_twin(n, 2 + n, q) + x_in[n, rows].astype(F32)
        z_out[n, rows] = total.astype(BF16)

        @pl.when(c + 2 * i != z)
        def _():
            z_copy(n, q).start()

        @pl.when(c + 2 * i == z)
        def _():
            z_in[p, rows] = z_out[n, rows]

    def to_across(n):
        for q in range(SLICES):
            x_out[n, pl.ds(q * SLICE, SLICE)] = add_twin(2, n, q).astype(BF16)
            x_copy(n, q).start()

    emb_o[...] = emb[...]
    e_start(0)
    loads[0].wait()
    loads[1].wait()
    for_twin(0, 2 * (1 - c + 2 * gates[0]) + 1 - x)
    e_finish(0)
    e_start(1)
    keep(2, 2 * (c + 2 * gates[0]) + 1 - x)
    to_across(0)
    for_twin(2, 2 * (1 - c + 2 * gates[0]) + x)
    keep(0, 2 * (c + 2 * gates[0]) + x)
    pass_on(0, 0)
    e_finish(1)
    e_start(2)
    for_twin(1, 2 * (1 - c + 2 * gates[1]) + 1 - x)
    keep(2, 2 * (c + 2 * gates[1]) + 1 - x)
    pass_on(0, 1)
    to_across(1)
    loads[2].wait()
    loads[3].wait()
    for q in range(2, SLICES):
        pass_on(0, q)
        if q == 2:
            for n in range(HID // 512):
                dh0[:, pl.ds(n * 512, 512)] = dot(dg[...], w2[:, pl.ds(n * 512, 512)])
            early()
        if q == 3:
            e_finish(2)
            e_start(3)
            for_twin(3, 2 * (1 - c + 2 * gates[1]) + x)
        if q == 4:
            keep(1, 2 * (c + 2 * gates[1]) + x)
        if q == 6:
            e_finish(3)
            e_start(4)
    for q in range(SLICES):
        pass_on(1, q)
        if q == 1:
            e_finish(4)
            e_start(5)
    e_finish(5)

    squares = jnp.zeros((1, 1), F32)

    def square_sum(value):
        return jnp.sum(jnp.sum(value * value, axis=1, keepdims=True), axis=0, keepdims=True)

    squares = squares + square_sum(gdec_own[...])
    for q in range(SLICES):
        rows = pl.ds(q * SLICE, SLICE)
        for n in (0, 1):

            @pl.when(jnp.logical_or(core != c, p != n))
            def _():
                z_wait(n, q)

        final = z_in[0, rows].astype(F32) + z_in[1, rows].astype(F32)
        grad_o[rows, :] = final
        squares = squares + square_sum(final)

    def n_copy(n):
        if n < 7:
            return remote(n_out.at[0], n_in.at[n], n_send.at[n], n_recv.at[n], column_to(*column[n]))
        return remote(n_out.at[1], n_in.at[n], n_send.at[n], n_recv.at[n], plane_to(*plane[n - 7]))

    n_out[0] = jnp.broadcast_to(squares, (8, 128))
    for n in range(7):
        n_copy(n).start()
    own = aligned(k * 64, 64)
    total = dh0[own, :]
    for d in (1, 2, 3):
        for copy in state_copies(d):
            copy.wait_recv()
        total = total + gh_in[d - 1].astype(F32)
    gh_o[...] = total
    for xb in (0, 1):
        gc_o[:, cols(stripe(y, zi, xb))] = dc0[own, pl.ds(xb * ROWS, ROWS)]
        for d in (1, 2, 3):
            there = peers[d]
            gc_o[:, cols(stripe(there["y"], there["zi"], xb))] = gc_in[d - 1, :, pl.ds(xb * ROWS, ROWS)].astype(F32)
    total = n_out[0]
    for n in range(7):
        n_copy(n).wait_recv()
        total = total + n_in[n]
    n_out[1] = total
    for n in range(7, 10):
        n_copy(n).start()
    at_row = lax.broadcasted_iota(jnp.int32, (288, 128), 0)
    shared = square_sum(jnp.where(at_row == 279, 0.0, emb_o[...]))
    for n in range(7, 10):
        n_copy(n).wait_recv()
        total = total + n_in[n]
    norm_o[...] = total + shared

    for n in range(4):
        for q in range(SLICES):
            c_copy(n, q).wait_send()
    for i in (0, 1):
        for q in range(SLICES):
            x_copy(i, q).wait_send()

            @pl.when(c + 2 * gates[i] != z)
            def _():
                z_copy(i, q).wait_send()

    for d in (1, 2, 3):
        for copy in state_copies(d):
            copy.wait_send()
    for n in range(10):
        n_copy(n).wait_send()


def finish_kernel(
    streams_all,
    grad,
    emb,
    squares,
    gdec,
    gh,
    gc,
    m_embed,
    m_input,
    m_hidden,
    m_gate,
    m_decoder,
    m_outbias,
    loss_o,
    norm_o,
    gh_o,
    gc_o,
    g_embed,
    g_input,
    g_hidden,
    g_gate,
    g_decoder,
    g_outbias,
    n_embed,
    n_input,
    n_hidden,
    n_gate,
    n_decoder,
    n_outbias,
):
    norm = jnp.sqrt(squares[0:1, 0:1])
    norm_o[...] = norm
    factor = CLIP / jnp.maximum(norm, CLIP)
    loss_o[...] = emb[279:280, 0:1] / streams_all
    gh_o[...] = gh[...]
    gc_o[...] = gc[...]

    def out(value, momentum, grad_ref, new_ref):
        grad_ref[...] = value
        new_ref[...] = MOMENTUM * momentum[...] + factor * value

    vocab = m_outbias.shape[1]
    out(emb[pl.ds(0, vocab), pl.ds(0, INPUTS)], m_embed, g_embed, n_embed)
    turned = grad[:, pl.ds(HID, WIDE - HID)].T
    out(turned[0:INPUTS, :], m_input, g_input, n_input)
    out(turned[INPUTS : INPUTS + 1, :], m_gate, g_gate, n_gate)
    out(grad[:, pl.ds(0, HID)], m_hidden, g_hidden, n_hidden)
    out(gdec[:, pl.ds(0, vocab)], m_decoder, g_decoder, n_decoder)
    row = jnp.concatenate([emb[276 + n : 277 + n, :] for n in range(3)], axis=1)
    out(row[:, 0:vocab], m_outbias, g_outbias, n_outbias)


def split_local(
    char_ids,
    targets,
    hidden_start,
    cell_start,
    embedding,
    input_weight,
    hidden_weight,
    gate_bias,
    decoder_weight,
    decoder_bias,
    momentum_embed,
    momentum_input,
    momentum_hidden,
    momentum_gate,
    momentum_decoder,
    momentum_outbias,
):
    streams = char_ids.shape[0]
    vocab = embedding.shape[0]
    shape = jax.ShapeDtypeStruct
    vm = pl.BlockSpec(memory_space=pltpu.VMEM)
    hbm = pl.BlockSpec(memory_space=pl.ANY)
    dma = pltpu.SemaphoreType.DMA
    hx, dgt, dg, w2, dc0, emb, gdec_own = pl.pallas_call(
        step_kernel,
        out_shape=(
            shape((STEPS, ROWS, WIDE), BF16),
            shape((STEPS, HID, ROWS), BF16),
            shape((ROWS, HID), BF16),
            shape((HID, WIDE), BF16),
            shape((ROWS, 512), F32),
            shape((288, 128), F32),
            shape((64, CHARS), F32),
        ),
        in_specs=[vm] * 10,
        out_specs=(hbm,) * 4 + (vm,) * 3,
        scratch_shapes=[
            pltpu.VMEM((HID, WIDE), BF16),
            pltpu.VMEM((8, WIDE, ROWS), BF16),
            pltpu.VMEM((STEPS + 1, ROWS, WIDE), BF16),
            pltpu.VMEM((STEPS, 8, ROWS, ROWS), F32),
            pltpu.VMEM((STEPS + 1, 2, ROWS, ROWS), F32),
            pltpu.VMEM((STEPS, ROWS, HID), BF16),
            pltpu.VMEM((STEPS, HID, ROWS), BF16),
            pltpu.VMEM((STEPS - 1, 3, ROWS, 512), BF16),
            pltpu.VMEM((STEPS - 1, 3, ROWS, 512), BF16),
            pltpu.VMEM((ROWS, 512), F32),
            pltpu.VMEM((2, ROWS, ROWS), F32),
            pltpu.VMEM((8, 4, 64, CHARS), BF16),
            pltpu.VMEM((STEPS, ROWS, CHARS), BF16),
            pltpu.VMEM((ROWS, 128), jnp.int32),
            pltpu.VMEM((CHARS, 128), F32),
            pltpu.VMEM((2, ROWS, ROWS), BF16),
            pltpu.VMEM((2, ROWS, CHARS), F32),
            pltpu.VMEM((3, 2, 64, CHARS), BF16),
            pltpu.VMEM((3, 2, 64, CHARS), BF16),
            pltpu.VMEM((2, 64, CHARS), BF16),
            pltpu.VMEM((2, 64, CHARS), BF16),
            pltpu.VMEM((ROWS, WIDE), BF16),
            pltpu.VMEM((64, HID), BF16),
            pltpu.VMEM((64, HID), BF16),
            pltpu.VMEM((64, 128), jnp.int32),
            pltpu.VMEM((64, CHARS), BF16),
            pltpu.VMEM((CHARS, 128), F32),
            pltpu.VMEM((8, CHARS), F32),
            pltpu.VMEM((128, ROWS), F32),
            pltpu.VMEM((128, 128), jnp.int32),
            dma((3, 5)),
            dma((3, 5)),
            dma((2, SLICES)),
            dma((2, SLICES)),
            dma((2, SLICES)),
            dma((2, SLICES)),
            dma((2, 2, SLICES)),
            dma((2, 2, SLICES)),
            dma((4,)),
            dma((4,)),
            dma((STEPS, SPLIT, 2, 3)),
            dma((STEPS, SPLIT, 2, 3)),
            dma((STEPS - 1, SPLIT, 3)),
            dma((STEPS - 1, SPLIT, 3)),
            dma((3,)),
            dma((3,)),
            dma((2,)),
            dma((2,)),
            dma((3 + STEPS,)),
        ],
        compiler_params=pltpu.CompilerParams(
            collective_id=0, has_side_effects=True, vmem_limit_bytes=60 * 2**20
        ),
    )(
        char_ids.T,
        targets.T,
        hidden_start,
        cell_start,
        embedding,
        input_weight.T,
        hidden_weight,
        gate_bias[None, :],
        decoder_weight,
        decoder_bias[None, :],
    )
    grad, emb, norm, grad_hidden_start, grad_cell_start = pl.pallas_call(
        sum_kernel,
        out_shape=(
            shape((ROWS, WIDE), F32),
            shape((288, 128), F32),
            shape((8, 128), F32),
            shape((64, HID), F32),
            shape((64, HID), F32),
        ),
        in_specs=[hbm] * 4 + [vm] * 3,
        out_specs=(vm,) * 5,
        scratch_shapes=[
            pltpu.VMEM((STEPS, HID, ROWS), BF16),
            pltpu.VMEM((STEPS, ROWS, WIDE), BF16),
            pltpu.VMEM((ROWS, HID), BF16),
            pltpu.VMEM((HID, WIDE), BF16),
            pltpu.VMEM((ROWS, HID), F32),
            pltpu.VMEM((4, ROWS, WIDE), BF16),
            pltpu.VMEM((4, ROWS, WIDE), BF16),
            pltpu.VMEM((3, ROWS, WIDE), F32),
            pltpu.VMEM((2, ROWS, WIDE), BF16),
            pltpu.VMEM((2, ROWS, WIDE), BF16),
            pltpu.VMEM((2, ROWS, WIDE), BF16),
            pltpu.VMEM((2, ROWS, WIDE), BF16),
            pltpu.VMEM((3, 64, HID), BF16),
            pltpu.VMEM((3, 64, HID), BF16),
            pltpu.VMEM((3, 64, 512), BF16),
            pltpu.VMEM((3, 64, 512), BF16),
            pltpu.VMEM((10, 144, 128), F32),
            pltpu.VMEM((2, 8, 128), F32),
            pltpu.VMEM((10, 8, 128), F32),
            dma((4, SLICES)),
            dma((4, SLICES)),
            dma((2, SLICES)),
            dma((2, SLICES)),
            dma((2, SLICES)),
            dma((2, SLICES)),
            dma((3, 2)),
            dma((3, 2)),
            dma((6,)),
            dma((6,)),
            dma((10,)),
            dma((10,)),
            dma((4,)),
        ],
        compiler_params=pltpu.CompilerParams(
            collective_id=1, has_side_effects=True, vmem_limit_bytes=60 * 2**20
        ),
    )(dgt, hx, dg, w2, dc0, emb, gdec_own)
    streams_all = streams * lax.axis_size("dp") * lax.axis_size("shard")
    whole = lambda a: pl.BlockSpec(a, lambda n: (0, 0))
    rows = lambda r, w: pl.BlockSpec((r, w), lambda n: (n, 0))
    lanes = lambda r: pl.BlockSpec((r, ROWS // 2), lambda n: (0, n))
    weights = [
        (whole((vocab, INPUTS)), (vocab, INPUTS)),
        (lanes(INPUTS), (INPUTS, ROWS)),
        (rows(ROWS // 2, HID), (ROWS, HID)),
        (lanes(1), (1, ROWS)),
        (whole((64, vocab)), (64, vocab)),
        (whole((1, vocab)), (1, vocab)),
    ]
    state = (rows(32, HID), (64, HID))
    scalar = (whole((1, 1)), (1, 1))
    results = [scalar, scalar, state, state] + weights + weights
    loss, norm, gh, gc, *rest = pl.pallas_call(
        functools.partial(finish_kernel, float(streams_all)),
        grid=(2,),
        out_shape=[shape(dims, F32) for _, dims in results],
        in_specs=[
            rows(ROWS // 2, WIDE),
            whole((288, 128)),
            whole((8, 128)),
            whole((64, CHARS)),
            state[0],
            state[0],
        ]
        + [spec for spec, _ in weights],
        out_specs=[spec for spec, _ in results],
        compiler_params=pltpu.CompilerParams(vmem_limit_bytes=60 * 2**20),
    )(
        grad,
        emb,
        norm,
        gdec_own,
        grad_hidden_start,
        grad_cell_start,
        momentum_embed,
        momentum_input.T,
        momentum_hidden,
        momentum_gate[None, :],
        momentum_decoder,
        momentum_outbias[None, :],
    )
    for n in (0, 6):
        rest[n + 1] = rest[n + 1].T
        rest[n + 3] = rest[n + 3].reshape(-1)
        rest[n + 5] = rest[n + 5].reshape(-1)
    return (loss.reshape(1), norm.reshape(1), gh, gc, *rest)


def solution(mesh):
    fits = mesh.shape["dp"] == 8 and mesh.shape["shard"] == 4
    placed = (
        P(("dp", "shard"), None),
        P(("dp", "shard"), None),
        P(("dp", "shard"), None),
        P(("dp", "shard"), None),
        P(),
        P(("dp", "shard"), None),
        P(("dp", "shard"), None),
        P(("dp", "shard")),
        P(("dp", "shard"), None),
        P(),
        P(),
        P(("dp", "shard"), None),
        P(("dp", "shard"), None),
        P(("dp", "shard")),
        P(("dp", "shard"), None),
        P(),
    )
    return jax.shard_map(
        split_local if fits else local,
        mesh=mesh,
        in_specs=placed,
        out_specs=(
            P(),
            P(),
            P(("dp", "shard"), None),
            P(("dp", "shard"), None),
            P(),
            P(("dp", "shard"), None),
            P(("dp", "shard"), None),
            P(("dp", "shard")),
            P(("dp", "shard"), None),
            P(),
            P(),
            P(("dp", "shard"), None),
            P(("dp", "shard"), None),
            P(("dp", "shard")),
            P(("dp", "shard"), None),
            P(),
        ),
        check_vma=False,
    )
```

```python
import functools

import jax
import jax.numpy as jnp
from jax import lax
from jax.experimental import pallas as pl
from jax.experimental.pallas import tpu as pltpu
from jax.sharding import PartitionSpec as P

MESH = pl.DeviceIdType.MESH
F32 = jnp.float32
BF16 = jnp.bfloat16

MICRO = 2


CLIP = 0.25
MOMENTUM = 0.5


def contract_rows(left, right):
    return lax.dot_general(
        left, right, (((0,), (0,)), ((), ())), preferred_element_type=jnp.float32
    )


def contract_last(left, right):
    return lax.dot_general(
        left, right, (((1,), (1,)), ((), ())), preferred_element_type=jnp.float32
    )


def local(
    char_ids,
    targets,
    hidden_start,
    cell_start,
    embedding,
    input_weight,
    hidden_weight,
    gate_bias,
    decoder_weight,
    decoder_bias,
    momentum_embed,
    momentum_input,
    momentum_hidden,
    momentum_gate,
    momentum_decoder,
    momentum_outbias,
):
    streams, seq_len = char_ids.shape
    micro_rows = streams // MICRO
    vocab_size = embedding.shape[0]
    hidden_size = hidden_start.shape[1]
    low_input = input_weight.astype(jnp.bfloat16)
    low_hidden = hidden_weight.astype(jnp.bfloat16)
    low_bias = gate_bias.astype(jnp.bfloat16)
    low_decoder = decoder_weight.astype(jnp.bfloat16)
    inner_rows = (
        lax.all_gather(low_input, "shard", axis=0, tiled=True),
        lax.all_gather(low_hidden, "shard", axis=0, tiled=True),
        lax.all_gather(low_bias, "shard", axis=0, tiled=True),
        lax.all_gather(low_decoder, "shard", axis=0, tiled=True),
    )
    weight_in, weight_rec, bias_low, weight_out = (
        lax.all_gather(inner_rows[0], "dp", axis=0, tiled=True),
        lax.all_gather(inner_rows[1], "dp", axis=0, tiled=True),
        lax.all_gather(inner_rows[2], "dp", axis=0, tiled=True),
        lax.all_gather(inner_rows[3], "dp", axis=0, tiled=True),
    )
    columns = jnp.arange(vocab_size, dtype=jnp.int32)
    table = embedding.astype(jnp.bfloat16)
    bias_row = bias_low.astype(jnp.float32)[None, :]

    def forward_step(carried, input_now):
        hidden_low, cell = carried
        preact = input_now + contract_last(hidden_low, weight_rec)
        input_gate = jax.nn.sigmoid(preact[:, :hidden_size])
        forget_gate = jax.nn.sigmoid(preact[:, hidden_size : 2 * hidden_size])
        candidate = jnp.tanh(preact[:, 2 * hidden_size : 3 * hidden_size])
        output_gate = jax.nn.sigmoid(preact[:, 3 * hidden_size :])
        cell_next = forget_gate * cell + input_gate * candidate
        hidden_next = (output_gate * jnp.tanh(cell_next)).astype(jnp.bfloat16)
        activations = jnp.concatenate([input_gate, forget_gate, candidate, output_gate], axis=1)
        return ((hidden_next, cell_next), (hidden_low, cell, activations, cell_next, hidden_next))

    def backward_step(carried, inputs):
        hidden_grad_next, cell_grad_next = carried
        out_grad, cell_before, gate_values, cell_now = inputs
        hidden_grad = out_grad + hidden_grad_next
        input_gate = gate_values[:, :hidden_size]
        forget_gate = gate_values[:, hidden_size : 2 * hidden_size]
        candidate = gate_values[:, 2 * hidden_size : 3 * hidden_size]
        output_gate = gate_values[:, 3 * hidden_size :]
        cell_tanh = jnp.tanh(cell_now)
        cell_grad = cell_grad_next + hidden_grad * output_gate * (1.0 - cell_tanh * cell_tanh)
        input_term = cell_grad * candidate * input_gate * (1.0 - input_gate)
        forget_term = cell_grad * cell_before * forget_gate * (1.0 - forget_gate)
        candidate_term = cell_grad * input_gate * (1.0 - candidate * candidate)
        output_term = hidden_grad * cell_tanh * output_gate * (1.0 - output_gate)
        gate_grad = jnp.concatenate(
            [input_term, forget_term, candidate_term, output_term], axis=1
        ).astype(jnp.bfloat16)
        hidden_grad_prev = jnp.dot(gate_grad, weight_rec, preferred_element_type=jnp.float32)
        return ((hidden_grad_prev, cell_grad * forget_gate), gate_grad)

    def micro_pass(loss_total, inputs):
        ids_part, target_part, hidden_part, cell_part = inputs
        batch_rows = ids_part.shape[0]
        token_ids = ids_part.T.reshape(-1)
        token_targets = target_part.T.reshape(-1)
        one_input = (token_ids[:, None] == columns[None, :]).astype(jnp.bfloat16)
        one_target = (token_targets[:, None] == columns[None, :]).astype(jnp.float32)
        embedded = jnp.dot(one_input, table, preferred_element_type=jnp.float32).astype(
            jnp.bfloat16
        )
        input_part = contract_last(embedded, weight_in) + bias_row
        input_part = input_part.reshape(seq_len, batch_rows, 4 * hidden_size)
        start_pair = (hidden_part.astype(jnp.bfloat16), cell_part)
        final_pair, saved = lax.scan(forward_step, start_pair, input_part)
        hidden_prev, cell_prev, activations, cell_after, hidden_after = saved
        hidden_rows = hidden_after.reshape(seq_len * batch_rows, hidden_size)
        logits = (
            jnp.dot(hidden_rows, weight_out, preferred_element_type=jnp.float32)
            + decoder_bias[None, :]
        )
        log_total = jax.nn.logsumexp(logits, axis=1)
        local_loss = jnp.sum(log_total - jnp.sum(one_target * logits, axis=1)) / seq_len
        probs = jnp.exp(logits - log_total[:, None])
        logit_grad = ((probs - one_target) / seq_len).astype(jnp.bfloat16)
        hidden_from_out = contract_last(logit_grad, weight_out).reshape(
            seq_len, batch_rows, hidden_size
        )
        zero_state = jnp.zeros((batch_rows, hidden_size), jnp.float32)
        start_grads, gate_grads = lax.scan(
            backward_step,
            (zero_state, zero_state),
            (hidden_from_out, cell_prev, activations, cell_after),
            reverse=True,
        )
        gate_rows = gate_grads.reshape(seq_len * batch_rows, 4 * hidden_size)
        prev_rows = hidden_prev.reshape(seq_len * batch_rows, hidden_size)
        return (
            loss_total + local_loss,
            (
                token_ids,
                embedded,
                logit_grad,
                hidden_rows,
                gate_rows,
                prev_rows,
                start_grads[0],
                start_grads[1],
            ),
        )

    def by_micro(array):
        return array.reshape((MICRO, micro_rows) + array.shape[1:])

    local_loss, stacked = lax.scan(
        micro_pass,
        jnp.zeros((), jnp.float32),
        (by_micro(char_ids), by_micro(targets), by_micro(hidden_start), by_micro(cell_start)),
    )
    token_ids, embedded, logit_grad, hidden_rows, gate_rows, prev_rows, hidden_grads, cell_grads = (
        stacked
    )
    token_ids = token_ids.reshape(-1)
    embedded = embedded.reshape(-1, embedded.shape[-1])
    logit_grad = logit_grad.reshape(-1, vocab_size)
    hidden_rows = hidden_rows.reshape(-1, hidden_size)
    gate_rows = gate_rows.reshape(-1, 4 * hidden_size)
    prev_rows = prev_rows.reshape(-1, hidden_size)
    grad_hidden_start = hidden_grads.reshape(streams, hidden_size)
    grad_cell_start = cell_grads.reshape(streams, hidden_size)
    grad_outbias_local = jnp.sum(logit_grad.astype(jnp.float32), axis=0)
    grad_decoder_local = contract_rows(hidden_rows, logit_grad)
    grad_input_local = contract_rows(gate_rows, embedded)
    grad_hidden_local = contract_rows(gate_rows, prev_rows)
    grad_bias_local = jnp.sum(gate_rows.astype(jnp.float32), axis=0)
    embed_rows_grad = jnp.dot(gate_rows, weight_in, preferred_element_type=jnp.float32)
    one_all = (token_ids[:, None] == columns[None, :]).astype(jnp.float32)
    grad_embed_local = lax.dot_general(
        one_all,
        embed_rows_grad,
        (((0,), (0,)), ((), ())),
        precision=lax.Precision.HIGHEST,
        preferred_element_type=jnp.float32,
    )
    grad_embedding, grad_decoder_bias, loss_sum = lax.psum(
        (grad_embed_local, grad_outbias_local, local_loss), ("dp", "shard")
    )
    outer_sums = (
        lax.psum_scatter(
            grad_input_local.astype(jnp.bfloat16), "dp", scatter_dimension=0, tiled=True
        ).astype(jnp.float32),
        lax.psum_scatter(
            grad_hidden_local.astype(jnp.bfloat16), "dp", scatter_dimension=0, tiled=True
        ).astype(jnp.float32),
        lax.psum_scatter(
            grad_bias_local.astype(jnp.bfloat16), "dp", scatter_dimension=0, tiled=True
        ).astype(jnp.float32),
        lax.psum_scatter(
            grad_decoder_local.astype(jnp.bfloat16), "dp", scatter_dimension=0, tiled=True
        ).astype(jnp.float32),
    )
    grad_input_weight, grad_hidden_weight, grad_gate_bias, grad_decoder_weight = (
        lax.psum_scatter(
            outer_sums[0].astype(jnp.bfloat16), "shard", scatter_dimension=0, tiled=True
        ).astype(jnp.float32),
        lax.psum_scatter(
            outer_sums[1].astype(jnp.bfloat16), "shard", scatter_dimension=0, tiled=True
        ).astype(jnp.float32),
        lax.psum_scatter(
            outer_sums[2].astype(jnp.bfloat16), "shard", scatter_dimension=0, tiled=True
        ).astype(jnp.float32),
        lax.psum_scatter(
            outer_sums[3].astype(jnp.bfloat16), "shard", scatter_dimension=0, tiled=True
        ).astype(jnp.float32),
    )
    shard_squares = jnp.sum(grad_input_weight * grad_input_weight) + jnp.sum(
        grad_hidden_weight * grad_hidden_weight
    )
    shard_squares = (
        shard_squares
        + jnp.sum(grad_gate_bias * grad_gate_bias)
        + jnp.sum(grad_decoder_weight * grad_decoder_weight)
    )
    square_total = lax.psum(shard_squares, ("dp", "shard"))
    square_total = (
        square_total
        + jnp.sum(grad_embedding * grad_embedding)
        + jnp.sum(grad_decoder_bias * grad_decoder_bias)
    )
    grad_norm = jnp.sqrt(square_total)
    factor = CLIP / jnp.maximum(grad_norm, CLIP)
    streams_all = streams * lax.axis_size("dp") * lax.axis_size("shard")
    loss = loss_sum / streams_all
    momenta = (
        momentum_embed,
        momentum_input,
        momentum_hidden,
        momentum_gate,
        momentum_decoder,
        momentum_outbias,
    )
    weight_grads = (
        grad_embedding,
        grad_input_weight,
        grad_hidden_weight,
        grad_gate_bias,
        grad_decoder_weight,
        grad_decoder_bias,
    )
    new_momenta = [MOMENTUM * momenta[index] + factor * weight_grads[index] for index in range(6)]
    return (
        loss.reshape(1),
        grad_norm.reshape(1),
        grad_hidden_start,
        grad_cell_start,
        grad_embedding,
        grad_input_weight,
        grad_hidden_weight,
        grad_gate_bias,
        grad_decoder_weight,
        grad_decoder_bias,
        new_momenta[0],
        new_momenta[1],
        new_momenta[2],
        new_momenta[3],
        new_momenta[4],
        new_momenta[5],
    )


ROWS = 256
HID = 2048
WIDE = 2176
INPUTS = 100
CHARS = 384
SPLIT = 2
PART = ROWS // SPLIT
SLICES = 8
SLICE = ROWS // SLICES
PIECES = 4
PIECE = ROWS // PIECES
STEPS = 4


def spots():
    dp = lax.axis_index("dp")
    shard = lax.axis_index("shard")
    return dict(
        p=dp // 4,
        zi=(dp // 2) % 2,
        z=dp // 2,
        y=dp % 2,
        k=dp % 4,
        x=shard // 2,
        c=shard % 2,
        dp=dp,
        shard=shard,
    )


def device(s, z=None, y=None, x=None, c=None):
    z = s["z"] if z is None else z
    y = s["y"] if y is None else y
    x = s["x"] if x is None else x
    c = s["c"] if c is None else c
    return (z * 2 + y, x * 2 + c)


def peer(s, d):
    y = 1 - s["y"] if d % 2 else s["y"]
    zi = 1 - s["zi"] if d // 2 else s["zi"]
    z = 2 * s["p"] + zi
    return dict(y=y, zi=zi, k=2 * zi + y, dev=(z * 2 + y, s["shard"]))


def stripe(y, zi, xb):
    return 4 * y + 2 * xb + zi


def cols(index):
    return pl.ds(pl.multiple_of(index * ROWS, ROWS), ROWS)


def aligned(start, size):
    return pl.ds(pl.multiple_of(start, size), size)


def remote(src, dst, send, recv, dev):
    return pltpu.make_async_remote_copy(
        src_ref=src, dst_ref=dst, send_sem=send, recv_sem=recv, device_id=dev, device_id_type=MESH
    )


def dot(left, right):
    return jnp.dot(left, right, preferred_element_type=F32)


def dot_nt(left, right):
    return lax.dot_general(left, right, (((1,), (1,)), ((), ())), preferred_element_type=F32)


def dot_tn(left, right):
    return lax.dot_general(left, right, (((0,), (0,)), ((), ())), preferred_element_type=F32)


def signal(dev):
    pl.semaphore_signal(
        pltpu.get_barrier_semaphore(), inc=1, device_id=dev, device_id_type=MESH
    )


def step_kernel(
    ids_in,
    targets_in,
    hidden_in,
    cell_in,
    embedding_in,
    input_in,
    weight_in,
    gate_in,
    decoder_in,
    outbias_in,
    hx_o,
    dgt_o,
    dg_o,
    w2_o,
    dc0_o,
    emb_o,
    gdec_o,
    w2,
    wt,
    hx,
    act,
    call,
    dg,
    dgt,
    pbuf,
    rbuf,
    ownp,
    dcn,
    wo,
    dlog,
    metas,
    emb,
    cells,
    dpart,
    d_out,
    d_in,
    f_out,
    f_in,
    wext,
    h_own,
    cell_own,
    meta_own,
    wout_own,
    table,
    dbias,
    narrow,
    ids_wide,
    g_send,
    g_recv,
    wz_send,
    wz_recv,
    wx_send,
    wx_recv,
    wc_send,
    wc_recv,
    o_send,
    o_recv,
    h_send,
    h_recv,
    b_send,
    b_recv,
    d_send,
    d_recv,
    f_send,
    f_recv,
    out_sem,
):
    s = spots()
    z, y, x, c, k, zi, p = s["z"], s["y"], s["x"], s["c"], s["k"], s["zi"], s["p"]
    dp, shard = s["dp"], s["shard"]
    across = device(s, x=1 - x)
    twin = device(s, c=1 - c)
    far = device(s, z=2 * (1 - p) + zi)
    peers = {d: peer(s, d) for d in (1, 2, 3)}
    mine = [stripe(y, zi, xb) for xb in (0, 1)]
    core = z % 2
    off_core = jnp.where(core == c, 0, 1)
    quad = [(dx, dc) for dx in range(2) for dc in range(2) if (dx, dc) != (0, 0)]

    def flip(value, by):
        return 1 - value if by else value

    def quad_to(dx, dc):
        return device(s, x=flip(x, dx), c=flip(c, dc))

    def final_to(xb):
        return 4 * y + 2 * xb + zi

    def final_from(half):
        return 4 * half + 2 * y + p

    for d in (1, 2, 3):
        signal(peers[d]["dev"])
    signal(across)
    signal(twin)
    signal(far)

    signal(device(s, x=1 - x, c=1 - c))

    @pl.when(core != c)
    def _():
        for i in (0, 1):
            signal(device(s, z=c + 2 * i, c=core))

    away = 0
    for n in (0, 1):

        @pl.when(final_from(n) != dp)
        def _():
            signal((final_from(n), shard))

        away = away + jnp.where(final_to(n) != dp, 1, 0)

    narrow[...] = jnp.zeros_like(narrow)
    narrow[pl.ds(0, INPUTS), :] = input_in[...]
    narrow[pl.ds(INPUTS, 1), :] = gate_in[...]
    wext[:, pl.ds(HID, WIDE - HID)] = narrow[...].T.astype(BF16)
    wext[:, pl.ds(0, HID)] = weight_in[...].astype(BF16)
    ids_wide[...] = jnp.zeros_like(ids_wide)
    ids_wide[pl.ds(0, STEPS), pl.ds(0, 64)] = ids_in[...]
    ids_wide[pl.ds(STEPS, STEPS), pl.ds(0, 64)] = targets_in[...]
    meta_own[...] = ids_wide[...].T[0:64, :]
    h_own[...] = hidden_in[...].astype(BF16)
    vocab = decoder_in.shape[1]
    wout_own[...] = jnp.zeros_like(wout_own)
    wout_own[:, pl.ds(0, vocab)] = decoder_in[...].astype(BF16)
    cell_own[...] = cell_in[...].astype(BF16)
    pl.semaphore_wait(pltpu.get_barrier_semaphore(), 7 + 2 * off_core + away)

    def z_copy(target, q):
        rows = pl.ds(q * PIECE, PIECE)
        slot = aligned((2 * z + x) * ROWS + q * PIECE, PIECE)
        return remote(
            wext.at[rows],
            w2.at[slot],
            wz_send.at[target, q],
            wz_recv.at[z // 2, q],
            device(s, z=c + 2 * target, c=core),
        )

    def z_wait(i, q):
        slot = aligned((2 * (c + 2 * i) + x) * ROWS + q * PIECE, PIECE)
        remote(wext.at[pl.ds(q * PIECE, PIECE)], w2.at[slot], wz_send.at[0, q], wz_recv.at[i, q], across).wait_recv()

    def x_copy(i, q, sender=True):
        xs = x if sender else 1 - x
        slot = aligned((2 * (c + 2 * i) + xs) * ROWS + q * PIECE, PIECE)
        return remote(w2.at[slot], w2.at[slot], wx_send.at[i, q], wx_recv.at[i, q], across)

    def c_copy(i, q, n, other, sender=True):
        xs = 1 - x if other else x
        cs = c if sender else 1 - c
        slot = aligned((2 * (cs + 2 * i) + xs) * ROWS + q * PIECE, PIECE)
        return remote(
            w2.at[slot], w2.at[slot], wc_send.at[n, int(other), q], wc_recv.at[n, int(other), q], twin
        )

    near = p
    beyond = 1 - p

    def start_beyond():
        for q in range(PIECES):

            @pl.when(c + 2 * beyond != z)
            def _():
                z_copy(beyond, q).start()

    pl.when(zi != p)(start_beyond)
    own = aligned(k * 64, 64)

    def group_copy(d, n):
        dev = peers[d]["dev"]
        send, recv = g_send.at[d - 1, n], g_recv.at[d - 1, n]
        if n == 0:
            return remote(meta_own, metas.at[own], send, recv, dev)
        if n == 1:
            return remote(h_own, hx.at[0, own, pl.ds(0, HID)], send, recv, dev)
        if n == 2:
            return remote(wout_own, wo.at[dp, shard], send, recv, dev)
        theirs = stripe(peers[d]["y"], peers[d]["zi"], n - 3)
        return remote(cell_own.at[:, cols(theirs)], cells.at[n - 3, own], send, recv, dev)

    def corner_copy(n, sender=True):
        there = peers[2 if sender else 3]
        rows = aligned(there["k"] * 64, 64)
        send, recv = g_send.at[2, n], g_recv.at[2, n]
        dev = peers[1]["dev"]
        if n == 0:
            part = metas.at[rows]
        elif n == 1:
            part = hx.at[0, rows, pl.ds(0, HID)]
        else:
            part = wo.at[there["dev"][0], shard]
        return remote(part, part, send, recv, dev)

    @pl.when(c + 2 * near == z)
    def _():
        w2[aligned((2 * z + x) * ROWS, ROWS), :] = wext[...]

    for q in range(PIECES):

        @pl.when(c + 2 * near != z)
        def _():
            z_copy(near, q).start()

        if q == 0:
            for n in (0, 2, 1):
                for d in (2, 1):
                    group_copy(d, n).start()
    for n in (3, 4):
        for d in (3, 2, 1):
            group_copy(d, n).start()
    pl.when(zi == p)(start_beyond)
    metas[own, :] = meta_own[...]
    hx[0, own, pl.ds(0, HID)] = h_own[...]
    wo[dp, shard] = wout_own[...]
    for xb in (0, 1):
        cells[xb, own] = cell_own[:, cols(mine[xb])]

    dbias[...] = jnp.full(dbias.shape, -1e30, F32)
    dbias[pl.ds(0, 1), pl.ds(0, vocab)] = outbias_in[...].reshape(1, vocab)
    table[...] = jnp.where(lax.broadcasted_iota(jnp.int32, table.shape, 1) == INPUTS, 1.0, 0.0)
    table[pl.ds(0, vocab), pl.ds(0, INPUTS)] = embedding_in[...].astype(BF16).astype(F32)

    def group_wait(d, n):
        there = peers[d]
        rows = aligned(there["k"] * 64, 64)
        send, recv = g_send.at[d - 1, n], g_recv.at[d - 1, n]
        if n == 0:
            copy = remote(meta_own, metas.at[rows], send, recv, there["dev"])
        elif n == 1:
            copy = remote(h_own, hx.at[0, rows, pl.ds(0, HID)], send, recv, there["dev"])
        elif n == 2:
            copy = remote(wout_own, wo.at[there["dev"][0], shard], send, recv, there["dev"])
        else:
            copy = remote(cell_own.at[:, cols(mine[n - 3])], cells.at[n - 3, rows], send, recv, there["dev"])
        copy.wait_recv()

    lanes = lax.broadcasted_iota(jnp.int32, (ROWS, CHARS), 1)

    def first_step(g):
        for xb in (0, 1):
            act[0, 2 * g + xb] = dot(hx[0], wt[2 * g + xb])

    def embed_inputs():
        for t in range(STEPS):
            one = jnp.where(metas[:, t : t + 1] == lanes, 1.0, 0.0).astype(BF16)
            hx[t, :, pl.ds(HID, WIDE - HID)] = dot(one, table[...].astype(BF16)).astype(BF16)

    def turn(b):
        wt[b] = w2[cols(b), :].T

    order = [(n, q) for n in (0, 1) for q in range(PIECES)]
    gates = (p, 1 - p)
    for at, (n, q) in enumerate(order):
        i = gates[n]

        @pl.when(c + 2 * i != z)
        def _():
            z_wait(i, q)

        x_copy(i, q).start()
        c_copy(i, q, n, False).start()
        if at > 0:
            before, slot = order[at - 1]
            x_copy(gates[before], slot, False).wait_recv()
            c_copy(gates[before], slot, before, True).start()
        if n == 0 and q == PIECES - 1:
            for m in (0, 2, 1):
                group_wait(2, m)
                corner_copy(m).start()
        if n == 1 and q < 2:
            turn(2 * (c + 2 * p) + q)
        if n == 1 and q == 3:
            for m in (0, 1):
                group_wait(1, m)
                corner_copy(m, False).wait_recv()
            embed_inputs()
        if n == 1 and q == 3:
            first_step(2 * p)
            first_step(2 * p + 1)
        if n == 1 and q == 2:
            for other in (False, True):
                for slot in range(PIECES):
                    c_copy(p, slot, 0, other, False).wait_recv()
            for xs in (0, 1):
                turn(2 * (1 - c + 2 * p) + xs)
    x_copy(1 - p, PIECES - 1, False).wait_recv()
    c_copy(1 - p, PIECES - 1, 1, True).start()
    for xs in (0, 1):
        turn(2 * (c + 2 * (1 - p)) + xs)
    for other in (False, True):
        for q in range(PIECES):
            c_copy(1 - p, q, 1, other, False).wait_recv()
    for xs in (0, 1):
        turn(2 * (1 - c + 2 * (1 - p)) + xs)
    for a in (0, 1):
        first_step(2 * (1 - p) + a)
    w2_out = pltpu.make_async_copy(w2, w2_o, out_sem.at[6])
    w2_out.start()
    group_wait(1, 2)
    corner_copy(2, False).wait_recv()
    for n in (3, 4):
        for d in (1, 2, 3):
            group_wait(d, n)
        call[0, n - 3] = cells[n - 3].astype(F32)

    def far_copy(sender=True):
        first = 4 * p if sender else 4 * (1 - p)
        part = wo.at[pl.ds(first, 4), shard]
        return remote(part, part, o_send.at[0], o_recv.at[0], far)

    def over_copy(sender=True):
        part = wo.at[:, 2 * x + c if sender else 2 * (1 - x) + c]
        return remote(part, part, o_send.at[1], o_recv.at[1], across)

    def twin_copy(xs, sender=True):
        part = wo.at[:, 2 * xs + (c if sender else 1 - c)]
        return remote(part, part, o_send.at[2 + xs], o_recv.at[2 + xs], twin)

    def h_copy(t, part, xb, d, sender=True):
        there = peers[d]
        rows = pl.ds(part * PART, PART)
        at = mine[xb] if sender else stripe(there["y"], there["zi"], xb)
        block = hx.at[t + 1, rows, cols(at)]
        return remote(block, block, h_send.at[t, part, xb, d - 1], h_recv.at[t, part, xb, d - 1], there["dev"])

    def forward(t, part):
        rows = pl.ds(part * PART, PART)
        for xb in (0, 1):

            def pre(g):
                if t == 0:
                    return act[0, 2 * g + xb, rows]
                return dot(hx[t, rows, :], wt[2 * g + xb])

            gate_i = jax.nn.sigmoid(pre(0))
            act[t, xb, rows] = gate_i
            gate_f = jax.nn.sigmoid(pre(1))
            act[t, 2 + xb, rows] = gate_f
            gate_g = jnp.tanh(pre(2))
            act[t, 4 + xb, rows] = gate_g
            gate_o = jax.nn.sigmoid(pre(3))
            act[t, 6 + xb, rows] = gate_o
            cell = gate_f * call[t, xb, rows] + gate_i * gate_g
            call[t + 1, xb, rows] = cell
            hx[t + 1, rows, cols(mine[xb])] = (gate_o * jnp.tanh(cell)).astype(BF16)
            for d in (3, 1, 2):
                h_copy(t, part, xb, d).start()

    def h_wait(t, part):
        for xb in (0, 1):
            for d in (1, 2, 3):
                h_copy(t, part, xb, d, False).wait_recv()

    part_lanes = lax.broadcasted_iota(jnp.int32, (PART, CHARS), 1)
    part_rows = lax.broadcasted_iota(jnp.int32, (PART, 1), 0)
    totals = dict(loss=jnp.zeros((1, 1), F32), bias=jnp.zeros((1, CHARS), F32))

    def decode(t, part):
        rows = pl.ds(part * PART, PART)
        logits = dot(hx[t + 1, rows, pl.ds(0, HID)], wo[...].reshape(HID, CHARS)) + dbias[0:1, :]
        top = jnp.max(logits, axis=1, keepdims=True)
        grown = jnp.exp(logits - top)
        total = jnp.sum(grown, axis=1, keepdims=True)
        hit = metas[rows, STEPS + t : STEPS + t + 1] == part_lanes
        picked = jnp.sum(jnp.where(hit, logits, 0.0), axis=1, keepdims=True)
        low = ((grown / total - jnp.where(hit, 1.0, 0.0)) / STEPS).astype(BF16)
        dlog[t, rows] = low
        at = part_rows + part * PART
        ours = (at >= k * 64) & (at < k * 64 + 64)
        term = jnp.where(ours, (top + jnp.log(total) - picked) / STEPS, 0.0)
        totals["loss"] = totals["loss"] + jnp.sum(term, axis=0, keepdims=True)
        totals["bias"] = totals["bias"] + jnp.sum(jnp.where(ours, low.astype(F32), 0.0), axis=0, keepdims=True)

    far_copy().start()
    for part in range(SPLIT):
        forward(0, part)
    far_copy(False).wait_recv()
    over_copy().start()
    for part in range(SPLIT):
        h_wait(0, part)
        forward(1, part)
    over_copy(False).wait_recv()
    for xs in (0, 1):
        twin_copy(xs).start()
    for part in range(SPLIT):
        h_wait(1, part)
        forward(2, part)
    for xs in (0, 1):
        twin_copy(xs, False).wait_recv()
    for part in range(SPLIT):
        decode(0, part)
    for part in range(SPLIT):
        h_wait(2, part)
        forward(3, part)
    for part in range(SPLIT):
        decode(1, part)
    hx_out = pltpu.make_async_copy(hx.at[pl.ds(0, STEPS)], hx_o, out_sem.at[0])
    hx_out.start()
    for part in range(SPLIT):
        decode(2, part)

    emb[...] = jnp.zeros_like(emb)
    dcn[...] = jnp.zeros_like(dcn)

    def b_copy(t, part, d):
        rows = pl.ds(part * PART, PART)
        return remote(
            pbuf.at[t - 1, d - 1, rows],
            rbuf.at[t - 1, d - 1, rows],
            b_send.at[t - 1, part, d - 1],
            b_recv.at[t - 1, part, d - 1],
            peers[d]["dev"],
        )

    def backward(t, part):
        rows = pl.ds(part * PART, PART)
        if t < STEPS - 1:
            for d in (1, 2, 3):
                b_copy(t + 1, part, d).wait_recv()
        for xb in (0, 1):
            dh = dot_nt(dlog[t, rows], wo[mine[xb]].reshape(ROWS, CHARS))
            wide = pl.ds(xb * ROWS, ROWS)
            if t < STEPS - 1:
                dh = dh + ownp[rows, wide]
                for d in (1, 2, 3):
                    dh = dh + rbuf[t, d - 1, rows, wide].astype(F32)
            gate_i = act[t, xb, rows]
            gate_f = act[t, 2 + xb, rows]
            gate_g = act[t, 4 + xb, rows]
            gate_o = act[t, 6 + xb, rows]
            shown = jnp.tanh(call[t + 1, xb, rows])
            dc = dcn[xb, rows] + dh * gate_o * (1.0 - shown * shown)
            dcn[xb, rows] = dc * gate_f
            dg[t, rows, pl.ds(xb * ROWS, ROWS)] = (dc * gate_g * gate_i * (1.0 - gate_i)).astype(BF16)
            dg[t, rows, pl.ds((2 + xb) * ROWS, ROWS)] = (
                dc * call[t, xb, rows] * gate_f * (1.0 - gate_f)
            ).astype(BF16)
            dg[t, rows, pl.ds((4 + xb) * ROWS, ROWS)] = (dc * gate_i * (1.0 - gate_g * gate_g)).astype(BF16)
            dg[t, rows, pl.ds((6 + xb) * ROWS, ROWS)] = (dh * shown * gate_o * (1.0 - gate_o)).astype(BF16)
        if t > 0:
            for d in (3, 1, 2):
                there = peers[d]
                for xb in (0, 1):
                    pbuf[t - 1, d - 1, rows, pl.ds(xb * ROWS, ROWS)] = dot(
                        dg[t, rows, :], w2[:, cols(stripe(there["y"], there["zi"], xb))]
                    ).astype(BF16)
                b_copy(t, part, d).start()
            for xb in (0, 1):
                ownp[rows, pl.ds(xb * ROWS, ROWS)] = dot(dg[t, rows, :], w2[:, cols(mine[xb])])
        dgt[t, :, pl.ds(part * PART, PART)] = dg[t, rows, :].T

    def extras(t):
        dx = dot(dg[t], w2[:, pl.ds(HID, WIDE - HID)])
        high = dx.astype(BF16)
        rest = (dx - high.astype(F32)).astype(BF16)
        one = jnp.where(metas[:, t : t + 1] == lanes, 1.0, 0.0).astype(BF16)
        emb[...] += dot_tn(one, high) + dot_tn(one, rest)

    def d_copy(n):
        return remote(d_out.at[n], d_in.at[n], d_send.at[n], d_recv.at[n], quad_to(*quad[n]))

    def f_copy(xb):
        return remote(f_out.at[xb], f_in.at[p], f_send.at[xb], f_recv.at[p], (final_to(xb), shard))

    def f_wait(n):
        remote(f_out.at[n], f_in.at[n], f_send.at[n], f_recv.at[n], across).wait_recv()

    def decoder_start():
        for xb in (0, 1):
            total = dot_tn(hx[1, :, cols(mine[xb])], dlog[0])
            for t in range(1, STEPS):
                total = total + dot_tn(hx[t + 1, :, cols(mine[xb])], dlog[t])
            dpart[xb] = total
        for n, (dx, dc) in enumerate(quad):
            theirs = 2 * flip(x, dx) + flip(c, dc)
            for xb in (0, 1):
                d_out[n, xb] = dpart[xb, aligned(theirs * 64, 64), :].astype(BF16)
            d_copy(n).start()

    def decoder_middle():
        for n in range(3):
            d_copy(n).wait_recv()
        for xb in (0, 1):
            part = dpart[xb, aligned(shard * 64, 64), :]
            for n in range(3):
                part = part + d_in[n, xb].astype(F32)
            f_out[xb] = part.astype(BF16)

            @pl.when(final_to(xb) != dp)
            def _():
                f_copy(xb).start()

            @pl.when(final_to(xb) == dp)
            def _():
                f_in[p] = f_out[xb]

    def decoder_end():
        for n in (0, 1):

            @pl.when(final_from(n) != dp)
            def _():
                f_wait(n)

        gdec_o[...] = f_in[0].astype(F32) + f_in[1].astype(F32)

    for part in range(SPLIT):
        h_wait(STEPS - 1, part)
        decode(STEPS - 1, part)
        backward(STEPS - 1, part)
    decoder_start()
    extras(STEPS - 1)
    dg_out = [pltpu.make_async_copy(dgt.at[t], dgt_o.at[t], out_sem.at[1 + t]) for t in range(STEPS)]
    dg_last = pltpu.make_async_copy(dg.at[0], dg_o, out_sem.at[5])
    dg_out[STEPS - 1].start()
    for t in reversed(range(STEPS - 1)):
        for part in range(SPLIT):
            backward(t, part)
        dg_out[t].start()
        if t == 0:
            dg_last.start()
        if t == STEPS - 2:
            decoder_middle()
        extras(t)
    decoder_end()

    for xb in (0, 1):
        dc0_o[:, pl.ds(xb * ROWS, ROWS)] = dcn[xb]
    at_row = lax.broadcasted_iota(jnp.int32, (288, 128), 0)
    at_col = lax.broadcasted_iota(jnp.int32, (288, 128), 1)
    block = jnp.where((at_row < 275) & (at_col < INPUTS), emb[pl.ds(0, 288), :], 0.0)
    for n in range(3):
        block = jnp.where(at_row == 276 + n, totals["bias"][:, n * 128 : n * 128 + 128], block)
    block = jnp.where((at_row == 279) & (at_col == 0), totals["loss"], block)
    emb_o[...] = block

    for q in range(PIECES):
        for target in (0, 1):

            @pl.when(c + 2 * target != z)
            def _():
                z_copy(target, q).wait_send()

        for n in (0, 1):
            x_copy(gates[n], q).wait_send()
            c_copy(gates[n], q, n, False).wait_send()
            c_copy(gates[n], q, n, True).wait_send()
    for n in range(5):
        for d in (1, 2):
            group_copy(d, n).wait_send()
        if n < 3:
            corner_copy(n).wait_send()
        else:
            group_copy(3, n).wait_send()
    for n in range(3):
        d_copy(n).wait_send()
    for xb in (0, 1):

        @pl.when(final_to(xb) != dp)
        def _():
            f_copy(xb).wait_send()

    far_copy().wait_send()
    over_copy().wait_send()
    for xs in (0, 1):
        twin_copy(xs).wait_send()
    for t in range(STEPS):
        for part in range(SPLIT):
            for d in (1, 2, 3):
                for xb in (0, 1):
                    h_copy(t, part, xb, d).wait_send()
                if t > 0:
                    b_copy(t, part, d).wait_send()
    hx_out.wait()
    w2_out.wait()
    dg_last.wait()
    for t in range(STEPS):
        dg_out[t].wait()


def sum_kernel(
    dgt_in,
    hx_in,
    dg_in,
    w2_in,
    dc0,
    emb,
    gdec_own,
    grad_o,
    emb_o,
    norm_o,
    gh_o,
    gc_o,
    dgt,
    hx,
    dg,
    w2,
    dh0,
    c_out,
    c_in,
    kept,
    x_out,
    x_in,
    z_out,
    z_in,
    gh_out,
    gh_in,
    gh_mid,
    gh_last,
    gc_out,
    gc_in,
    e_in,
    n_out,
    n_in,
    c_send,
    c_recv,
    x_send,
    x_recv,
    z_send,
    z_recv,
    g_send,
    g_recv,
    e_send,
    e_recv,
    n_send,
    n_recv,
    in_sem,
):
    s = spots()
    z, y, x, c, k, zi, p = s["z"], s["y"], s["x"], s["c"], s["k"], s["zi"], s["p"]
    dp, shard = s["dp"], s["shard"]
    across = device(s, x=1 - x)
    twin = device(s, c=1 - c)
    far = device(s, z=2 * (1 - p) + zi)
    peers = {d: peer(s, d) for d in (1, 2, 3)}
    core = z % 2
    column = [(dz, dc) for dz in range(4) for dc in range(2) if (dz, dc) != (0, 0)]
    plane = [(dy, dx) for dy in range(2) for dx in range(2) if (dy, dx) != (0, 0)]

    def flip(value, by):
        return 1 - value if by else value

    def column_to(dz, dc):
        return device(s, z=(z + dz) % 4, c=flip(c, dc))

    def column_from(dz, dc):
        return device(s, z=(z + 4 - dz) % 4, c=flip(c, dc))

    def plane_to(dy, dx):
        return device(s, y=flip(y, dy), x=flip(x, dx))

    loads = [
        pltpu.make_async_copy(source, target, in_sem.at[n])
        for n, (source, target) in enumerate(((hx_in, hx), (dgt_in, dgt), (dg_in, dg), (w2_in, w2)))
    ]
    for load in loads:
        load.start()
    for dz, dc in column:
        signal(column_from(dz, dc))
    for dy, dx in plane:
        signal(plane_to(dy, dx))
    signal(peers[3]["dev"])
    pl.semaphore_wait(pltpu.get_barrier_semaphore(), 11)

    def gc_copy(d):
        return remote(
            gc_out.at[d - 1], gc_in.at[d - 1], g_send.at[d - 1, 1], g_recv.at[d - 1, 1], peers[d]["dev"]
        )

    def gh_copy(n):
        if n == 0:
            return remote(gh_out, gh_in, g_send.at[0, 0], g_recv.at[0, 0], peers[1]["dev"])
        return remote(gh_mid, gh_last, g_send.at[1, 0], g_recv.at[1, 0], peers[2]["dev"])

    def states_start():
        for n, there in enumerate((peers[1], peers[3])):
            gh_out[n] = dh0[aligned(there["k"] * 64, 64), :].astype(BF16)
        gh_copy(0).start()
        for d in (1, 3, 2):
            gc_out[d - 1] = dc0[aligned(peers[d]["k"] * 64, 64), :].astype(BF16)
            gc_copy(d).start()

    def states_middle():
        gh_copy(0).wait_recv()
        total = dh0[aligned(peers[2]["k"] * 64, 64), :] + gh_in[1].astype(F32)
        gh_mid[...] = total.astype(BF16)
        gh_copy(1).start()

    tiles = ((0, 512), (512, 512), (1024, 512), (1536, 640))

    def block_of(b, store):
        for start, size in tiles:
            at = pl.ds(start, size)
            total = dot(dgt[0, cols(b), :], hx[0, :, at])
            for t in range(1, STEPS):
                total = total + dot(dgt[t, cols(b), :], hx[t, :, at])
            store(at, total)

    def c_copy(n, q):
        rows = pl.ds(q * SLICE, SLICE)
        return remote(c_out.at[n, rows], c_in.at[n, rows], c_send.at[n, q], c_recv.at[n, q], twin)

    def x_copy(i, q):
        rows = pl.ds(q * SLICE, SLICE)
        return remote(x_out.at[i, rows], x_in.at[i, rows], x_send.at[i, q], x_recv.at[i, q], across)

    def z_copy(i, q):
        rows = pl.ds(q * SLICE, SLICE)
        return remote(
            z_out.at[i, rows],
            z_in.at[p, rows],
            z_send.at[i, q],
            z_recv.at[p, q],
            device(s, z=c + 2 * gates[i], c=core),
        )

    def z_wait(n, q):
        rows = pl.ds(q * SLICE, SLICE)
        remote(z_out.at[n, rows], z_in.at[n, rows], z_send.at[n, q], z_recv.at[n, q], across).wait_recv()

    def for_twin(n, b):
        def store(at, value):
            c_out[n, :, at] = value.astype(BF16)

        block_of(b, store)
        for q in range(SLICES):
            c_copy(n, q).start()

    def keep(i, b):
        def store(at, value):
            kept[i, :, at] = value

        block_of(b, store)

    def add_twin(i, n, q):
        rows = pl.ds(q * SLICE, SLICE)
        c_copy(n, q).wait_recv()
        return kept[i, rows] + c_in[n, rows].astype(F32)

    half = aligned(c * 144, 144)
    rest = aligned((1 - c) * 144, 144)
    hops = (twin, across, far, peers[2]["dev"], peers[1]["dev"], twin)

    def e_copy(n):
        if n == 0:
            return remote(emb_o.at[rest], e_in.at[0], e_send.at[0], e_recv.at[0], hops[0])
        if n == 5:
            return remote(emb_o.at[half], e_in.at[5], e_send.at[5], e_recv.at[5], hops[5])
        return remote(e_out_of(n), e_in.at[n], e_send.at[n], e_recv.at[n], hops[n])

    def e_out_of(n):
        return e_in.at[5 + n]

    def e_start(n):
        if n in (1, 2, 3, 4):
            e_in[5 + n] = emb_o[half, :]
        e_copy(n).start()

    def e_finish(n):
        if n == 5:
            e_copy(5).wait()
            emb_o[rest, :] = e_in[5]
            return
        e_copy(n).wait()
        emb_o[half, :] = emb_o[half, :] + e_in[n]

    gates = (zi, 1 - zi)

    def pass_on(n, q):
        i = gates[n]
        rows = pl.ds(q * SLICE, SLICE)
        x_copy(n, q).wait_recv()
        total = add_twin(n, 2 + n, q) + x_in[n, rows].astype(F32)
        z_out[n, rows] = total.astype(BF16)

        @pl.when(c + 2 * i != z)
        def _():
            z_copy(n, q).start()

        @pl.when(c + 2 * i == z)
        def _():
            z_in[p, rows] = z_out[n, rows]

    def to_across(n):
        for q in range(SLICES):
            x_out[n, pl.ds(q * SLICE, SLICE)] = add_twin(2, n, q).astype(BF16)
            x_copy(n, q).start()

    emb_o[...] = emb[...]
    e_start(0)
    loads[0].wait()
    loads[1].wait()
    for_twin(0, 2 * (1 - c + 2 * gates[0]) + 1 - x)
    e_finish(0)
    e_start(1)
    keep(2, 2 * (c + 2 * gates[0]) + 1 - x)
    to_across(0)
    for_twin(2, 2 * (1 - c + 2 * gates[0]) + x)
    keep(0, 2 * (c + 2 * gates[0]) + x)
    pass_on(0, 0)
    e_finish(1)
    e_start(2)
    for_twin(1, 2 * (1 - c + 2 * gates[1]) + 1 - x)
    keep(2, 2 * (c + 2 * gates[1]) + 1 - x)
    pass_on(0, 1)
    to_across(1)
    loads[2].wait()
    loads[3].wait()
    for q in range(2, SLICES):
        pass_on(0, q)
        if q == 2:
            for n in range(HID // 512):
                dh0[:, pl.ds(n * 512, 512)] = dot(dg[...], w2[:, pl.ds(n * 512, 512)])
            states_start()
        if q == 3:
            e_finish(2)
            e_start(3)
            for_twin(3, 2 * (1 - c + 2 * gates[1]) + x)
        if q == 4:
            keep(1, 2 * (c + 2 * gates[1]) + x)
        if q == 6:
            e_finish(3)
            e_start(4)
    for q in range(SLICES):
        pass_on(1, q)
        if q == 0:
            states_middle()
        if q == 1:
            e_finish(4)
            e_start(5)
    e_finish(5)

    squares = jnp.zeros((1, 1), F32)

    def square_sum(value):
        return jnp.sum(jnp.sum(value * value, axis=1, keepdims=True), axis=0, keepdims=True)

    squares = squares + square_sum(gdec_own[...])
    for q in range(SLICES):
        rows = pl.ds(q * SLICE, SLICE)
        for n in (0, 1):

            @pl.when(jnp.logical_or(core != c, p != n))
            def _():
                z_wait(n, q)

        final = z_in[0, rows].astype(F32) + z_in[1, rows].astype(F32)
        grad_o[rows, :] = final
        squares = squares + square_sum(final)

    def n_copy(n):
        if n < 7:
            return remote(n_out.at[0], n_in.at[n], n_send.at[n], n_recv.at[n], column_to(*column[n]))
        return remote(n_out.at[1], n_in.at[n], n_send.at[n], n_recv.at[n], plane_to(*plane[n - 7]))

    n_out[0] = jnp.broadcast_to(squares, (8, 128))
    for n in range(7):
        n_copy(n).start()
    own = aligned(k * 64, 64)
    gh_copy(1).wait_recv()
    gh_o[...] = dh0[own, :] + gh_in[0].astype(F32) + gh_last[...].astype(F32)
    for d in (1, 2, 3):
        gc_copy(d).wait_recv()
    for xb in (0, 1):
        gc_o[:, cols(stripe(y, zi, xb))] = dc0[own, pl.ds(xb * ROWS, ROWS)]
        for d in (1, 2, 3):
            there = peers[d]
            gc_o[:, cols(stripe(there["y"], there["zi"], xb))] = gc_in[d - 1, :, pl.ds(xb * ROWS, ROWS)].astype(F32)
    total = n_out[0]
    for n in range(7):
        n_copy(n).wait_recv()
        total = total + n_in[n]
    n_out[1] = total
    for n in range(7, 10):
        n_copy(n).start()
    at_row = lax.broadcasted_iota(jnp.int32, (288, 128), 0)
    shared = square_sum(jnp.where(at_row == 279, 0.0, emb_o[...]))
    for n in range(7, 10):
        n_copy(n).wait_recv()
        total = total + n_in[n]
    norm_o[...] = total + shared

    for n in range(4):
        for q in range(SLICES):
            c_copy(n, q).wait_send()
    for i in (0, 1):
        for q in range(SLICES):
            x_copy(i, q).wait_send()

            @pl.when(c + 2 * gates[i] != z)
            def _():
                z_copy(i, q).wait_send()

    for d in (1, 2, 3):
        gc_copy(d).wait_send()
    for n in (0, 1):
        gh_copy(n).wait_send()
    for n in range(10):
        n_copy(n).wait_send()


def finish_kernel(
    streams_all,
    grad,
    emb,
    squares,
    gdec,
    gh,
    gc,
    m_embed,
    m_input,
    m_hidden,
    m_gate,
    m_decoder,
    m_outbias,
    loss_o,
    norm_o,
    gh_o,
    gc_o,
    g_embed,
    g_input,
    g_hidden,
    g_gate,
    g_decoder,
    g_outbias,
    n_embed,
    n_input,
    n_hidden,
    n_gate,
    n_decoder,
    n_outbias,
):
    norm = jnp.sqrt(squares[0:1, 0:1])
    norm_o[...] = norm
    factor = CLIP / jnp.maximum(norm, CLIP)
    loss_o[...] = emb[279:280, 0:1] / streams_all
    gh_o[...] = gh[...]
    gc_o[...] = gc[...]

    def out(value, momentum, grad_ref, new_ref):
        grad_ref[...] = value
        new_ref[...] = MOMENTUM * momentum[...] + factor * value

    vocab = m_outbias.shape[1]
    out(emb[pl.ds(0, vocab), pl.ds(0, INPUTS)], m_embed, g_embed, n_embed)
    turned = grad[:, pl.ds(HID, WIDE - HID)].T
    out(turned[0:INPUTS, :], m_input, g_input, n_input)
    out(turned[INPUTS : INPUTS + 1, :], m_gate, g_gate, n_gate)
    out(grad[:, pl.ds(0, HID)], m_hidden, g_hidden, n_hidden)
    out(gdec[:, pl.ds(0, vocab)], m_decoder, g_decoder, n_decoder)
    row = jnp.concatenate([emb[276 + n : 277 + n, :] for n in range(3)], axis=1)
    out(row[:, 0:vocab], m_outbias, g_outbias, n_outbias)


def split_local(
    char_ids,
    targets,
    hidden_start,
    cell_start,
    embedding,
    input_weight,
    hidden_weight,
    gate_bias,
    decoder_weight,
    decoder_bias,
    momentum_embed,
    momentum_input,
    momentum_hidden,
    momentum_gate,
    momentum_decoder,
    momentum_outbias,
):
    streams = char_ids.shape[0]
    vocab = embedding.shape[0]
    shape = jax.ShapeDtypeStruct
    vm = pl.BlockSpec(memory_space=pltpu.VMEM)
    hbm = pl.BlockSpec(memory_space=pl.ANY)
    dma = pltpu.SemaphoreType.DMA
    hx, dgt, dg, w2, dc0, emb, gdec_own = pl.pallas_call(
        step_kernel,
        out_shape=(
            shape((STEPS, ROWS, WIDE), BF16),
            shape((STEPS, HID, ROWS), BF16),
            shape((ROWS, HID), BF16),
            shape((HID, WIDE), BF16),
            shape((ROWS, 512), F32),
            shape((288, 128), F32),
            shape((64, CHARS), F32),
        ),
        in_specs=[vm] * 10,
        out_specs=(hbm,) * 4 + (vm,) * 3,
        scratch_shapes=[
            pltpu.VMEM((HID, WIDE), BF16),
            pltpu.VMEM((8, WIDE, ROWS), BF16),
            pltpu.VMEM((STEPS + 1, ROWS, WIDE), BF16),
            pltpu.VMEM((STEPS, 8, ROWS, ROWS), F32),
            pltpu.VMEM((STEPS + 1, 2, ROWS, ROWS), F32),
            pltpu.VMEM((STEPS, ROWS, HID), BF16),
            pltpu.VMEM((STEPS, HID, ROWS), BF16),
            pltpu.VMEM((STEPS - 1, 3, ROWS, 512), BF16),
            pltpu.VMEM((STEPS - 1, 3, ROWS, 512), BF16),
            pltpu.VMEM((ROWS, 512), F32),
            pltpu.VMEM((2, ROWS, ROWS), F32),
            pltpu.VMEM((8, 4, 64, CHARS), BF16),
            pltpu.VMEM((STEPS, ROWS, CHARS), BF16),
            pltpu.VMEM((ROWS, 128), jnp.int32),
            pltpu.VMEM((CHARS, 128), F32),
            pltpu.VMEM((2, ROWS, ROWS), BF16),
            pltpu.VMEM((2, ROWS, CHARS), F32),
            pltpu.VMEM((3, 2, 64, CHARS), BF16),
            pltpu.VMEM((3, 2, 64, CHARS), BF16),
            pltpu.VMEM((2, 64, CHARS), BF16),
            pltpu.VMEM((2, 64, CHARS), BF16),
            pltpu.VMEM((ROWS, WIDE), BF16),
            pltpu.VMEM((64, HID), BF16),
            pltpu.VMEM((64, HID), BF16),
            pltpu.VMEM((64, 128), jnp.int32),
            pltpu.VMEM((64, CHARS), BF16),
            pltpu.VMEM((CHARS, 128), F32),
            pltpu.VMEM((8, CHARS), F32),
            pltpu.VMEM((128, ROWS), F32),
            pltpu.VMEM((128, 128), jnp.int32),
            dma((3, 5)),
            dma((3, 5)),
            dma((2, PIECES)),
            dma((2, PIECES)),
            dma((2, PIECES)),
            dma((2, PIECES)),
            dma((2, 2, PIECES)),
            dma((2, 2, PIECES)),
            dma((4,)),
            dma((4,)),
            dma((STEPS, SPLIT, 2, 3)),
            dma((STEPS, SPLIT, 2, 3)),
            dma((STEPS - 1, SPLIT, 3)),
            dma((STEPS - 1, SPLIT, 3)),
            dma((3,)),
            dma((3,)),
            dma((2,)),
            dma((2,)),
            dma((3 + STEPS,)),
        ],
        compiler_params=pltpu.CompilerParams(
            collective_id=0, has_side_effects=True, vmem_limit_bytes=60 * 2**20
        ),
    )(
        char_ids.T,
        targets.T,
        hidden_start,
        cell_start,
        embedding,
        input_weight.T,
        hidden_weight,
        gate_bias[None, :],
        decoder_weight,
        decoder_bias,
    )
    grad, emb, norm, grad_hidden_start, grad_cell_start = pl.pallas_call(
        sum_kernel,
        out_shape=(
            shape((ROWS, WIDE), F32),
            shape((288, 128), F32),
            shape((8, 128), F32),
            shape((64, HID), F32),
            shape((64, HID), F32),
        ),
        in_specs=[hbm] * 4 + [vm] * 3,
        out_specs=(vm,) * 5,
        scratch_shapes=[
            pltpu.VMEM((STEPS, HID, ROWS), BF16),
            pltpu.VMEM((STEPS, ROWS, WIDE), BF16),
            pltpu.VMEM((ROWS, HID), BF16),
            pltpu.VMEM((HID, WIDE), BF16),
            pltpu.VMEM((ROWS, HID), F32),
            pltpu.VMEM((4, ROWS, WIDE), BF16),
            pltpu.VMEM((4, ROWS, WIDE), BF16),
            pltpu.VMEM((3, ROWS, WIDE), F32),
            pltpu.VMEM((2, ROWS, WIDE), BF16),
            pltpu.VMEM((2, ROWS, WIDE), BF16),
            pltpu.VMEM((2, ROWS, WIDE), BF16),
            pltpu.VMEM((2, ROWS, WIDE), BF16),
            pltpu.VMEM((2, 64, HID), BF16),
            pltpu.VMEM((2, 64, HID), BF16),
            pltpu.VMEM((64, HID), BF16),
            pltpu.VMEM((64, HID), BF16),
            pltpu.VMEM((3, 64, 512), BF16),
            pltpu.VMEM((3, 64, 512), BF16),
            pltpu.VMEM((10, 144, 128), F32),
            pltpu.VMEM((2, 8, 128), F32),
            pltpu.VMEM((10, 8, 128), F32),
            dma((4, SLICES)),
            dma((4, SLICES)),
            dma((2, SLICES)),
            dma((2, SLICES)),
            dma((2, SLICES)),
            dma((2, SLICES)),
            dma((3, 2)),
            dma((3, 2)),
            dma((6,)),
            dma((6,)),
            dma((10,)),
            dma((10,)),
            dma((4,)),
        ],
        compiler_params=pltpu.CompilerParams(
            collective_id=1, has_side_effects=True, vmem_limit_bytes=60 * 2**20
        ),
    )(dgt, hx, dg, w2, dc0, emb, gdec_own)
    streams_all = streams * lax.axis_size("dp") * lax.axis_size("shard")
    whole = lambda a: pl.BlockSpec(a, lambda n: (0, 0))
    rows = lambda r, w: pl.BlockSpec((r, w), lambda n: (n, 0))
    lanes = lambda r: pl.BlockSpec((r, ROWS // 2), lambda n: (0, n))
    weights = [
        (whole((vocab, INPUTS)), (vocab, INPUTS)),
        (lanes(INPUTS), (INPUTS, ROWS)),
        (rows(ROWS // 2, HID), (ROWS, HID)),
        (lanes(1), (1, ROWS)),
        (whole((64, vocab)), (64, vocab)),
        (whole((1, vocab)), (1, vocab)),
    ]
    state = (rows(32, HID), (64, HID))
    scalar = (whole((1, 1)), (1, 1))
    results = [scalar, scalar, state, state] + weights + weights
    loss, norm, gh, gc, *rest = pl.pallas_call(
        functools.partial(finish_kernel, float(streams_all)),
        grid=(2,),
        out_shape=[shape(dims, F32) for _, dims in results],
        in_specs=[
            rows(ROWS // 2, WIDE),
            whole((288, 128)),
            whole((8, 128)),
            whole((64, CHARS)),
            state[0],
            state[0],
        ]
        + [spec for spec, _ in weights],
        out_specs=[spec for spec, _ in results],
        compiler_params=pltpu.CompilerParams(vmem_limit_bytes=60 * 2**20),
    )(
        grad,
        emb,
        norm,
        gdec_own,
        grad_hidden_start,
        grad_cell_start,
        momentum_embed,
        momentum_input.T,
        momentum_hidden,
        momentum_gate[None, :],
        momentum_decoder,
        momentum_outbias[None, :],
    )
    for n in (0, 6):
        rest[n + 1] = rest[n + 1].T
        rest[n + 3] = rest[n + 3].reshape(-1)
        rest[n + 5] = rest[n + 5].reshape(-1)
    return (loss.reshape(1), norm.reshape(1), gh, gc, *rest)


def solution(mesh):
    fits = mesh.shape["dp"] == 8 and mesh.shape["shard"] == 4
    placed = (
        P(("dp", "shard"), None),
        P(("dp", "shard"), None),
        P(("dp", "shard"), None),
        P(("dp", "shard"), None),
        P(),
        P(("dp", "shard"), None),
        P(("dp", "shard"), None),
        P(("dp", "shard")),
        P(("dp", "shard"), None),
        P(),
        P(),
        P(("dp", "shard"), None),
        P(("dp", "shard"), None),
        P(("dp", "shard")),
        P(("dp", "shard"), None),
        P(),
    )
    return jax.shard_map(
        split_local if fits else local,
        mesh=mesh,
        in_specs=placed,
        out_specs=(
            P(),
            P(),
            P(("dp", "shard"), None),
            P(("dp", "shard"), None),
            P(),
            P(("dp", "shard"), None),
            P(("dp", "shard"), None),
            P(("dp", "shard")),
            P(("dp", "shard"), None),
            P(),
            P(),
            P(("dp", "shard"), None),
            P(("dp", "shard"), None),
            P(("dp", "shard")),
            P(("dp", "shard"), None),
            P(),
        ),
        check_vma=False,
    )
```
